32 devices in a mesh: row: 4 (over z), col: 8 (over y, x, core).
Axes of the slice: x: 2, y: 2, z: 4, core: 2. Of those that a mesh axis runs over, the one named last changes fastest.
Arguments:
- gradient: bfloat16 [4096, 6144], P('row', 'col'), may hold values from -1.5 to 1.5
- left_stat: float32 [4096, 4096], P('col', 'row'), may hold values from -6 to 6
- left_basis: bfloat16 [4096, 4096], P('col', 'row'), may hold values from -0.09375 to 0.09375
- right_basis: bfloat16 [6144, 6144], P('row', 'col'), may hold values from -0.078125 to 0.078125
- first_moment: float32 [4096, 6144], P('row', 'col'), may hold values from -0.625 to 0.625
- second_moment: float32 [4096, 6144], P('row', 'col'), may hold values from 0.01 to 0.1
Outputs:
- left_next: float32 [4096, 4096], P('col', 'row')
- first_next: float32 [4096, 6144], P('row', 'col')
- second_next: float32 [4096, 6144], P('row', 'col')
- direction: bfloat16 [4096, 6144], P('row', 'col')
The draws below stay inside these ranges and needn't reach their ends.
All inputs are finite; a program needn't handle non-finite values.
Results may differ from the reference program's by a relative error of at most 0.015.
Values may be sent and summed in bfloat16 or wider, within the bound.
No kernel may reach another device: no remote copies, remote signals or barrier semaphores. Data moves between devices by JAX's collectives and lax.ppermute only.
A program may use at most 128 MiB of HBM per device.

```python
import math
import jax
import jax.numpy as jnp
from jax import lax

D = 4096
FF = 6144
N_COL = 8


def raised(result, own_key, source, target, blocks, factor):
    def block_of(position):
        return (jnp.arange(result.shape[position]) // (result.shape[position] // blocks)).reshape((-1,) + (1,) * (result.ndim - 1 - position))

    first = jax.random.permutation(own_key, blocks)[block_of(target)]
    far = (block_of(target) + blocks // 2) % blocks
    return jnp.where((block_of(source) == first) | (block_of(source) == far), factor * result, result)


def level_of(own_key, extent, shards, least, top_value):
    level = 1.0
    for dim, shards_of in shards:
        steps = jax.random.uniform(jax.random.fold_in(jax.random.fold_in(own_key, 6), dim), (shards_of,), jnp.float32, least / len(shards), top_value / len(shards))
        level = level * jnp.repeat(jnp.exp(steps), extent[dim] // shards_of).reshape((-1,) + (1,) * (len(extent) - 1 - dim))
    return level


def gaussian(rng, dims, spread, most, cuts=(), kind=jnp.bfloat16):
    gain = level_of(rng, dims, cuts, -0.22, 0.18) if cuts else 1.0
    drawn = jax.random.normal(rng, dims, jnp.float32) * spread * gain
    return jnp.minimum(jnp.maximum(drawn, -most), most).astype(kind)


def bell_draw_with(key, extent, spread, most, shards, heavy, held_as=jnp.bfloat16):
    drawn = spread * jax.random.normal(key, extent, jnp.float32)
    if shards:
        drawn = drawn * level_of(key, extent, shards, -0.22, 0.18)
    return jnp.clip(raised(drawn, jax.random.fold_in(key, 3), *heavy), -most, most).astype(held_as)


def setup_inputs(seed: int = 0) -> dict:
    seeds = jax.random.split(jax.random.key(seed), 7)
    return {
        "gradient": bell_draw_with(seeds[0], (D, FF), 0.25, 1.5, ((0, 4), (1, 8)), (1, 0, 8, 2.0)),
        "left_stat": gaussian(seeds[1], (D, D), 1.0, 6.0, ((0, 8), (1, 4)), jnp.float32),
        "left_basis": gaussian(seeds[2], (D, D), D ** -0.5, 0.09375, ((0, 8), (1, 4))),
        "right_basis": gaussian(seeds[3], (FF, FF), FF ** -0.5, 0.078125, ((0, 4), (1, 8))),
        "first_moment": gaussian(seeds[4], (D, FF), 0.1, 0.625, ((0, 4), (1, 8)), jnp.float32),
        "second_moment": jnp.clip(jnp.exp(math.log(0.1) - 2.3025851 * jax.random.uniform(seeds[5], (D, FF), jnp.float32) ** level_of(seeds[5], (D, FF), ((0, 4), (1, 8)), -0.2, 0.2)), 0.01, 0.1),
    }


def reference(gradient, left_stat, left_basis, right_basis, first_moment, second_moment):
    half_rotated = jnp.dot(gradient, right_basis, preferred_element_type=jnp.float32).astype(jnp.bfloat16)
    rotated = jnp.dot(left_basis.T, half_rotated, preferred_element_type=jnp.float32)
    left_next = 0.95 * left_stat + 0.05 * jnp.dot(gradient, gradient.T, preferred_element_type=jnp.float32)
    first_next = 0.9 * first_moment + 0.1 * rotated
    second_next = 0.95 * second_moment + 0.05 * rotated * rotated
    scaled_first = first_next / (1.0 - 0.9 ** 10)
    scaled_second = second_next / (1.0 - 0.95 ** 10)
    normalized = (scaled_first / (jnp.sqrt(scaled_second) + 1e-08)).astype(jnp.bfloat16)
    width = FF // N_COL

    def add_block(running, number):
        offset = number * width
        left_part = lax.dynamic_slice_in_dim(normalized, offset, width, 1)
        right_part = lax.dynamic_slice_in_dim(right_basis, offset, width, 1)
        product = jnp.dot(left_part, right_part.T, preferred_element_type=jnp.float32)
        rounded = lax.optimization_barrier(product.astype(jnp.bfloat16))
        return (running + rounded.astype(jnp.float32), None)
    start_sum = jnp.zeros((D, FF), jnp.float32)
    total, unused = lax.scan(add_block, start_sum, jnp.arange(N_COL, dtype=jnp.int32))
    back = total.astype(jnp.bfloat16)
    direction = jnp.dot(left_basis, back, preferred_element_type=jnp.float32).astype(jnp.bfloat16)
    return (left_next, first_next, second_next, direction)
```

```python
import jax
import jax.numpy as jnp
from jax import lax
from jax.sharding import PartitionSpec as P


def contract_last(first, second):
    return lax.dot_general(
        first, second, (((1,), (1,)), ((), ())), preferred_element_type=jnp.float32
    )


def contract_first(first, second):
    return lax.dot_general(
        first, second, (((0,), (0,)), ((), ())), preferred_element_type=jnp.float32
    )


def body(gradient, left_stat, left_basis, right_basis, first_moment, second_moment):
    columns = lax.all_gather(gradient, "row", axis=0, tiled=True)
    left_cols = lax.all_gather(left_basis, "col", axis=0, tiled=True)
    right_cols = lax.all_gather(right_basis, "row", axis=0, tiled=True)
    left_rotated = contract_first(left_cols, columns).astype(jnp.bfloat16)
    left_rotated = lax.all_gather(left_rotated, "col", axis=1, tiled=True)
    product = lax.psum_scatter(
        contract_last(columns, gradient).astype(jnp.bfloat16), "col", scatter_dimension=0, tiled=True
    ).astype(jnp.float32)
    left_next = 0.95 * left_stat + 0.05 * product
    rotated = jnp.dot(left_rotated, right_cols, preferred_element_type=jnp.float32)
    first_next = 0.9 * first_moment + 0.1 * rotated
    second_next = 0.95 * second_moment + 0.05 * rotated * rotated
    scaled_first = first_next / (1.0 - 0.9**10)
    scaled_second = second_next / (1.0 - 0.95**10)
    normalized = (scaled_first / (jnp.sqrt(scaled_second) + 1e-08)).astype(jnp.bfloat16)
    back = lax.psum_scatter(
        jnp.dot(left_cols, normalized, preferred_element_type=jnp.float32).astype(jnp.bfloat16),
        "row",
        scatter_dimension=0,
        tiled=True,
    )
    direction = lax.psum_scatter(
        contract_last(back, right_cols).astype(jnp.bfloat16), "col", scatter_dimension=1, tiled=True
    )
    return (left_next, first_next, second_next, direction)


def solution(mesh):
    return jax.shard_map(
        body,
        mesh=mesh,
        in_specs=(
            P("row", "col"),
            P("col", "row"),
            P("col", "row"),
            P("row", "col"),
            P("row", "col"),
            P("row", "col"),
        ),
        out_specs=(P("col", "row"), P("row", "col"), P("row", "col"), P("row", "col")),
        check_vma=False,
    )
```

```python
import jax
import jax.numpy as jnp
from jax import lax
from jax.sharding import PartitionSpec as P


def contract_last(first, second):
    return lax.dot_general(
        first, second, (((1,), (1,)), ((), ())), preferred_element_type=jnp.float32
    )


def contract_first(first, second):
    return lax.dot_general(
        first, second, (((0,), (0,)), ((), ())), preferred_element_type=jnp.float32
    )


def exchange(x, axis, target):
    n = lax.axis_size(axis)
    return lax.ppermute(x, axis, [(j, target(j)) for j in range(n)])


def inner_of_four(axis):
    i = lax.axis_index(axis)
    return (i == 1) | (i == 2)


def relay_target(j):
    return (2, 0, 3, 1)[j]


def gather_rows(x, axis):
    n = lax.axis_size(axis)
    i = lax.axis_index(axis)
    if n == 4:
        mirror = exchange(x, axis, lambda j: j ^ 3)
        near = exchange(x, axis, lambda j: j ^ 1)
        relay = exchange(jnp.where(inner_of_four(axis), mirror, x), axis, relay_target)
        pieces = [(i, x), (i ^ 1, near), (i ^ 3, mirror), (i ^ 2, relay)]
    else:
        pieces = [(i, x)]
        for s in range(1, n):
            pieces.append(((i + s) % n, exchange(x, axis, lambda j: (j - s) % n)))
    rows, cols = x.shape
    whole = jnp.zeros((n * rows, cols), x.dtype)
    for index, piece in pieces:
        whole = lax.dynamic_update_slice(whole, piece, (index * rows, 0))
    return whole


def scatter_rows(x, axis):
    n = lax.axis_size(axis)
    i = lax.axis_index(axis)
    rows = x.shape[0] // n

    def part(index):
        return lax.dynamic_slice_in_dim(x, index * rows, rows, 0)

    total = part(i).astype(jnp.float32)
    if n == 4:
        inner = inner_of_four(axis)
        relay = exchange(part(i ^ 2), axis, lambda j: (1, 3, 0, 2)[j])
        near = exchange(part(i ^ 1), axis, lambda j: j ^ 1)
        mirror = part(i ^ 3).astype(jnp.float32) + jnp.where(inner, relay, 0).astype(jnp.float32)
        mirror = exchange(mirror.astype(x.dtype), axis, lambda j: j ^ 3)
        total = total + near.astype(jnp.float32) + mirror.astype(jnp.float32)
        total = total + jnp.where(inner, 0, relay).astype(jnp.float32)
    else:
        for s in range(1, n):
            total = total + exchange(part((i - s) % n), axis, lambda j: (j - s) % n).astype(jnp.float32)
    return total.astype(x.dtype)


def body(gradient, left_stat, left_basis, right_basis, first_moment, second_moment):
    left_cols = lax.all_gather(left_basis, "col", axis=0, tiled=True)
    columns = gather_rows(gradient, "row")
    left_rotated = contract_first(left_cols, columns).astype(jnp.bfloat16)
    left_rotated = lax.all_gather(left_rotated, "col", axis=1, tiled=True)
    product = lax.psum_scatter(
        contract_last(columns, gradient).astype(jnp.bfloat16), "col", scatter_dimension=0, tiled=True
    ).astype(jnp.float32)
    left_next = 0.95 * left_stat + 0.05 * product

    width = gradient.shape[1]
    parts = 3 if width % 384 == 0 else 1
    step = width // parts
    first_out, second_out, right_cols, turned = [], [], [], []
    for p in range(parts):
        cut = slice(p * step, (p + 1) * step)
        right_part = gather_rows(right_basis[:, cut], "row")
        rotated = jnp.dot(left_rotated, right_part, preferred_element_type=jnp.float32)
        first_next = 0.9 * first_moment[:, cut] + 0.1 * rotated
        second_next = 0.95 * second_moment[:, cut] + 0.05 * rotated * rotated
        scaled_first = first_next / (1.0 - 0.9**10)
        scaled_second = second_next / (1.0 - 0.95**10)
        normalized = (scaled_first / (jnp.sqrt(scaled_second) + 1e-08)).astype(jnp.bfloat16)
        back = jnp.dot(left_cols, normalized, preferred_element_type=jnp.float32).astype(jnp.bfloat16)
        turned.append(scatter_rows(back, "row"))
        first_out.append(first_next)
        second_out.append(second_next)
        right_cols.append(right_part)
    direction = lax.psum_scatter(
        contract_last(jnp.concatenate(turned, axis=1), jnp.concatenate(right_cols, axis=1)).astype(jnp.bfloat16),
        "col",
        scatter_dimension=1,
        tiled=True,
    )
    return (left_next, jnp.concatenate(first_out, axis=1), jnp.concatenate(second_out, axis=1), direction)


def solution(mesh):
    return jax.shard_map(
        body,
        mesh=mesh,
        in_specs=(
            P("row", "col"),
            P("col", "row"),
            P("col", "row"),
            P("row", "col"),
            P("row", "col"),
            P("row", "col"),
        ),
        out_specs=(P("col", "row"), P("row", "col"), P("row", "col"), P("row", "col")),
        check_vma=False,
    )
```

```python
import jax
import jax.numpy as jnp
from jax import lax
from jax.sharding import PartitionSpec as P

BF16 = jnp.bfloat16
F32 = jnp.float32

PAIRS = [(0, 1), (1, 0), (2, 3), (3, 2)]
MIDDLE = [(1, 2), (2, 1)]
OUTWARD = [(1, 0), (2, 3)]
INWARD = [(0, 1), (3, 2)]


def contract_last(first, second):
    return lax.dot_general(first, second, (((1,), (1,)), ((), ())), preferred_element_type=F32)


def contract_first(first, second):
    return lax.dot_general(first, second, (((0,), (0,)), ((), ())), preferred_element_type=F32)


def after(x, *earlier):
    return lax.optimization_barrier((x,) + earlier)[0]


def joined(keep_order, first, second):
    return jnp.where(keep_order, jnp.concatenate([first, second]), jnp.concatenate([second, first]))


def halves(keep_order, x):
    n = x.shape[0] // 2
    return jnp.where(keep_order, x[:n], x[n:]), jnp.where(keep_order, x[n:], x[:n])


class Line:
    def __init__(self, axis):
        self.axis = axis
        self.i = lax.axis_index(axis)
        self.even = self.i % 2 == 0
        self.lower = self.i < 2
        self.inner = (self.i == 1) | (self.i == 2)

    def send(self, x, pairs):
        return lax.ppermute(x, self.axis, pairs)

    def pair(self, x, *earlier):
        got = self.send(after(x, *earlier), PAIRS)
        return got, joined(self.even, x, got)

    def middle(self, near, *earlier):
        return self.send(after(near, *earlier), MIDDLE)

    def outward(self, middle, *earlier):
        return self.send(after(middle, *earlier), OUTWARD)

    def whole(self, near, middle, out):
        return joined(self.lower, near, jnp.where(self.inner, middle, out))

    def scatter_start(self, x):
        near, far = halves(self.lower, x)
        return near, far, self.send(far, INWARD)

    def scatter_end(self, near, through):
        got = self.send(through, MIDDLE)
        mine, other = halves(self.even, near.astype(F32) + got.astype(F32))
        got = self.send(other.astype(near.dtype), PAIRS)
        return (mine + got.astype(F32)).astype(near.dtype)


def add(first, second):
    return (first.astype(F32) + second.astype(F32)).astype(first.dtype)


def scatter_columns(rows, right_rel, axis):
    def swap(x, bit):
        return lax.ppermute(x, axis, [(j, j ^ bit) for j in range(8)])

    width = right_rel.shape[0] // 8
    kept = []
    cuts = 2
    size = rows.shape[0] // cuts
    for s in range(cuts):
        part = rows[s * size : (s + 1) * size]
        away = contract_last(part, right_rel[4 * width :]).astype(rows.dtype)
        here = contract_last(part, right_rel[: 4 * width])
        mine = (here + swap(away, 1).astype(F32)).astype(rows.dtype)
        half = size // 2
        block = lambda b, h: mine[h * half : (h + 1) * half, b * width : (b + 1) * width]
        by_x = swap(jnp.concatenate([block(1, 0), block(3, 0)], axis=1), 2)
        by_y = swap(jnp.concatenate([block(2, 1), block(3, 1)], axis=1), 4)
        then_y = swap(add(block(2, 0), by_x[:, width:]), 4)
        then_x = swap(add(block(1, 1), by_y[:, width:]), 2)
        kept.append(block(0, 0).astype(F32) + by_x[:, :width].astype(F32) + then_y.astype(F32))
        kept.append(block(0, 1).astype(F32) + by_y[:, :width].astype(F32) + then_x.astype(F32))
    return jnp.concatenate(kept).astype(rows.dtype)


def moments(rotated, first_moment, second_moment):
    first_next = 0.9 * first_moment + 0.1 * rotated
    second_next = 0.95 * second_moment + 0.05 * rotated * rotated
    scaled_first = first_next / (1.0 - 0.9**10)
    scaled_second = second_next / (1.0 - 0.95**10)
    normalized = (scaled_first / (jnp.sqrt(scaled_second) + 1e-08)).astype(BF16)
    return first_next, second_next, normalized


def cuts_of(width):
    sixth = width // 6
    ends = (0, 3 * sixth, 5 * sixth, width)
    return [slice(a, b) for a, b in zip(ends, ends[1:])]


def body_on_line(gradient, left_stat, left_basis, right_basis, first_moment, second_moment):
    line = Line("row")
    width = gradient.shape[1]
    cuts = cuts_of(width)
    left_cols = lax.all_gather(left_basis, "col", axis=0, tiled=True)
    items = [gradient[:, : width // 2], gradient[:, width // 2 :]] + [right_basis[:, cut] for cut in cuts]

    def left_rotated(columns):
        return lax.all_gather(contract_first(left_cols, columns).astype(BF16), "col", axis=1, tiled=True)

    pair0, near0 = line.pair(items[0])
    middle0 = line.middle(near0)
    pair1, near1 = line.pair(items[1], pair0)
    pair2, near2 = line.pair(items[2], pair1)
    out0 = line.outward(middle0, pair2)
    middle1 = line.middle(near1, middle0)
    columns0 = line.whole(near0, middle0, out0)
    rotated0 = left_rotated(columns0)
    pair3, near3 = line.pair(items[3], out0)
    out1 = line.outward(middle1, out0)
    middle2 = line.middle(near2, middle1)
    columns1 = line.whole(near1, middle1, out1)
    rotated1 = left_rotated(columns1)
    pair4, near4 = line.pair(items[4], out1)
    out2 = line.outward(middle2, out1)
    middle3 = line.middle(near3, middle2)
    out3 = line.outward(middle3, out2)
    middle4 = line.middle(near4, middle3)

    product = contract_last(jnp.concatenate([columns0, columns1], axis=1), gradient).astype(BF16)
    product = lax.psum_scatter(product, "col", scatter_dimension=0, tiled=True).astype(F32)
    left_next = 0.95 * left_stat + 0.05 * product

    first_out, second_out = [], []

    def part(cut, right_part, *earlier):
        split = right_part.reshape(8, 2, width // 2, right_part.shape[1])
        rotated = sum(
            jnp.dot(left, split[:, h].reshape(-1, right_part.shape[1]), preferred_element_type=F32)
            for h, left in enumerate((rotated0, rotated1))
        )
        first_next, second_next, normalized = moments(rotated, first_moment[:, cut], second_moment[:, cut])
        first_out.append(first_next)
        second_out.append(second_next)
        back = jnp.dot(left_cols, after(normalized, *earlier), preferred_element_type=F32).astype(BF16)
        return line.scatter_start(back)

    right0 = line.whole(near2, middle2, after(out2, middle4))
    back0, far0, sent0 = part(cuts[0], right0)
    out4 = line.outward(middle4, out3, far0)
    right1 = line.whole(near3, middle3, after(out3, far0))
    back1, far1, sent1 = part(cuts[1], right1, sent0)
    through0 = add(far0, sent0)
    right2 = line.whole(near4, middle4, after(out4, through0, far1))
    back2, far2, sent2 = part(cuts[2], right2, sent1)
    turned0 = line.scatter_end(back0, through0)
    turned1 = line.scatter_end(back1, add(far1, sent1))
    turned2 = line.scatter_end(back2, add(far2, sent2))

    i = lax.axis_index("col")
    right_cols = jnp.concatenate([right0, right1, right2], axis=1)
    blocks = [lax.dynamic_slice_in_dim(right_cols, (i ^ r) * width, width, 0) for r in (0, 2, 4, 6, 1, 3, 5, 7)]
    turned = jnp.concatenate([turned0, turned1, turned2], axis=1)
    direction = scatter_columns(turned, jnp.concatenate(blocks), "col")
    return (left_next, jnp.concatenate(first_out, axis=1), jnp.concatenate(second_out, axis=1), direction)


def body(gradient, left_stat, left_basis, right_basis, first_moment, second_moment):
    columns = lax.all_gather(gradient, "row", axis=0, tiled=True)
    left_cols = lax.all_gather(left_basis, "col", axis=0, tiled=True)
    right_cols = lax.all_gather(right_basis, "row", axis=0, tiled=True)
    left_rotated = lax.all_gather(contract_first(left_cols, columns).astype(BF16), "col", axis=1, tiled=True)
    product = contract_last(columns, gradient).astype(BF16)
    product = lax.psum_scatter(product, "col", scatter_dimension=0, tiled=True).astype(F32)
    left_next = 0.95 * left_stat + 0.05 * product
    rotated = jnp.dot(left_rotated, right_cols, preferred_element_type=F32)
    first_next, second_next, normalized = moments(rotated, first_moment, second_moment)
    back = jnp.dot(left_cols, normalized, preferred_element_type=F32).astype(BF16)
    back = lax.psum_scatter(back, "row", scatter_dimension=0, tiled=True)
    direction = contract_last(back, right_cols).astype(BF16)
    direction = lax.psum_scatter(direction, "col", scatter_dimension=1, tiled=True)
    return (left_next, first_next, second_next, direction)


def solution(mesh):
    on_line = mesh.shape["row"] == 4 and mesh.shape["col"] == 8
    return jax.shard_map(
        body_on_line if on_line else body,
        mesh=mesh,
        in_specs=(
            P("row", "col"),
            P("col", "row"),
            P("col", "row"),
            P("row", "col"),
            P("row", "col"),
            P("row", "col"),
        ),
        out_specs=(P("col", "row"), P("row", "col"), P("row", "col"), P("row", "col")),
        check_vma=False,
    )
```

```python
import jax
import jax.numpy as jnp
from jax import lax
from jax.experimental.layout import Layout, with_layout_constraint
from jax.sharding import PartitionSpec as P

BF16 = jnp.bfloat16
F32 = jnp.float32

PAIRS = [(0, 1), (1, 0), (2, 3), (3, 2)]
MIDDLE = [(1, 2), (2, 1)]
OUTWARD = [(1, 0), (2, 3)]
INWARD = [(0, 1), (3, 2)]
MIRROR = [(0, 3), (1, 2), (2, 1), (3, 0)]
RELAY = [(0, 2), (1, 0), (2, 3), (3, 1)]
RELAY_BACK = [(0, 1), (1, 3), (2, 0), (3, 2)]


def contract_last(first, second):
    return lax.dot_general(first, second, (((1,), (1,)), ((), ())), preferred_element_type=F32)


def contract_first(first, second):
    return lax.dot_general(first, second, (((0,), (0,)), ((), ())), preferred_element_type=F32)


def together(operands, *earlier):
    return lax.optimization_barrier(tuple(operands) + earlier)[: len(operands)]


def after(x, *earlier):
    return together([x], *earlier)[0]


def joined(keep_order, first, second):
    return jnp.where(keep_order, jnp.concatenate([first, second]), jnp.concatenate([second, first]))


def halves(keep_order, x):
    n = x.shape[0] // 2
    return jnp.where(keep_order, x[:n], x[n:]), jnp.where(keep_order, x[n:], x[:n])


class Line:
    def __init__(self, axis):
        self.axis = axis
        self.i = lax.axis_index(axis)
        self.even = self.i % 2 == 0
        self.lower = self.i < 2
        self.inner = (self.i == 1) | (self.i == 2)

    def send(self, x, pairs):
        return lax.ppermute(x, self.axis, pairs)

    def near(self, x, got):
        return joined(self.even, x, got)

    def whole(self, near, middle, out):
        return joined(self.lower, near, jnp.where(self.inner, middle, out))

    def placed(self, whole, piece, bits):
        return lax.dynamic_update_slice(whole, piece, ((self.i ^ bits) * piece.shape[0], 0))

    def block(self, x, bits):
        n = x.shape[0] // 4
        return lax.dynamic_slice_in_dim(x, (self.i ^ bits) * n, n, 0)

    def scatter_start(self, x):
        near, far = halves(self.lower, x)
        return near, far, self.send(far, INWARD)

    def scatter_end(self, near, through):
        got = self.send(through, MIDDLE)
        mine, other = halves(self.even, near.astype(F32) + got.astype(F32))
        got = self.send(other.astype(near.dtype), PAIRS)
        return (mine + got.astype(F32)).astype(near.dtype)

    def scatter_fast(self, x):
        relay = self.send(self.block(x, 2), RELAY_BACK)
        near = self.send(self.block(x, 1), PAIRS)
        mirror = add(self.block(x, 3), jnp.where(self.inner, relay, 0))
        mirror = self.send(mirror, MIRROR)
        total = self.block(x, 0).astype(F32) + near.astype(F32) + jnp.where(self.inner, 0, relay).astype(F32)
        return (total + mirror.astype(F32)).astype(x.dtype)


def add(first, second):
    return (first.astype(F32) + second.astype(F32)).astype(first.dtype)


def scatter_columns(rows, right_rel, axis):
    def swap(x, bit):
        return lax.ppermute(x, axis, [(j, j ^ bit) for j in range(8)])

    width = right_rel.shape[0] // 8
    kept = []
    cuts = 2
    size = rows.shape[0] // cuts
    for s in range(cuts):
        part = rows[s * size : (s + 1) * size]
        part = after(part, mine) if s else part
        away = contract_last(part, right_rel[4 * width :]).astype(rows.dtype)
        here = contract_last(part, right_rel[: 4 * width]).astype(rows.dtype)
        mine = add(after(here, away), swap(away, 1))
        half = size // 2
        block = lambda b, h: mine[h * half : (h + 1) * half, b * width : (b + 1) * width]
        by_x = swap(jnp.concatenate([block(1, 0), block(3, 0)], axis=1), 2)
        by_y = swap(jnp.concatenate([block(2, 1), block(3, 1)], axis=1), 4)
        then_y = swap(add(block(2, 0), by_x[:, width:]), 4)
        then_x = swap(add(block(1, 1), by_y[:, width:]), 2)
        kept.append(block(0, 0).astype(F32) + by_x[:, :width].astype(F32) + then_y.astype(F32))
        kept.append(block(0, 1).astype(F32) + by_y[:, :width].astype(F32) + then_x.astype(F32))
    return jnp.concatenate(kept).astype(rows.dtype)


def moments(rotated, first_moment, second_moment):
    first_next = 0.9 * first_moment + 0.1 * rotated
    second_next = 0.95 * second_moment + 0.05 * rotated * rotated
    scaled_first = first_next / (1.0 - 0.9**10)
    scaled_second = second_next / (1.0 - 0.95**10)
    normalized = (scaled_first / (jnp.sqrt(scaled_second) + 1e-08)).astype(BF16)
    return first_next, second_next, normalized


def body_on_line(gradient, left_stat, left_basis, right_basis, first_moment, second_moment):
    line = Line("row")
    send = line.send
    height, width = gradient.shape
    cuts = [slice(p * width // 3, (p + 1) * width // 3) for p in range(3)]
    left_cols = lax.all_gather(left_basis, "col", axis=0, tiled=True)
    own0, own1, own2 = [right_basis[:, cut] for cut in cuts]

    mirror = send(gradient, MIRROR)
    pair = send(gradient, PAIRS)

    relay, own0 = together([jnp.where(line.inner, mirror, gradient), own0], pair)
    relay = send(relay, RELAY)
    pair0 = send(own0, PAIRS)
    columns = jnp.zeros((4 * height, width), BF16)
    for bits, piece in ((0, gradient), (1, pair), (3, mirror)):
        columns = line.placed(columns, piece, bits)

    near0, own1, own2 = together([line.near(own0, pair0), own1, own2], relay)
    middle0 = send(near0, MIDDLE)
    pair1 = send(own1, PAIRS)
    pair2 = send(own2, PAIRS)
    columns = line.placed(columns, after(relay, pair1), 2)
    left_part = contract_first(left_cols, columns).astype(BF16)
    left_rotated = lax.all_gather(left_part, "col", axis=1, tiled=True)

    middle0, near1 = together([middle0, line.near(own1, pair1)], pair2, left_part)
    out0 = send(middle0, OUTWARD)
    middle1 = send(near1, MIDDLE)
    product = contract_last(after(columns, near1), gradient).astype(BF16)
    product = after(product, left_rotated)
    product = lax.psum_scatter(product, "col", scatter_dimension=0, tiled=True).astype(F32)
    left_next = 0.95 * left_stat + 0.05 * product

    middle1, near2 = together([middle1, line.near(own2, pair2)], out0)
    out1 = send(middle1, OUTWARD)
    middle2 = send(near2, MIDDLE)

    first_out, second_out = [], []

    def part(cut, right_part, *earlier):
        rotated = jnp.dot(left_rotated, right_part, preferred_element_type=F32)
        first_next, second_next, normalized = moments(rotated, first_moment[:, cut], second_moment[:, cut])
        first_out.append(first_next)
        second_out.append(second_next)
        return jnp.dot(left_cols, after(normalized, *earlier), preferred_element_type=F32).astype(BF16)

    right0 = line.whole(near0, middle0, after(out0, near2))
    back0, far0, sent0 = line.scatter_start(part(cuts[0], right0))
    out2 = send(after(middle2, out1, far0), OUTWARD)
    right1 = line.whole(near1, middle1, after(out1, far0))
    back1, far1, sent1 = line.scatter_start(part(cuts[1], right1, sent0))
    through0 = add(far0, sent0)
    right2 = line.whole(near2, middle2, after(out2, through0, far1))
    back2 = part(cuts[2], right2, sent1)
    turned2 = line.scatter_fast(back2)
    turned0 = line.scatter_end(back0, through0)
    turned1 = line.scatter_end(back1, add(far1, sent1))

    i = lax.axis_index("col")
    right_cols = jnp.concatenate(together([right0, right1, right2], back2), axis=1)
    blocks = [lax.dynamic_slice_in_dim(right_cols, (i ^ r) * width, width, 0) for r in (0, 2, 4, 6, 1, 3, 5, 7)]
    first_next, second_next = [
        with_layout_constraint(jnp.concatenate(together(x, back2), axis=1), Layout((0, 1)))
        for x in (first_out, second_out)
    ]
    turned = jnp.concatenate([turned0, turned1, turned2], axis=1)
    turned, right_rel, left_next, first_next, second_next = together(
        [turned, jnp.concatenate(blocks), left_next, first_next, second_next]
    )
    direction = scatter_columns(turned, right_rel, "col")
    return (left_next, first_next, second_next, direction)


def body(gradient, left_stat, left_basis, right_basis, first_moment, second_moment):
    columns = lax.all_gather(gradient, "row", axis=0, tiled=True)
    left_cols = lax.all_gather(left_basis, "col", axis=0, tiled=True)
    right_cols = lax.all_gather(right_basis, "row", axis=0, tiled=True)
    left_rotated = lax.all_gather(contract_first(left_cols, columns).astype(BF16), "col", axis=1, tiled=True)
    product = contract_last(columns, gradient).astype(BF16)
    product = lax.psum_scatter(product, "col", scatter_dimension=0, tiled=True).astype(F32)
    left_next = 0.95 * left_stat + 0.05 * product
    rotated = jnp.dot(left_rotated, right_cols, preferred_element_type=F32)
    first_next, second_next, normalized = moments(rotated, first_moment, second_moment)
    back = jnp.dot(left_cols, normalized, preferred_element_type=F32).astype(BF16)
    back = lax.psum_scatter(back, "row", scatter_dimension=0, tiled=True)
    direction = contract_last(back, right_cols).astype(BF16)
    direction = lax.psum_scatter(direction, "col", scatter_dimension=1, tiled=True)
    return (left_next, first_next, second_next, direction)


def solution(mesh):
    on_line = mesh.shape["row"] == 4 and mesh.shape["col"] == 8
    return jax.shard_map(
        body_on_line if on_line else body,
        mesh=mesh,
        in_specs=(
            P("row", "col"),
            P("col", "row"),
            P("col", "row"),
            P("row", "col"),
            P("row", "col"),
            P("row", "col"),
        ),
        out_specs=(P("col", "row"), P("row", "col"), P("row", "col"), P("row", "col")),
        check_vma=False,
    )
```

```python
import jax
import jax.numpy as jnp
from jax import lax
from jax.experimental.layout import Layout, with_layout_constraint
from jax.sharding import PartitionSpec as P

BF16 = jnp.bfloat16
F32 = jnp.float32

PAIRS = [(0, 1), (1, 0), (2, 3), (3, 2)]
MIDDLE = [(1, 2), (2, 1)]
OUTWARD = [(1, 0), (2, 3)]
INWARD = [(0, 1), (3, 2)]
MIRROR = [(0, 3), (1, 2), (2, 1), (3, 0)]
RELAY = [(0, 2), (1, 0), (2, 3), (3, 1)]
RELAY_BACK = [(0, 1), (1, 3), (2, 0), (3, 2)]


def contract_last(first, second):
    return lax.dot_general(first, second, (((1,), (1,)), ((), ())), preferred_element_type=F32)


def contract_first(first, second):
    return lax.dot_general(first, second, (((0,), (0,)), ((), ())), preferred_element_type=F32)


def together(operands, *earlier):
    return lax.optimization_barrier(tuple(operands) + earlier)[: len(operands)]


def after(x, *earlier):
    return together([x], *earlier)[0]


def joined(keep_order, first, second):
    return jnp.where(keep_order, jnp.concatenate([first, second]), jnp.concatenate([second, first]))


def halves(keep_order, x):
    n = x.shape[0] // 2
    return jnp.where(keep_order, x[:n], x[n:]), jnp.where(keep_order, x[n:], x[:n])


class Line:
    def __init__(self, axis):
        self.axis = axis
        self.i = lax.axis_index(axis)
        self.even = self.i % 2 == 0
        self.lower = self.i < 2
        self.inner = (self.i == 1) | (self.i == 2)

    def send(self, x, pairs):
        return lax.ppermute(x, self.axis, pairs)

    def near(self, x, got):
        return joined(self.even, x, got)

    def whole(self, near, middle, out):
        return joined(self.lower, near, jnp.where(self.inner, middle, out))

    def placed(self, whole, piece, bits):
        return lax.dynamic_update_slice(whole, piece, ((self.i ^ bits) * piece.shape[0], 0))

    def block(self, x, bits):
        n = x.shape[0] // 4
        return lax.dynamic_slice_in_dim(x, (self.i ^ bits) * n, n, 0)

    def scatter_start(self, x):
        near, far = halves(self.lower, x)
        return near, far, self.send(far, INWARD)

    def scatter_end(self, near, through):
        got = self.send(through, MIDDLE)
        mine, other = halves(self.even, near.astype(F32) + got.astype(F32))
        got = self.send(other.astype(near.dtype), PAIRS)
        return (mine + got.astype(F32)).astype(near.dtype)

    def scatter_fast(self, x):
        relay = self.send(self.block(x, 2), RELAY_BACK)
        near = self.send(self.block(x, 1), PAIRS)
        mirror = add(self.block(x, 3), jnp.where(self.inner, relay, 0))
        mirror = self.send(mirror, MIRROR)
        total = self.block(x, 0).astype(F32) + near.astype(F32) + jnp.where(self.inner, 0, relay).astype(F32)
        return (total + mirror.astype(F32)).astype(x.dtype)


def add(first, second):
    return (first.astype(F32) + second.astype(F32)).astype(first.dtype)


def scatter_columns(rows, right_rel, axis):
    def swap(x, bit):
        return lax.ppermute(x, axis, [(j, j ^ bit) for j in range(8)])

    width = right_rel.shape[0] // 8
    kept = []
    cuts = 2
    size = rows.shape[0] // cuts
    parts = [rows[s * size : (s + 1) * size] for s in range(cuts)]
    away = [contract_last(part, right_rel[4 * width :]).astype(rows.dtype) for part in parts]
    here = [contract_last(part, right_rel[: 4 * width]).astype(rows.dtype) for part in parts]
    here = together(here, *away)
    for s in range(cuts):
        mine = add(here[s], swap(away[s], 1))
        half = size // 2
        block = lambda b, h: mine[h * half : (h + 1) * half, b * width : (b + 1) * width]
        to_x = jnp.concatenate([block(1, 0), block(3, 0)], axis=1)
        to_y = jnp.concatenate([block(2, 1), block(3, 1)], axis=1)
        to_x, to_y = together([to_x, to_y])
        by_x = swap(to_x, 2)
        by_y = swap(to_y, 4)
        then_y = swap(add(block(2, 0), by_x[:, width:]), 4)
        then_x = swap(add(block(1, 1), by_y[:, width:]), 2)
        kept.append(block(0, 0).astype(F32) + by_x[:, :width].astype(F32) + then_y.astype(F32))
        kept.append(block(0, 1).astype(F32) + by_y[:, :width].astype(F32) + then_x.astype(F32))
    return jnp.concatenate(kept).astype(rows.dtype)


def moments(rotated, first_moment, second_moment):
    first_next = 0.9 * first_moment + 0.1 * rotated
    second_next = 0.95 * second_moment + 0.05 * rotated * rotated
    scaled_first = first_next / (1.0 - 0.9**10)
    scaled_second = second_next / (1.0 - 0.95**10)
    normalized = (scaled_first / (jnp.sqrt(scaled_second) + 1e-08)).astype(BF16)
    return first_next, second_next, normalized


def body_on_line(gradient, left_stat, left_basis, right_basis, first_moment, second_moment):
    line = Line("row")
    send = line.send
    height, width = gradient.shape
    cuts = [slice(p * width // 3, (p + 1) * width // 3) for p in range(3)]
    left_cols = lax.all_gather(left_basis, "col", axis=0, tiled=True)
    own0, own1, own2 = [right_basis[:, cut] for cut in cuts]

    mirror = send(gradient, MIRROR)
    pair = send(gradient, PAIRS)
    columns = line.placed(jnp.zeros((4 * height, width), BF16), gradient, 0)

    relay, own0 = together([jnp.where(line.inner, mirror, gradient), own0], pair)
    relay = send(relay, RELAY)
    pair0 = send(own0, PAIRS)
    turn = lambda x, bits: contract_first(line.block(left_cols, bits), x)
    left_sum = turn(gradient, 0) + turn(pair, 1) + turn(mirror, 3)

    near0, own1 = together([line.near(own0, pair0), own1], left_sum)
    middle0 = send(near0, MIDDLE)
    pair1 = send(own1, PAIRS)
    near1 = line.near(own1, pair1)

    left_part = (left_sum + turn(after(relay, near1, middle0), 2)).astype(BF16)
    left_rotated = lax.all_gather(left_part, "col", axis=1, tiled=True)

    middle0, near1, own2 = together([middle0, near1, own2])
    out0 = send(middle0, OUTWARD)
    middle1 = send(near1, MIDDLE)
    pair2 = send(own2, PAIRS)
    for bits, piece in zip((1, 3, 2), together([pair, mirror, relay], left_part)):
        columns = line.placed(columns, piece, bits)
    product = contract_last(columns, gradient).astype(BF16)
    product = after(product, left_rotated)
    product = lax.psum_scatter(product, "col", scatter_dimension=0, tiled=True).astype(F32)
    left_next = 0.95 * left_stat + 0.05 * product

    middle1, near2 = together([middle1, line.near(own2, pair2)], out0)
    out1 = send(middle1, OUTWARD)
    middle2 = send(near2, MIDDLE)

    first_out, second_out = [], []

    def part(cut, right_part, *earlier):
        rotated = jnp.dot(left_rotated, right_part, preferred_element_type=F32)
        first_next, second_next, normalized = moments(rotated, first_moment[:, cut], second_moment[:, cut])
        first_out.append(first_next)
        second_out.append(second_next)
        return jnp.dot(left_cols, after(normalized, *earlier), preferred_element_type=F32).astype(BF16)

    right0 = line.whole(near0, middle0, after(out0, near2))
    back0, far0, sent0 = line.scatter_start(part(cuts[0], right0))
    out2 = send(after(middle2, out1, far0), OUTWARD)
    right1 = line.whole(near1, middle1, after(out1, far0))
    back1, far1, sent1 = line.scatter_start(part(cuts[1], right1, sent0))
    through0 = add(far0, sent0)
    right2 = line.whole(near2, middle2, after(out2, through0, far1))
    back2 = part(cuts[2], right2, sent1)
    turned2 = line.scatter_fast(back2)
    turned0 = line.scatter_end(back0, through0)
    turned1 = line.scatter_end(back1, add(far1, sent1))

    i = lax.axis_index("col")
    right_cols = jnp.concatenate(together([right0, right1, right2], back2), axis=1)
    blocks = [lax.dynamic_slice_in_dim(right_cols, (i ^ r) * width, width, 0) for r in (0, 2, 4, 6, 1, 3, 5, 7)]
    first_next, second_next = [
        with_layout_constraint(jnp.concatenate(together(x, back2), axis=1), Layout((0, 1)))
        for x in (first_out, second_out)
    ]
    turned = jnp.concatenate([turned0, turned1, turned2], axis=1)
    turned, right_rel, left_next, first_next, second_next = together(
        [turned, jnp.concatenate(blocks), left_next, first_next, second_next]
    )
    direction = scatter_columns(turned, right_rel, "col")
    return (left_next, first_next, second_next, direction)


def body(gradient, left_stat, left_basis, right_basis, first_moment, second_moment):
    columns = lax.all_gather(gradient, "row", axis=0, tiled=True)
    left_cols = lax.all_gather(left_basis, "col", axis=0, tiled=True)
    right_cols = lax.all_gather(right_basis, "row", axis=0, tiled=True)
    left_rotated = lax.all_gather(contract_first(left_cols, columns).astype(BF16), "col", axis=1, tiled=True)
    product = contract_last(columns, gradient).astype(BF16)
    product = lax.psum_scatter(product, "col", scatter_dimension=0, tiled=True).astype(F32)
    left_next = 0.95 * left_stat + 0.05 * product
    rotated = jnp.dot(left_rotated, right_cols, preferred_element_type=F32)
    first_next, second_next, normalized = moments(rotated, first_moment, second_moment)
    back = jnp.dot(left_cols, normalized, preferred_element_type=F32).astype(BF16)
    back = lax.psum_scatter(back, "row", scatter_dimension=0, tiled=True)
    direction = contract_last(back, right_cols).astype(BF16)
    direction = lax.psum_scatter(direction, "col", scatter_dimension=1, tiled=True)
    return (left_next, first_next, second_next, direction)


def solution(mesh):
    on_line = mesh.shape["row"] == 4 and mesh.shape["col"] == 8
    return jax.shard_map(
        body_on_line if on_line else body,
        mesh=mesh,
        in_specs=(
            P("row", "col"),
            P("col", "row"),
            P("col", "row"),
            P("row", "col"),
            P("row", "col"),
            P("row", "col"),
        ),
        out_specs=(P("col", "row"), P("row", "col"), P("row", "col"), P("row", "col")),
        check_vma=False,
    )
```

```python
import jax
import jax.numpy as jnp
from jax import lax
from jax.experimental import pallas as pl
from jax.experimental.pallas import tpu as pltpu
from jax.sharding import PartitionSpec as P

BF16 = jnp.bfloat16
F32 = jnp.float32
VMEM = 40 * 2**20
QUICK = pl.CostEstimate(flops=2**20, bytes_accessed=2**16, transcendentals=0)

PAIRS = [(0, 1), (1, 0), (2, 3), (3, 2)]
MIDDLE = [(1, 2), (2, 1)]
OUTWARD = [(1, 0), (2, 3)]
INWARD = [(0, 1), (3, 2)]
MIRROR = [(0, 3), (1, 2), (2, 1), (3, 0)]
RELAY = [(0, 2), (1, 0), (2, 3), (3, 1)]
RELAY_BACK = [(0, 1), (1, 3), (2, 0), (3, 2)]


def contract_last(first, second):
    return lax.dot_general(first, second, (((1,), (1,)), ((), ())), preferred_element_type=F32)


def contract_first(first, second):
    return lax.dot_general(first, second, (((0,), (0,)), ((), ())), preferred_element_type=F32)


def together(operands, *earlier):
    return lax.optimization_barrier(tuple(operands) + earlier)[: len(operands)]


def after(x, *earlier):
    return together([x], *earlier)[0]


def joined(keep_order, first, second):
    return jnp.where(keep_order, jnp.concatenate([first, second]), jnp.concatenate([second, first]))


def halves(keep_order, x):
    n = x.shape[0] // 2
    return jnp.where(keep_order, x[:n], x[n:]), jnp.where(keep_order, x[n:], x[:n])


class Line:
    def __init__(self, axis):
        self.axis = axis
        self.i = lax.axis_index(axis)
        self.even = self.i % 2 == 0
        self.lower = self.i < 2
        self.inner = (self.i == 1) | (self.i == 2)

    def send(self, x, pairs):
        return lax.ppermute(x, self.axis, pairs)

    def near(self, x, got):
        return joined(self.even, x, got)

    def whole(self, near, middle, out):
        return joined(self.lower, near, jnp.where(self.inner, middle, out))

    def placed(self, whole, piece, bits):
        return lax.dynamic_update_slice(whole, piece, ((self.i ^ bits) * piece.shape[0], 0))

    def block(self, x, bits):
        n = x.shape[0] // 4
        return lax.dynamic_slice_in_dim(x, (self.i ^ bits) * n, n, 0)

    def scatter_start(self, x):
        near, far = halves(self.lower, x)
        return near, far, self.send(far, INWARD)

    def scatter_end(self, near, through):
        got = self.send(through, MIDDLE)
        mine, other = halves(self.even, near.astype(F32) + got.astype(F32))
        got = self.send(other.astype(near.dtype), PAIRS)
        return (mine + got.astype(F32)).astype(near.dtype)

    def scatter_fast(self, x):
        relay = self.send(self.block(x, 2), RELAY_BACK)
        near = self.send(self.block(x, 1), PAIRS)
        mirror = add(self.block(x, 3), jnp.where(self.inner, relay, 0))
        mirror = self.send(mirror, MIRROR)
        total = self.block(x, 0).astype(F32) + near.astype(F32) + jnp.where(self.inner, 0, relay).astype(F32)
        return (total + mirror.astype(F32)).astype(x.dtype), relay


def add(first, second):
    return (first.astype(F32) + second.astype(F32)).astype(first.dtype)


def products_kernel(rows_ref, right_ref, out_ref):
    out_ref[...] = contract_last(rows_ref[...], right_ref[...]).astype(out_ref.dtype)


def products(rows, right, start, count):
    height, depth = rows.shape
    width = right.shape[0] // 8
    return pl.pallas_call(
        products_kernel,
        grid=(count,),
        in_specs=[
            pl.BlockSpec((height, depth), lambda b: (0, 0)),
            pl.BlockSpec((width, depth), lambda b: (start + b, 0)),
        ],
        out_specs=pl.BlockSpec((height, width), lambda b: (0, b)),
        out_shape=jax.ShapeDtypeStruct((height, count * width), rows.dtype),
        compiler_params=pltpu.CompilerParams(vmem_limit_bytes=VMEM),
        cost_estimate=QUICK,
    )(rows, right)


def scatter_columns(rows, right_rel, axis):
    def swap(x, bit):
        return lax.ppermute(x, axis, [(j, j ^ bit) for j in range(8)])

    width = right_rel.shape[0] // 8
    kept = []
    cuts = 2
    size = rows.shape[0] // cuts
    parts = [rows[s * size : (s + 1) * size] for s in range(cuts)]
    away = [products(part, right_rel, 4, 4) for part in parts]
    got = [swap(x, 1) for x in away]
    here = [products(part, right_rel, 0, 4) for part in together(parts, *away)]
    for s in range(cuts):
        mine = add(here[s], got[s])
        half = size // 2
        block = lambda b, h: mine[h * half : (h + 1) * half, b * width : (b + 1) * width]
        by_x = swap(jnp.concatenate([block(1, 0), block(3, 0)], axis=1), 2)
        by_y = swap(jnp.concatenate([block(2, 1), block(3, 1)], axis=1), 4)
        then_y = swap(add(block(2, 0), by_x[:, width:]), 4)
        then_x = swap(add(block(1, 1), by_y[:, width:]), 2)
        kept.append(block(0, 0).astype(F32) + by_x[:, :width].astype(F32) + then_y.astype(F32))
        kept.append(block(0, 1).astype(F32) + by_y[:, :width].astype(F32) + then_x.astype(F32))
    return jnp.concatenate(kept).astype(rows.dtype)


def moments(rotated, first_moment, second_moment):
    first_next = 0.9 * first_moment + 0.1 * rotated
    second_next = 0.95 * second_moment + 0.05 * rotated * rotated
    scaled_first = first_next / (1.0 - 0.9**10)
    scaled_second = second_next / (1.0 - 0.95**10)
    normalized = (scaled_first / (jnp.sqrt(scaled_second) + 1e-08)).astype(BF16)
    return first_next, second_next, normalized


STEPS = 4


def part_kernel(place, left, near, middle, out, first, second, basis, *rest):
    first_out, second_out, back, total, normalized = rest[-5:]
    step = pl.program_id(0)

    @pl.when(step == 0)
    def _():
        total[...] = jnp.zeros_like(total)

    def accumulate(right):
        total[...] += jnp.dot(left[...], right[...], preferred_element_type=F32)

    @pl.when(step < STEPS)
    def _():
        accumulate(near)

    far = (step >= STEPS) & (step < 2 * STEPS)

    @pl.when(far & (place[2] == 1))
    def _():
        accumulate(middle)

    @pl.when(far & (place[2] == 0))
    def _():
        accumulate(out)

    @pl.when(step == 2 * STEPS - 1)
    def _():
        first_out[...], second_out[...], normalized[...] = moments(total[...], first[...], second[...])

    @pl.when(step >= 2 * STEPS)
    def _():
        back[...] = jnp.dot(basis[...], normalized[...], preferred_element_type=F32).astype(BF16)


def part(number, place, left_rotated, near, middle, out, first_moment, second_moment, left_cols, before):
    height, width = first_moment.shape
    size = near.shape[1]
    deep = near.shape[0] // STEPS
    tall = left_cols.shape[0] // 4
    near_step = lambda s: jnp.minimum(s, STEPS - 1)
    far_step = lambda s: jnp.clip(s - STEPS, 0, STEPS - 1)
    last_step = lambda s: jnp.maximum(s - 2 * STEPS, 0)

    def left_block(s, place):
        return jnp.where(s < STEPS, place[0] + near_step(s), place[1] + far_step(s)), 0, 0

    moment = pl.BlockSpec((height, size), lambda s, place: (0, number))
    before = list(before)
    return pl.pallas_call(
        part_kernel,
        grid_spec=pltpu.PrefetchScalarGridSpec(
            num_scalar_prefetch=1,
            grid=(2 * STEPS + 4,),
            in_specs=[
                pl.BlockSpec((None, height, deep), left_block),
                pl.BlockSpec((deep, size), lambda s, place: (near_step(s), 0)),
                pl.BlockSpec((deep, size), lambda s, place: (far_step(s) * place[2], 0)),
                pl.BlockSpec((deep, size), lambda s, place: (far_step(s) * (1 - place[2]), 0)),
                moment,
                moment,
                pl.BlockSpec((tall, height), lambda s, place: (last_step(s), 0)),
            ]
            + [pl.BlockSpec(memory_space=pl.ANY)] * len(before),
            out_specs=[moment, moment, pl.BlockSpec((tall, size), lambda s, place: (last_step(s), 0))],
            scratch_shapes=[pltpu.VMEM((height, size), F32), pltpu.VMEM((height, size), BF16)],
        ),
        out_shape=[
            jax.ShapeDtypeStruct((height, width), F32),
            jax.ShapeDtypeStruct((height, width), F32),
            jax.ShapeDtypeStruct((left_cols.shape[0], size), BF16),
        ],
        input_output_aliases={8: 0, 9: 1} if before else {},
        compiler_params=pltpu.CompilerParams(vmem_limit_bytes=VMEM),
        cost_estimate=QUICK,
    )(place, left_rotated, near, middle, out, first_moment, second_moment, left_cols, *before)


def body_on_line(gradient, left_stat, left_basis, right_basis, first_moment, second_moment):
    line = Line("row")
    send = line.send
    height, width = gradient.shape
    cuts = [slice(p * width // 3, (p + 1) * width // 3) for p in range(3)]
    left_cols = lax.all_gather(left_basis, "col", axis=0, tiled=True)
    own0, own1, own2 = [right_basis[:, cut] for cut in cuts]

    mirror = send(gradient, MIRROR)
    pair = send(gradient, PAIRS)
    relay = send(after(jnp.where(line.inner, mirror, gradient), pair), RELAY)
    turn = lambda x, bits: contract_first(line.block(left_cols, bits), x)
    left_sum = turn(gradient, 0) + turn(pair, 1) + turn(mirror, 3)
    pair0 = send(after(own0, left_sum), PAIRS)

    near0, own1 = together([line.near(own0, pair0), own1])
    middle0 = send(near0, MIDDLE)
    pair1 = send(own1, PAIRS)
    near1 = line.near(own1, pair1)

    left_part = (left_sum + turn(after(relay, near0), 2)).astype(BF16)
    left_rotated = lax.all_gather(left_part, "col")

    middle0, near1, own2 = together([middle0, near1, own2])
    out0 = send(middle0, OUTWARD)
    middle1 = send(near1, MIDDLE)
    pair2 = send(own2, PAIRS)
    columns = jnp.zeros((4 * height, width), BF16)
    for bits, piece in zip((0, 1, 3, 2), together([gradient, pair, mirror, relay], left_part)):
        columns = line.placed(columns, piece, bits)
    product = contract_last(columns, gradient).astype(BF16)
    left_rotated, product = together([left_rotated, product])
    product = lax.psum_scatter(product, "col", scatter_dimension=0, tiled=True).astype(F32)
    left_next = 0.95 * left_stat + 0.05 * product

    middle1, near2 = together([middle1, line.near(own2, pair2)], out0)
    out1 = send(middle1, OUTWARD)
    middle2 = send(near2, MIDDLE)

    steps = jnp.where(line.lower, jnp.array([0, STEPS]), jnp.array([STEPS, 0]))
    place = jnp.concatenate([steps, line.inner[None]]).astype(jnp.int32)

    def next_part(number, near, middle, out, before):
        *before, back = part(
            number, place, left_rotated, near, middle, out, first_moment, second_moment, left_cols, before
        )
        return before, back

    moments0, back0 = next_part(0, near0, middle0, after(out0, near2), ())
    back0, far0, sent0 = line.scatter_start(back0)
    out2 = send(after(middle2, out1, far0), OUTWARD)
    moments1, back1 = next_part(1, near1, middle1, after(out1, far0), moments0)
    back1, far1, sent1 = line.scatter_start(after(back1, sent0))
    through0 = add(far0, sent0)
    moments2, back2 = next_part(2, near2, middle2, after(out2, through0, far1), moments1)
    turned2, relayed = line.scatter_fast(after(back2, sent1))
    turned0 = line.scatter_end(back0, through0)
    turned1 = line.scatter_end(back1, add(far1, sent1))
    first_next, second_next = moments2

    near0, near1, near2, middle0, middle1, middle2, out0, out1, out2 = together(
        [near0, near1, near2, middle0, middle1, middle2, out0, out1, out2], relayed
    )
    right0 = line.whole(near0, middle0, out0)
    right1 = line.whole(near1, middle1, out1)
    right2 = line.whole(near2, middle2, out2)
    i = lax.axis_index("col")
    right_cols = jnp.concatenate([right0, right1, right2], axis=1)
    blocks = [lax.dynamic_slice_in_dim(right_cols, (i ^ r) * width, width, 0) for r in (0, 2, 4, 6, 1, 3, 5, 7)]
    turned = jnp.concatenate([turned0, turned1, turned2], axis=1)
    turned, right_rel, left_next = together([turned, jnp.concatenate(blocks), left_next])
    direction = scatter_columns(turned, right_rel, "col")
    return (left_next, first_next, second_next, direction)


def body(gradient, left_stat, left_basis, right_basis, first_moment, second_moment):
    columns = lax.all_gather(gradient, "row", axis=0, tiled=True)
    left_cols = lax.all_gather(left_basis, "col", axis=0, tiled=True)
    right_cols = lax.all_gather(right_basis, "row", axis=0, tiled=True)
    left_rotated = lax.all_gather(contract_first(left_cols, columns).astype(BF16), "col", axis=1, tiled=True)
    product = contract_last(columns, gradient).astype(BF16)
    product = lax.psum_scatter(product, "col", scatter_dimension=0, tiled=True).astype(F32)
    left_next = 0.95 * left_stat + 0.05 * product
    rotated = jnp.dot(left_rotated, right_cols, preferred_element_type=F32)
    first_next, second_next, normalized = moments(rotated, first_moment, second_moment)
    back = jnp.dot(left_cols, normalized, preferred_element_type=F32).astype(BF16)
    back = lax.psum_scatter(back, "row", scatter_dimension=0, tiled=True)
    direction = contract_last(back, right_cols).astype(BF16)
    direction = lax.psum_scatter(direction, "col", scatter_dimension=1, tiled=True)
    return (left_next, first_next, second_next, direction)


def solution(mesh):
    on_line = mesh.shape["row"] == 4 and mesh.shape["col"] == 8
    return jax.shard_map(
        body_on_line if on_line else body,
        mesh=mesh,
        in_specs=(
            P("row", "col"),
            P("col", "row"),
            P("col", "row"),
            P("row", "col"),
            P("row", "col"),
            P("row", "col"),
        ),
        out_specs=(P("col", "row"), P("row", "col"), P("row", "col"), P("row", "col")),
        check_vma=False,
    )
```

```python
import jax
import jax.numpy as jnp
from jax import lax
from jax.experimental import pallas as pl
from jax.experimental.pallas import tpu as pltpu
from jax.sharding import PartitionSpec as P

BF16 = jnp.bfloat16
F32 = jnp.float32
VMEM = 40 * 2**20
QUICK = pl.CostEstimate(flops=2**20, bytes_accessed=2**16, transcendentals=0)

PAIRS = [(0, 1), (1, 0), (2, 3), (3, 2)]
MIDDLE = [(1, 2), (2, 1)]
OUTWARD = [(1, 0), (2, 3)]
INWARD = [(0, 1), (3, 2)]
MIRROR = [(0, 3), (1, 2), (2, 1), (3, 0)]
RELAY = [(0, 2), (1, 0), (2, 3), (3, 1)]
RELAY_BACK = [(0, 1), (1, 3), (2, 0), (3, 2)]


def contract_last(first, second):
    return lax.dot_general(first, second, (((1,), (1,)), ((), ())), preferred_element_type=F32)


def contract_first(first, second):
    return lax.dot_general(first, second, (((0,), (0,)), ((), ())), preferred_element_type=F32)


def together(operands, *earlier):
    return lax.optimization_barrier(tuple(operands) + earlier)[: len(operands)]


def after(x, *earlier):
    return together([x], *earlier)[0]


def joined(keep_order, first, second):
    return jnp.where(keep_order, jnp.concatenate([first, second]), jnp.concatenate([second, first]))


def halves(keep_order, x):
    n = x.shape[0] // 2
    return jnp.where(keep_order, x[:n], x[n:]), jnp.where(keep_order, x[n:], x[:n])


class Line:
    def __init__(self, axis):
        self.axis = axis
        self.i = lax.axis_index(axis)
        self.even = self.i % 2 == 0
        self.lower = self.i < 2
        self.inner = (self.i == 1) | (self.i == 2)

    def send(self, x, pairs):
        return lax.ppermute(x, self.axis, pairs)

    def near(self, x, got):
        return joined(self.even, x, got)

    def whole(self, near, middle, out):
        return joined(self.lower, near, jnp.where(self.inner, middle, out))

    def placed(self, whole, piece, bits):
        return lax.dynamic_update_slice(whole, piece, ((self.i ^ bits) * piece.shape[0], 0))

    def block(self, x, bits):
        n = x.shape[0] // 4
        return lax.dynamic_slice_in_dim(x, (self.i ^ bits) * n, n, 0)

    def scatter_start(self, x):
        near, far = halves(self.lower, x)
        return near, far, self.send(far, INWARD)

    def scatter_end(self, near, through):
        got = self.send(through, MIDDLE)
        mine, other = halves(self.even, near.astype(F32) + got.astype(F32))
        got = self.send(other.astype(near.dtype), PAIRS)
        return (mine + got.astype(F32)).astype(near.dtype)

    def scatter_fast(self, x):
        relay = self.send(self.block(x, 2), RELAY_BACK)
        near = self.send(self.block(x, 1), PAIRS)
        mirror = add(self.block(x, 3), jnp.where(self.inner, relay, 0))
        mirror = self.send(mirror, MIRROR)
        total = self.block(x, 0).astype(F32) + near.astype(F32) + jnp.where(self.inner, 0, relay).astype(F32)
        return (total + mirror.astype(F32)).astype(x.dtype), relay


def add(first, second):
    return (first.astype(F32) + second.astype(F32)).astype(first.dtype)


def products_kernel(rows_ref, right_ref, out_ref):
    out_ref[...] = contract_last(rows_ref[...], right_ref[...]).astype(out_ref.dtype)


def products(rows, right, start, count):
    height, depth = rows.shape
    width = right.shape[0] // 8
    return pl.pallas_call(
        products_kernel,
        grid=(count,),
        in_specs=[
            pl.BlockSpec((height, depth), lambda b: (0, 0)),
            pl.BlockSpec((width, depth), lambda b: (start + b, 0)),
        ],
        out_specs=pl.BlockSpec((height, width), lambda b: (0, b)),
        out_shape=jax.ShapeDtypeStruct((height, count * width), rows.dtype),
        compiler_params=pltpu.CompilerParams(vmem_limit_bytes=VMEM),
        cost_estimate=QUICK,
    )(rows, right)


def scatter_columns(rows, right_rel, axis):
    def swap(x, bit):
        return lax.ppermute(x, axis, [(j, j ^ bit) for j in range(8)])

    width = right_rel.shape[0] // 8
    height = rows.shape[0] // 2
    low, high = slice(0, height // 2), slice(height // 2, height)

    def pair_sum(part):
        away = products(part, right_rel, 4, 4)
        got = swap(away, 1)
        return add(products(after(part, away), right_rel, 0, 4), got)

    def block(x, b, rows):
        return x[rows, b * width : (b + 1) * width]

    def first_sends(x):
        return [
            jnp.concatenate([block(x, 1, low), block(x, 3, low)], axis=1),
            jnp.concatenate([block(x, 2, high), block(x, 3, high)], axis=1),
        ]

    def second_sends(x, by_x, by_y):
        return [add(block(x, 2, low), by_x[:, width:]), add(block(x, 1, high), by_y[:, width:])]

    def sums(x, by_x, by_y, then_y, then_x):
        total = lambda a, b, c: a.astype(F32) + b[:, :width].astype(F32) + c.astype(F32)
        return [total(block(x, 0, low), by_x, then_y), total(block(x, 0, high), by_y, then_x)]

    sum0 = pair_sum(rows[:height])
    by_x0, by_y0 = together(first_sends(sum0))
    by_x0, by_y0 = swap(by_x0, 2), swap(by_y0, 4)
    sum1 = pair_sum(after(rows[height:], sum0))
    then_y0, then_x0, by_x1, by_y1 = together(second_sends(sum0, by_x0, by_y0) + first_sends(sum1))
    then_y0, then_x0 = swap(then_y0, 4), swap(then_x0, 2)
    by_x1, by_y1 = swap(by_x1, 2), swap(by_y1, 4)
    then_y1, then_x1 = together(second_sends(sum1, by_x1, by_y1))
    then_y1, then_x1 = swap(then_y1, 4), swap(then_x1, 2)
    kept = sums(sum0, by_x0, by_y0, then_y0, then_x0) + sums(sum1, by_x1, by_y1, then_y1, then_x1)
    return jnp.concatenate(kept).astype(rows.dtype)


def moments(rotated, first_moment, second_moment):
    first_next = 0.9 * first_moment + 0.1 * rotated
    second_next = 0.95 * second_moment + 0.05 * rotated * rotated
    scaled_first = first_next / (1.0 - 0.9**10)
    scaled_second = second_next / (1.0 - 0.95**10)
    normalized = (scaled_first / (jnp.sqrt(scaled_second) + 1e-08)).astype(BF16)
    return first_next, second_next, normalized


STEPS = 2


def part_kernel(place, left, near, middle, out, first, second, basis, *rest):
    first_out, second_out, back, total, normalized = rest[-5:]
    step = pl.program_id(0)

    @pl.when(step == 0)
    def _():
        total[...] = jnp.zeros_like(total)

    def accumulate(right):
        depth = left.shape[2]
        for b in range(left.shape[0]):
            total[...] += jnp.dot(left[b], right[b * depth : (b + 1) * depth, :], preferred_element_type=F32)

    @pl.when(step < STEPS)
    def _():
        accumulate(near)

    far = (step >= STEPS) & (step < 2 * STEPS)

    @pl.when(far & (place[2] == 1))
    def _():
        accumulate(middle)

    @pl.when(far & (place[2] == 0))
    def _():
        accumulate(out)

    @pl.when(step == 2 * STEPS - 1)
    def _():
        first_out[...], second_out[...], normalized[...] = moments(total[...], first[...], second[...])

    @pl.when(step >= 2 * STEPS)
    def _():
        back[...] = jnp.dot(basis[...], normalized[...], preferred_element_type=F32).astype(BF16)


def part(number, place, left_rotated, near, middle, out, first_moment, second_moment, left_cols, before):
    height, width = first_moment.shape
    size = near.shape[1]
    deep = near.shape[0] // STEPS
    tall = left_cols.shape[0] // 2
    near_step = lambda s: jnp.minimum(s, STEPS - 1)
    far_step = lambda s: jnp.clip(s - STEPS, 0, STEPS - 1)
    last_step = lambda s: jnp.maximum(s - 2 * STEPS, 0)

    def left_block(s, place):
        return jnp.where(s < STEPS, place[0] + near_step(s), place[1] + far_step(s)), 0, 0

    moment = pl.BlockSpec((height, size), lambda s, place: (0, number))
    before = list(before)
    return pl.pallas_call(
        part_kernel,
        grid_spec=pltpu.PrefetchScalarGridSpec(
            num_scalar_prefetch=1,
            grid=(2 * STEPS + 2,),
            in_specs=[
                pl.BlockSpec((4 // STEPS, height, width), left_block),
                pl.BlockSpec((deep, size), lambda s, place: (near_step(s), 0)),
                pl.BlockSpec((deep, size), lambda s, place: (far_step(s) * place[2], 0)),
                pl.BlockSpec((deep, size), lambda s, place: (far_step(s) * (1 - place[2]), 0)),
                moment,
                moment,
                pl.BlockSpec((tall, height), lambda s, place: (last_step(s), 0)),
            ]
            + [pl.BlockSpec(memory_space=pl.ANY)] * len(before),
            out_specs=[moment, moment, pl.BlockSpec((tall, size), lambda s, place: (last_step(s), 0))],
            scratch_shapes=[pltpu.VMEM((height, size), F32), pltpu.VMEM((height, size), BF16)],
        ),
        out_shape=[
            jax.ShapeDtypeStruct((height, width), F32),
            jax.ShapeDtypeStruct((height, width), F32),
            jax.ShapeDtypeStruct((left_cols.shape[0], size), BF16),
        ],
        input_output_aliases={8: 0, 9: 1} if before else {},
        compiler_params=pltpu.CompilerParams(vmem_limit_bytes=VMEM),
        cost_estimate=QUICK,
    )(place, left_rotated, near, middle, out, first_moment, second_moment, left_cols, *before)


def body_on_line(gradient, left_stat, left_basis, right_basis, first_moment, second_moment):
    line = Line("row")
    send = line.send
    height, width = gradient.shape
    cuts = [slice(p * width // 3, (p + 1) * width // 3) for p in range(3)]
    left_cols = lax.all_gather(left_basis, "col", axis=0, tiled=True)
    own0, own1, own2 = [right_basis[:, cut] for cut in cuts]

    mirror = send(gradient, MIRROR)
    pair = send(gradient, PAIRS)
    relay = send(after(jnp.where(line.inner, mirror, gradient), pair), RELAY)
    turn = lambda x, bits: contract_first(line.block(left_cols, bits), x)
    left_sum = turn(gradient, 0) + turn(pair, 1) + turn(mirror, 3)
    pair0 = send(after(own0, left_sum), PAIRS)

    near0, own1 = together([line.near(own0, pair0), own1])
    middle0 = send(near0, MIDDLE)
    pair1 = send(own1, PAIRS)
    near1 = line.near(own1, pair1)
    pair2 = send(after(own2, near1), PAIRS)

    left_part = (left_sum + turn(after(relay, near0), 2)).astype(BF16)
    left_rotated = lax.all_gather(left_part, "col")

    middle0, near1 = together([middle0, near1], left_part, pair2)
    out0 = send(middle0, OUTWARD)
    middle1 = send(near1, MIDDLE)
    columns = jnp.zeros((4 * height, width), BF16)
    for bits, piece in zip((0, 1, 3, 2), together([gradient, pair, mirror, relay], left_part)):
        columns = line.placed(columns, piece, bits)
    product_here = contract_last(columns, gradient).astype(BF16)
    left_rotated, product = together([left_rotated, product_here])
    product = lax.psum_scatter(product, "col", scatter_dimension=0, tiled=True).astype(F32)
    left_next = 0.95 * left_stat + 0.05 * product

    middle1, near2 = together([middle1, line.near(own2, pair2)], out0, product_here)
    out1 = send(middle1, OUTWARD)
    middle2 = send(near2, MIDDLE)

    steps = jnp.where(line.lower, jnp.array([0, STEPS]), jnp.array([STEPS, 0]))
    place = jnp.concatenate([steps, line.inner[None]]).astype(jnp.int32)

    def next_part(number, near, middle, out, before):
        *before, back = part(
            number, place, left_rotated, near, middle, out, first_moment, second_moment, left_cols, before
        )
        return before, back

    moments0, back0 = next_part(0, near0, middle0, after(out0, near2), ())
    back0, far0, sent0 = line.scatter_start(back0)
    out2 = send(after(middle2, out1, far0), OUTWARD)
    moments1, back1 = next_part(1, near1, middle1, after(out1, far0), moments0)
    back1, far1, sent1 = line.scatter_start(after(back1, sent0))
    through0 = add(far0, sent0)
    moments2, back2 = next_part(2, near2, middle2, after(out2, through0, far1), moments1)
    turned2, relayed = line.scatter_fast(after(back2, sent1))
    turned0 = line.scatter_end(back0, through0)
    turned1 = line.scatter_end(back1, add(far1, sent1))
    first_next, second_next = moments2

    near0, near1, near2, middle0, middle1, middle2, out0, out1, out2 = together(
        [near0, near1, near2, middle0, middle1, middle2, out0, out1, out2], relayed
    )
    right0 = line.whole(near0, middle0, out0)
    right1 = line.whole(near1, middle1, out1)
    right2 = line.whole(near2, middle2, out2)
    i = lax.axis_index("col")
    right_cols = after(jnp.concatenate([right0, right1, right2], axis=1), left_next)
    blocks = [lax.dynamic_slice_in_dim(right_cols, (i ^ r) * width, width, 0) for r in (0, 2, 4, 6, 1, 3, 5, 7)]
    turned = jnp.concatenate([turned0, turned1, turned2], axis=1)
    direction = scatter_columns(turned, jnp.concatenate(blocks), "col")
    return (left_next, first_next, second_next, direction)


def body(gradient, left_stat, left_basis, right_basis, first_moment, second_moment):
    columns = lax.all_gather(gradient, "row", axis=0, tiled=True)
    left_cols = lax.all_gather(left_basis, "col", axis=0, tiled=True)
    right_cols = lax.all_gather(right_basis, "row", axis=0, tiled=True)
    left_rotated = lax.all_gather(contract_first(left_cols, columns).astype(BF16), "col", axis=1, tiled=True)
    product = contract_last(columns, gradient).astype(BF16)
    product = lax.psum_scatter(product, "col", scatter_dimension=0, tiled=True).astype(F32)
    left_next = 0.95 * left_stat + 0.05 * product
    rotated = jnp.dot(left_rotated, right_cols, preferred_element_type=F32)
    first_next, second_next, normalized = moments(rotated, first_moment, second_moment)
    back = jnp.dot(left_cols, normalized, preferred_element_type=F32).astype(BF16)
    back = lax.psum_scatter(back, "row", scatter_dimension=0, tiled=True)
    direction = contract_last(back, right_cols).astype(BF16)
    direction = lax.psum_scatter(direction, "col", scatter_dimension=1, tiled=True)
    return (left_next, first_next, second_next, direction)


def solution(mesh):
    on_line = mesh.shape["row"] == 4 and mesh.shape["col"] == 8
    return jax.shard_map(
        body_on_line if on_line else body,
        mesh=mesh,
        in_specs=(
            P("row", "col"),
            P("col", "row"),
            P("col", "row"),
            P("row", "col"),
            P("row", "col"),
            P("row", "col"),
        ),
        out_specs=(P("col", "row"), P("row", "col"), P("row", "col"), P("row", "col")),
        check_vma=False,
    )
```

```python
import jax
import jax.numpy as jnp
from jax import lax
from jax.experimental import pallas as pl
from jax.experimental.pallas import tpu as pltpu
from jax.sharding import PartitionSpec as P

BF16 = jnp.bfloat16
F32 = jnp.float32
VMEM = 40 * 2**20
QUICK = pl.CostEstimate(flops=2**20, bytes_accessed=2**16, transcendentals=0)

PAIRS = [(0, 1), (1, 0), (2, 3), (3, 2)]
MIDDLE = [(1, 2), (2, 1)]
OUTWARD = [(1, 0), (2, 3)]
INWARD = [(0, 1), (3, 2)]
MIRROR = [(0, 3), (1, 2), (2, 1), (3, 0)]
RELAY = [(0, 2), (1, 0), (2, 3), (3, 1)]
RELAY_BACK = [(0, 1), (1, 3), (2, 0), (3, 2)]


def contract_last(first, second):
    return lax.dot_general(first, second, (((1,), (1,)), ((), ())), preferred_element_type=F32)


def contract_first(first, second):
    return lax.dot_general(first, second, (((0,), (0,)), ((), ())), preferred_element_type=F32)


def together(operands, *earlier):
    return lax.optimization_barrier(tuple(operands) + earlier)[: len(operands)]


def after(x, *earlier):
    return together([x], *earlier)[0]


def joined(keep_order, first, second):
    return jnp.where(keep_order, jnp.concatenate([first, second]), jnp.concatenate([second, first]))


def halves(keep_order, x):
    n = x.shape[0] // 2
    return jnp.where(keep_order, x[:n], x[n:]), jnp.where(keep_order, x[n:], x[:n])


class Line:
    def __init__(self, axis):
        self.axis = axis
        self.i = lax.axis_index(axis)
        self.even = self.i % 2 == 0
        self.lower = self.i < 2
        self.inner = (self.i == 1) | (self.i == 2)

    def send(self, x, pairs):
        return lax.ppermute(x, self.axis, pairs)

    def near(self, x, got):
        return joined(self.even, x, got)

    def whole(self, near, middle, out):
        return joined(self.lower, near, jnp.where(self.inner, middle, out))

    def placed(self, whole, piece, bits):
        return lax.dynamic_update_slice(whole, piece, ((self.i ^ bits) * piece.shape[0], 0))

    def block(self, x, bits):
        n = x.shape[0] // 4
        return lax.dynamic_slice_in_dim(x, (self.i ^ bits) * n, n, 0)


def add(first, second):
    return (first.astype(F32) + second.astype(F32)).astype(first.dtype)


def products_kernel(order, *refs):
    parts = len(refs) // 2
    total = sum(contract_last(rows[...], right[...]) for rows, right in zip(refs[:parts], refs[parts:]))
    refs[-1][...] = total.astype(refs[-1].dtype)


def products(rows, half, right, order, start):
    height, depth = rows[0].shape[0] // 2, rows[0].shape[1]
    width = right[0].shape[0] // 8
    return pl.pallas_call(
        products_kernel,
        grid_spec=pltpu.PrefetchScalarGridSpec(
            num_scalar_prefetch=1,
            grid=(4,),
            in_specs=[pl.BlockSpec((height, depth), lambda b, order: (half, 0))] * len(rows)
            + [pl.BlockSpec((width, depth), lambda b, order: (order[start + b], 0))] * len(right),
            out_specs=pl.BlockSpec((height, width), lambda b, order: (0, b)),
        ),
        out_shape=jax.ShapeDtypeStruct((height, 4 * width), rows[0].dtype),
        compiler_params=pltpu.CompilerParams(vmem_limit_bytes=VMEM),
        cost_estimate=QUICK,
    )(order, *rows, *right)


def scatter_columns(rows, right, axis):
    def swap(x, bit):
        return lax.ppermute(x, axis, [(j, j ^ bit) for j in range(8)])

    order = lax.axis_index(axis) ^ jnp.array([0, 2, 4, 6, 1, 3, 5, 7], jnp.int32)
    width = right[0].shape[0] // 8
    height = rows[0].shape[0] // 2
    low, high = slice(0, height // 2), slice(height // 2, height)

    def pair_sum(half, rows):
        away = products(rows, half, right, order, 4)
        got = swap(away, 1)
        return add(products(together(rows, away), half, right, order, 0), got)

    def block(x, b, rows):
        return x[rows, b * width : (b + 1) * width]

    def first_sends(x):
        return [
            jnp.concatenate([block(x, 1, low), block(x, 3, low)], axis=1),
            jnp.concatenate([block(x, 2, high), block(x, 3, high)], axis=1),
        ]

    def second_sends(x, by_x, by_y):
        return [add(block(x, 2, low), by_x[:, width:]), add(block(x, 1, high), by_y[:, width:])]

    def sums(x, by_x, by_y, then_y, then_x):
        total = lambda a, b, c: a.astype(F32) + b[:, :width].astype(F32) + c.astype(F32)
        return [total(block(x, 0, low), by_x, then_y), total(block(x, 0, high), by_y, then_x)]

    sum0 = pair_sum(0, rows)
    by_x0, by_y0 = together(first_sends(sum0))
    by_x0, by_y0 = swap(by_x0, 2), swap(by_y0, 4)
    sum1 = pair_sum(1, together(rows, sum0))
    then_y0, then_x0, by_x1, by_y1 = together(
        second_sends(sum0, *together([by_x0, by_y0], sum1)) + first_sends(sum1)
    )
    then_y0, then_x0 = swap(then_y0, 4), swap(then_x0, 2)
    by_x1, by_y1 = swap(by_x1, 2), swap(by_y1, 4)
    then_y1, then_x1 = together(second_sends(sum1, by_x1, by_y1))
    then_y1, then_x1 = swap(then_y1, 4), swap(then_x1, 2)
    kept = sums(sum0, by_x0, by_y0, then_y0, then_x0) + sums(sum1, by_x1, by_y1, then_y1, then_x1)
    return jnp.concatenate(kept).astype(sum0.dtype)


def moments(rotated, first_moment, second_moment):
    first_next = 0.9 * first_moment + 0.1 * rotated
    second_next = 0.95 * second_moment + 0.05 * rotated * rotated
    scaled_first = first_next / (1.0 - 0.9**10)
    scaled_second = second_next / (1.0 - 0.95**10)
    normalized = (scaled_first / (jnp.sqrt(scaled_second) + 1e-08)).astype(BF16)
    return first_next, second_next, normalized


STEPS = 2


def part_kernel(place, left, near, middle, out, first, second, basis, *rest):
    first_out, second_out, back, total, normalized = rest[-5:]
    step = pl.program_id(0)

    @pl.when(step == 0)
    def _():
        total[...] = jnp.zeros_like(total)

    def accumulate(right):
        depth = left.shape[2]
        for b in range(left.shape[0]):
            total[...] += jnp.dot(left[b], right[b * depth : (b + 1) * depth, :], preferred_element_type=F32)

    @pl.when(step < STEPS)
    def _():
        accumulate(near)

    far = (step >= STEPS) & (step < 2 * STEPS)

    @pl.when(far & (place[2] == 1))
    def _():
        accumulate(middle)

    @pl.when(far & (place[2] == 0))
    def _():
        accumulate(out)

    @pl.when(step == 2 * STEPS - 1)
    def _():
        first_out[...], second_out[...], normalized[...] = moments(total[...], first[...], second[...])

    @pl.when(step >= 2 * STEPS)
    def _():
        back[...] = jnp.dot(basis[...], normalized[...], preferred_element_type=F32).astype(BF16)


def part(number, place, left_rotated, near, middle, out, first_moment, second_moment, left_cols, before):
    height, width = first_moment.shape
    size = near.shape[1]
    deep = near.shape[0] // STEPS
    tall = left_cols.shape[0] // 2
    near_step = lambda s: jnp.minimum(s, STEPS - 1)
    far_step = lambda s: jnp.clip(s - STEPS, 0, STEPS - 1)
    last_step = lambda s: jnp.maximum(s - 2 * STEPS, 0)

    def left_block(s, place):
        return jnp.where(s < STEPS, place[0] + near_step(s), place[1] + far_step(s)), 0, 0

    moment = pl.BlockSpec((height, size), lambda s, place: (0, number))
    before = list(before)
    return pl.pallas_call(
        part_kernel,
        grid_spec=pltpu.PrefetchScalarGridSpec(
            num_scalar_prefetch=1,
            grid=(2 * STEPS + 2,),
            in_specs=[
                pl.BlockSpec((4 // STEPS, height, width), left_block),
                pl.BlockSpec((deep, size), lambda s, place: (near_step(s), 0)),
                pl.BlockSpec((deep, size), lambda s, place: (far_step(s) * place[2], 0)),
                pl.BlockSpec((deep, size), lambda s, place: (far_step(s) * (1 - place[2]), 0)),
                moment,
                moment,
                pl.BlockSpec((tall, height), lambda s, place: (last_step(s), 0)),
            ]
            + [pl.BlockSpec(memory_space=pl.ANY)] * len(before),
            out_specs=[moment, moment, pl.BlockSpec((tall, size), lambda s, place: (last_step(s), 0))],
            scratch_shapes=[pltpu.VMEM((height, size), F32), pltpu.VMEM((height, size), BF16)],
        ),
        out_shape=[
            jax.ShapeDtypeStruct((height, width), F32),
            jax.ShapeDtypeStruct((height, width), F32),
            jax.ShapeDtypeStruct((left_cols.shape[0], size), BF16),
        ],
        input_output_aliases={8: 0, 9: 1} if before else {},
        compiler_params=pltpu.CompilerParams(vmem_limit_bytes=VMEM),
        cost_estimate=QUICK,
    )(place, left_rotated, near, middle, out, first_moment, second_moment, left_cols, *before)


def body_on_line(gradient, left_stat, left_basis, right_basis, first_moment, second_moment):
    line = Line("row")
    send = line.send
    height, width = gradient.shape
    cuts = [slice(p * width // 3, (p + 1) * width // 3) for p in range(3)]
    left_cols = lax.all_gather(left_basis, "col", axis=0, tiled=True)
    own0, own1, own2 = [right_basis[:, cut] for cut in cuts]

    mirror = send(gradient, MIRROR)
    pair = send(gradient, PAIRS)
    relay = send(after(jnp.where(line.inner, mirror, gradient), pair), RELAY)
    turn = lambda x, bits: contract_first(line.block(left_cols, bits), x)
    left_sum = turn(gradient, 0) + turn(pair, 1) + turn(mirror, 3)
    pair0 = send(after(own0, left_sum), PAIRS)

    near0, own1 = together([line.near(own0, pair0), own1])
    middle0 = send(near0, MIDDLE)
    pair1 = send(own1, PAIRS)
    near1 = line.near(own1, pair1)
    pair2 = send(after(own2, near1), PAIRS)

    left_part = (left_sum + turn(after(relay, near0), 2)).astype(BF16)
    left_rotated = lax.all_gather(left_part, "col")

    middle0, near1 = together([middle0, near1], left_part, pair2)
    out0 = send(middle0, OUTWARD)
    middle1 = send(near1, MIDDLE)
    columns = jnp.zeros((4 * height, width), BF16)
    for bits, piece in zip((0, 1, 3, 2), together([gradient, pair, mirror, relay], left_part)):
        columns = line.placed(columns, piece, bits)
    product_here = contract_last(columns, gradient).astype(BF16)
    left_rotated, product = together([left_rotated, product_here])
    product = lax.psum_scatter(product, "col", scatter_dimension=0, tiled=True).astype(F32)
    left_next = 0.95 * left_stat + 0.05 * product

    middle1, near2 = together([middle1, line.near(own2, pair2)], out0, product_here)
    out1 = send(middle1, OUTWARD)
    middle2 = send(near2, MIDDLE)

    steps = jnp.where(line.lower, jnp.array([0, STEPS]), jnp.array([STEPS, 0]))
    place = jnp.concatenate([steps, line.inner[None]]).astype(jnp.int32)

    def next_part(number, near, middle, out, before):
        *before, back = part(
            number, place, left_rotated, near, middle, out, first_moment, second_moment, left_cols, before
        )
        return before, back

    moments0, back0 = next_part(0, near0, middle0, after(out0, near2), ())
    stay0, far0 = halves(line.lower, back0)
    got0 = send(far0, INWARD)
    out2 = send(after(middle2, out1, far0), OUTWARD)
    moments1, back1 = next_part(1, near1, middle1, after(out1, far0), moments0)
    stay1, far1 = halves(line.lower, after(back1, got0))
    got1 = send(far1, INWARD)
    through0 = send(add(far0, after(got0, far1)), MIDDLE)
    right0 = line.whole(near0, middle0, after(out0, far1))
    right1 = line.whole(near1, middle1, after(out1, far1))
    mine0, other0 = halves(line.even, stay0.astype(F32) + through0.astype(F32))
    other0 = other0.astype(BF16)
    through1 = add(far1, got1)
    moments2, back2 = next_part(2, near2, middle2, after(out2, other0, through1, right0, right1), moments1)
    other0 = send(other0, PAIRS)
    turned0 = (mine0 + other0.astype(F32)).astype(BF16)
    through1 = send(through1, MIDDLE)
    mine1, other1 = halves(line.even, stay1.astype(F32) + through1.astype(F32))
    turned1 = (mine1 + send(other1.astype(BF16), PAIRS).astype(F32)).astype(BF16)
    first_next, second_next = moments2

    relay = send(line.block(back2, 2), RELAY_BACK)
    pair = send(line.block(back2, 1), PAIRS)
    relay = after(relay, through1, other0)
    mirror = send(add(line.block(back2, 3), jnp.where(line.inner, relay, 0)), MIRROR)
    right2 = line.whole(near2, middle2, after(out2, relay))
    mirror, pair = together([mirror, pair], right2, left_next)
    turned2 = line.block(back2, 0).astype(F32) + jnp.where(line.inner, 0, relay).astype(F32)
    turned2 = (turned2 + pair.astype(F32) + mirror.astype(F32)).astype(BF16)

    direction = scatter_columns([turned0, turned1, turned2], [right0, right1, right2], "col")
    return (left_next, first_next, second_next, direction)


def body(gradient, left_stat, left_basis, right_basis, first_moment, second_moment):
    columns = lax.all_gather(gradient, "row", axis=0, tiled=True)
    left_cols = lax.all_gather(left_basis, "col", axis=0, tiled=True)
    right_cols = lax.all_gather(right_basis, "row", axis=0, tiled=True)
    left_rotated = lax.all_gather(contract_first(left_cols, columns).astype(BF16), "col", axis=1, tiled=True)
    product = contract_last(columns, gradient).astype(BF16)
    product = lax.psum_scatter(product, "col", scatter_dimension=0, tiled=True).astype(F32)
    left_next = 0.95 * left_stat + 0.05 * product
    rotated = jnp.dot(left_rotated, right_cols, preferred_element_type=F32)
    first_next, second_next, normalized = moments(rotated, first_moment, second_moment)
    back = jnp.dot(left_cols, normalized, preferred_element_type=F32).astype(BF16)
    back = lax.psum_scatter(back, "row", scatter_dimension=0, tiled=True)
    direction = contract_last(back, right_cols).astype(BF16)
    direction = lax.psum_scatter(direction, "col", scatter_dimension=1, tiled=True)
    return (left_next, first_next, second_next, direction)


def solution(mesh):
    on_line = mesh.shape["row"] == 4 and mesh.shape["col"] == 8
    return jax.shard_map(
        body_on_line if on_line else body,
        mesh=mesh,
        in_specs=(
            P("row", "col"),
            P("col", "row"),
            P("col", "row"),
            P("row", "col"),
            P("row", "col"),
            P("row", "col"),
        ),
        out_specs=(P("col", "row"), P("row", "col"), P("row", "col"), P("row", "col")),
        check_vma=False,
    )
```

```python
import jax
import jax.numpy as jnp
from jax import lax
from jax.experimental import pallas as pl
from jax.experimental.pallas import tpu as pltpu
from jax.sharding import PartitionSpec as P

BF16 = jnp.bfloat16
F32 = jnp.float32
VMEM = 40 * 2**20
QUICK = pl.CostEstimate(flops=2**20, bytes_accessed=2**16, transcendentals=0)

PAIRS = [(0, 1), (1, 0), (2, 3), (3, 2)]
MIDDLE = [(1, 2), (2, 1)]
OUTWARD = [(1, 0), (2, 3)]
INWARD = [(0, 1), (3, 2)]
MIRROR = [(0, 3), (1, 2), (2, 1), (3, 0)]
RELAY = [(0, 2), (1, 0), (2, 3), (3, 1)]
RELAY_BACK = [(0, 1), (1, 3), (2, 0), (3, 2)]


def contract_last(first, second):
    return lax.dot_general(first, second, (((1,), (1,)), ((), ())), preferred_element_type=F32)


def contract_first(first, second):
    return lax.dot_general(first, second, (((0,), (0,)), ((), ())), preferred_element_type=F32)


def together(operands, *earlier):
    return lax.optimization_barrier(tuple(operands) + earlier)[: len(operands)]


def after(x, *earlier):
    return together([x], *earlier)[0]


def joined(keep_order, first, second):
    return jnp.where(keep_order, jnp.concatenate([first, second]), jnp.concatenate([second, first]))


def halves(keep_order, x):
    n = x.shape[0] // 2
    return jnp.where(keep_order, x[:n], x[n:]), jnp.where(keep_order, x[n:], x[:n])


class Line:
    def __init__(self, axis):
        self.axis = axis
        self.i = lax.axis_index(axis)
        self.even = self.i % 2 == 0
        self.lower = self.i < 2
        self.inner = (self.i == 1) | (self.i == 2)

    def send(self, x, pairs):
        return lax.ppermute(x, self.axis, pairs)

    def near(self, x, got):
        return joined(self.even, x, got)

    def whole(self, near, middle, out):
        return joined(self.lower, near, jnp.where(self.inner, middle, out))

    def placed(self, whole, piece, bits):
        return lax.dynamic_update_slice(whole, piece, ((self.i ^ bits) * piece.shape[0], 0))

    def block(self, x, bits):
        n = x.shape[0] // 4
        return lax.dynamic_slice_in_dim(x, (self.i ^ bits) * n, n, 0)


def add(first, second):
    return (first.astype(F32) + second.astype(F32)).astype(first.dtype)


def products_kernel(order, *refs):
    parts = len(refs) // 2
    total = sum(contract_last(rows[...], right[...]) for rows, right in zip(refs[:parts], refs[parts:]))
    refs[-1][...] = total.astype(refs[-1].dtype)


def products(rows, half, right, order, start):
    height, depth = rows[0].shape[0] // 2, rows[0].shape[1]
    width = right[0].shape[0] // 8
    return pl.pallas_call(
        products_kernel,
        grid_spec=pltpu.PrefetchScalarGridSpec(
            num_scalar_prefetch=1,
            grid=(4,),
            in_specs=[pl.BlockSpec((height, depth), lambda b, order: (half, 0))] * len(rows)
            + [pl.BlockSpec((width, depth), lambda b, order: (order[start + b], 0))] * len(right),
            out_specs=pl.BlockSpec((height, width), lambda b, order: (0, b)),
        ),
        out_shape=jax.ShapeDtypeStruct((height, 4 * width), rows[0].dtype),
        compiler_params=pltpu.CompilerParams(vmem_limit_bytes=VMEM),
        cost_estimate=QUICK,
    )(order, *rows, *right)


def scatter_columns(rows, right, axis):
    def swap(x, bit):
        return lax.ppermute(x, axis, [(j, j ^ bit) for j in range(8)])

    order = lax.axis_index(axis) ^ jnp.array([0, 2, 4, 6, 1, 3, 5, 7], jnp.int32)
    width = right[0].shape[0] // 8
    height = rows[0].shape[0] // 2
    low, high = slice(0, height // 2), slice(height // 2, height)

    def pair_sum(half, rows):
        away = products(rows, half, right, order, 4)
        got = swap(away, 1)
        return add(products(together(rows, away), half, right, order, 0), got)

    def block(x, b, rows):
        return x[rows, b * width : (b + 1) * width]

    def first_sends(x):
        return [
            jnp.concatenate([block(x, 1, low), block(x, 3, low)], axis=1),
            jnp.concatenate([block(x, 2, high), block(x, 3, high)], axis=1),
        ]

    def second_sends(x, by_x, by_y):
        return [add(block(x, 2, low), by_x[:, width:]), add(block(x, 1, high), by_y[:, width:])]

    def sums(x, by_x, by_y, then_y, then_x):
        total = lambda a, b, c: a.astype(F32) + b[:, :width].astype(F32) + c.astype(F32)
        return [total(block(x, 0, low), by_x, then_y), total(block(x, 0, high), by_y, then_x)]

    sum0 = pair_sum(0, rows)
    by_x0, by_y0 = together(first_sends(sum0))
    by_x0, by_y0 = swap(by_x0, 2), swap(by_y0, 4)
    sum1 = pair_sum(1, together(rows, sum0))
    then_y0, then_x0, by_x1, by_y1 = together(
        second_sends(sum0, *together([by_x0, by_y0], sum1)) + first_sends(sum1)
    )
    then_y0, then_x0 = swap(then_y0, 4), swap(then_x0, 2)
    by_x1, by_y1 = swap(by_x1, 2), swap(by_y1, 4)
    then_y1, then_x1 = together(second_sends(sum1, by_x1, by_y1))
    then_y1, then_x1 = swap(then_y1, 4), swap(then_x1, 2)
    kept = sums(sum0, by_x0, by_y0, then_y0, then_x0) + sums(sum1, by_x1, by_y1, then_y1, then_x1)
    return jnp.concatenate(kept).astype(sum0.dtype)


def moments(rotated, first_moment, second_moment):
    first_next = 0.9 * first_moment + 0.1 * rotated
    second_next = 0.95 * second_moment + 0.05 * rotated * rotated
    scaled_first = first_next / (1.0 - 0.9**10)
    scaled_second = second_next / (1.0 - 0.95**10)
    normalized = (scaled_first / (jnp.sqrt(scaled_second) + 1e-08)).astype(BF16)
    return first_next, second_next, normalized


STEPS = 2


def part_kernel(place, left, near, middle, out, first, second, basis, *rest):
    first_out, second_out, back, total, normalized = rest[-5:]
    step = pl.program_id(0)

    @pl.when(step == 0)
    def _():
        total[...] = jnp.zeros_like(total)

    def accumulate(right):
        depth = left.shape[2]
        for b in range(left.shape[0]):
            total[...] += jnp.dot(left[b], right[b * depth : (b + 1) * depth, :], preferred_element_type=F32)

    @pl.when(step < STEPS)
    def _():
        accumulate(near)

    far = (step >= STEPS) & (step < 2 * STEPS)

    @pl.when(far & (place[2] == 1))
    def _():
        accumulate(middle)

    @pl.when(far & (place[2] == 0))
    def _():
        accumulate(out)

    @pl.when(step == 2 * STEPS - 1)
    def _():
        first_out[...], second_out[...], normalized[...] = moments(total[...], first[...], second[...])

    @pl.when(step >= 2 * STEPS)
    def _():
        back[...] = jnp.dot(basis[...], normalized[...], preferred_element_type=F32).astype(BF16)


def part(number, place, left_rotated, near, middle, out, first_moment, second_moment, left_cols, before):
    height, width = first_moment.shape
    size = near.shape[1]
    deep = near.shape[0] // STEPS
    tall = left_cols.shape[0] // 2
    near_step = lambda s: jnp.minimum(s, STEPS - 1)
    far_step = lambda s: jnp.clip(s - STEPS, 0, STEPS - 1)
    last_step = lambda s: jnp.maximum(s - 2 * STEPS, 0)

    def left_block(s, place):
        return jnp.where(s < STEPS, place[0] + near_step(s), place[1] + far_step(s)), 0, 0

    moment = pl.BlockSpec((height, size), lambda s, place: (0, number))
    before = list(before)
    return pl.pallas_call(
        part_kernel,
        grid_spec=pltpu.PrefetchScalarGridSpec(
            num_scalar_prefetch=1,
            grid=(2 * STEPS + 2,),
            in_specs=[
                pl.BlockSpec((4 // STEPS, height, width), left_block),
                pl.BlockSpec((deep, size), lambda s, place: (near_step(s), 0)),
                pl.BlockSpec((deep, size), lambda s, place: (far_step(s) * place[2], 0)),
                pl.BlockSpec((deep, size), lambda s, place: (far_step(s) * (1 - place[2]), 0)),
                moment,
                moment,
                pl.BlockSpec((tall, height), lambda s, place: (last_step(s), 0)),
            ]
            + [pl.BlockSpec(memory_space=pl.ANY)] * len(before),
            out_specs=[moment, moment, pl.BlockSpec((tall, size), lambda s, place: (last_step(s), 0))],
            scratch_shapes=[pltpu.VMEM((height, size), F32), pltpu.VMEM((height, size), BF16)],
        ),
        out_shape=[
            jax.ShapeDtypeStruct((height, width), F32),
            jax.ShapeDtypeStruct((height, width), F32),
            jax.ShapeDtypeStruct((left_cols.shape[0], size), BF16),
        ],
        input_output_aliases={8: 0, 9: 1} if before else {},
        compiler_params=pltpu.CompilerParams(vmem_limit_bytes=VMEM),
        cost_estimate=QUICK,
    )(place, left_rotated, near, middle, out, first_moment, second_moment, left_cols, *before)


def body_on_line(gradient, left_stat, left_basis, right_basis, first_moment, second_moment):
    line = Line("row")
    send = line.send
    height, width = gradient.shape
    cuts = [slice(p * width // 3, (p + 1) * width // 3) for p in range(3)]
    left_cols = lax.all_gather(left_basis, "col", axis=0, tiled=True)
    own0, own1, own2 = [right_basis[:, cut] for cut in cuts]

    mirror = send(gradient, MIRROR)
    pair = send(gradient, PAIRS)
    relay = send(after(jnp.where(line.inner, mirror, gradient), pair), RELAY)
    turn = lambda x, bits: contract_first(line.block(left_cols, bits), x)
    left_sum = turn(gradient, 0) + turn(pair, 1) + turn(mirror, 3)
    pair0 = send(after(own0, left_sum), PAIRS)

    near0, own1 = together([line.near(own0, pair0), own1])
    middle0 = send(near0, MIDDLE)
    pair1 = send(own1, PAIRS)
    near1 = line.near(own1, pair1)
    pair2 = send(after(own2, near1), PAIRS)

    left_part = (left_sum + turn(after(relay, near0), 2)).astype(BF16)
    left_rotated = lax.all_gather(left_part, "col")

    middle0, near1 = together([middle0, near1], left_part, pair2)
    out0 = send(middle0, OUTWARD)
    middle1 = send(near1, MIDDLE)
    columns = jnp.zeros((4 * height, width), BF16)
    for bits, piece in zip((0, 1, 3, 2), together([gradient, pair, mirror, relay], left_part)):
        columns = line.placed(columns, piece, bits)
    product_here = contract_last(columns, gradient).astype(BF16)
    product = lax.psum_scatter(after(product_here, out0), "col", scatter_dimension=0, tiled=True).astype(F32)
    left_next = 0.95 * left_stat + 0.05 * product

    middle1, near2 = together([middle1, line.near(own2, pair2)], out0, product_here)
    out1 = send(middle1, OUTWARD)
    middle2 = send(near2, MIDDLE)

    steps = jnp.where(line.lower, jnp.array([0, STEPS]), jnp.array([STEPS, 0]))
    place = jnp.concatenate([steps, line.inner[None]]).astype(jnp.int32)

    def next_part(number, near, middle, out, before):
        *before, back = part(
            number, place, left_rotated, near, middle, out, first_moment, second_moment, left_cols, before
        )
        return before, back

    moments0, back0 = next_part(0, near0, middle0, after(out0, near2), ())
    stay0, far0 = halves(line.lower, back0)
    got0 = send(far0, INWARD)
    out2 = send(after(middle2, out1, far0), OUTWARD)
    moments1, back1 = next_part(1, near1, middle1, after(out1, far0), moments0)
    stay1, far1 = halves(line.lower, after(back1, got0))
    got1 = send(far1, INWARD)
    through0 = send(add(far0, after(got0, far1)), MIDDLE)
    right0 = line.whole(near0, middle0, after(out0, far1))
    right1 = line.whole(near1, middle1, after(out1, far1))
    mine0, other0 = halves(line.even, stay0.astype(F32) + through0.astype(F32))
    other0 = other0.astype(BF16)
    through1 = add(far1, got1)
    moments2, back2 = next_part(2, near2, middle2, after(out2, other0, through1, right0, right1), moments1)
    other0 = send(other0, PAIRS)
    turned0 = (mine0 + other0.astype(F32)).astype(BF16)
    through1 = send(through1, MIDDLE)
    mine1, other1 = halves(line.even, stay1.astype(F32) + through1.astype(F32))
    turned1 = (mine1 + send(other1.astype(BF16), PAIRS).astype(F32)).astype(BF16)
    first_next, second_next = moments2

    relay = send(line.block(back2, 2), RELAY_BACK)
    pair = send(line.block(back2, 1), PAIRS)
    relay = after(relay, through1, other0)
    mirror = send(add(line.block(back2, 3), jnp.where(line.inner, relay, 0)), MIRROR)
    right2 = line.whole(near2, middle2, after(out2, relay))
    mirror, pair = together([mirror, pair], right2)
    turned2 = line.block(back2, 0).astype(F32) + jnp.where(line.inner, 0, relay).astype(F32)
    turned2 = (turned2 + pair.astype(F32) + mirror.astype(F32)).astype(BF16)

    right = together([right0, right1, right2], left_next)
    direction = scatter_columns([turned0, turned1, turned2], right, "col")
    return (left_next, first_next, second_next, direction)


def body(gradient, left_stat, left_basis, right_basis, first_moment, second_moment):
    columns = lax.all_gather(gradient, "row", axis=0, tiled=True)
    left_cols = lax.all_gather(left_basis, "col", axis=0, tiled=True)
    right_cols = lax.all_gather(right_basis, "row", axis=0, tiled=True)
    left_rotated = lax.all_gather(contract_first(left_cols, columns).astype(BF16), "col", axis=1, tiled=True)
    product = contract_last(columns, gradient).astype(BF16)
    product = lax.psum_scatter(product, "col", scatter_dimension=0, tiled=True).astype(F32)
    left_next = 0.95 * left_stat + 0.05 * product
    rotated = jnp.dot(left_rotated, right_cols, preferred_element_type=F32)
    first_next, second_next, normalized = moments(rotated, first_moment, second_moment)
    back = jnp.dot(left_cols, normalized, preferred_element_type=F32).astype(BF16)
    back = lax.psum_scatter(back, "row", scatter_dimension=0, tiled=True)
    direction = contract_last(back, right_cols).astype(BF16)
    direction = lax.psum_scatter(direction, "col", scatter_dimension=1, tiled=True)
    return (left_next, first_next, second_next, direction)


def solution(mesh):
    on_line = mesh.shape["row"] == 4 and mesh.shape["col"] == 8
    return jax.shard_map(
        body_on_line if on_line else body,
        mesh=mesh,
        in_specs=(
            P("row", "col"),
            P("col", "row"),
            P("col", "row"),
            P("row", "col"),
            P("row", "col"),
            P("row", "col"),
        ),
        out_specs=(P("col", "row"), P("row", "col"), P("row", "col"), P("row", "col")),
        check_vma=False,
    )
```

```python
import jax
import jax.numpy as jnp
from jax import lax
from jax.experimental import pallas as pl
from jax.experimental.pallas import tpu as pltpu
from jax.sharding import PartitionSpec as P

BF16 = jnp.bfloat16
F32 = jnp.float32
VMEM = 60 * 2**20
QUICK = pl.CostEstimate(flops=2**20, bytes_accessed=2**16, transcendentals=0)

PAIRS = [(0, 1), (1, 0), (2, 3), (3, 2)]
MIDDLE = [(1, 2), (2, 1)]
OUTWARD = [(1, 0), (2, 3)]
INWARD = [(0, 1), (3, 2)]
MIRROR = [(0, 3), (1, 2), (2, 1), (3, 0)]
RELAY = [(0, 2), (1, 0), (2, 3), (3, 1)]
RELAY_BACK = [(0, 1), (1, 3), (2, 0), (3, 2)]


def contract_last(first, second):
    return lax.dot_general(first, second, (((1,), (1,)), ((), ())), preferred_element_type=F32)


def contract_first(first, second):
    return lax.dot_general(first, second, (((0,), (0,)), ((), ())), preferred_element_type=F32)


def together(operands, *earlier):
    return lax.optimization_barrier(tuple(operands) + earlier)[: len(operands)]


def after(x, *earlier):
    return together([x], *earlier)[0]


def joined(keep_order, first, second):
    return jnp.where(keep_order, jnp.concatenate([first, second]), jnp.concatenate([second, first]))


def halves(keep_order, x):
    n = x.shape[0] // 2
    return jnp.where(keep_order, x[:n], x[n:]), jnp.where(keep_order, x[n:], x[:n])


class Line:
    def __init__(self, axis):
        self.axis = axis
        self.i = lax.axis_index(axis)
        self.even = self.i % 2 == 0
        self.lower = self.i < 2
        self.inner = (self.i == 1) | (self.i == 2)

    def send(self, x, pairs):
        return lax.ppermute(x, self.axis, pairs)

    def near(self, x, got):
        return joined(self.even, x, got)

    def whole(self, near, middle, out):
        return joined(self.lower, near, jnp.where(self.inner, middle, out))

    def placed(self, whole, piece, bits):
        return lax.dynamic_update_slice(whole, piece, ((self.i ^ bits) * piece.shape[0], 0))

    def block(self, x, bits):
        n = x.shape[0] // 4
        return lax.dynamic_slice_in_dim(x, (self.i ^ bits) * n, n, 0)


def add(first, second):
    return (first.astype(F32) + second.astype(F32)).astype(first.dtype)


def products_kernel(order, *refs):
    parts = len(refs) // 2
    total = sum(contract_last(rows[...], right[...]) for rows, right in zip(refs[:parts], refs[parts:]))
    refs[-1][...] = total.astype(refs[-1].dtype)


def products(rows, half, right, order, start):
    height, depth = rows[0].shape[0] // 2, rows[0].shape[1]
    width = right[0].shape[0] // 8
    return pl.pallas_call(
        products_kernel,
        grid_spec=pltpu.PrefetchScalarGridSpec(
            num_scalar_prefetch=1,
            grid=(4,),
            in_specs=[pl.BlockSpec((height, depth), lambda b, order: (half, 0))] * len(rows)
            + [pl.BlockSpec((width, depth), lambda b, order: (order[start + b], 0))] * len(right),
            out_specs=pl.BlockSpec((height, width), lambda b, order: (0, b)),
        ),
        out_shape=jax.ShapeDtypeStruct((height, 4 * width), rows[0].dtype),
        compiler_params=pltpu.CompilerParams(vmem_limit_bytes=VMEM // 2),
        cost_estimate=QUICK,
    )(order, *rows, *right)


def scatter_columns(rows, right, axis):
    def swap(x, bit):
        return lax.ppermute(x, axis, [(j, j ^ bit) for j in range(8)])

    order = lax.axis_index(axis) ^ jnp.array([0, 2, 4, 6, 1, 3, 5, 7], jnp.int32)
    width = right[0].shape[0] // 8
    height = rows[0].shape[0] // 2
    low, high = slice(0, height // 2), slice(height // 2, height)

    def pair_sum(half, rows):
        away = products(rows, half, right, order, 4)
        got = swap(away, 1)
        return add(products(together(rows, away), half, right, order, 0), got)

    def block(x, b, rows):
        return x[rows, b * width : (b + 1) * width]

    def first_sends(x):
        return [
            jnp.concatenate([block(x, 1, low), block(x, 3, low)], axis=1),
            jnp.concatenate([block(x, 2, high), block(x, 3, high)], axis=1),
        ]

    def second_sends(x, by_x, by_y):
        return [add(block(x, 2, low), by_x[:, width:]), add(block(x, 1, high), by_y[:, width:])]

    def sums(x, by_x, by_y, then_y, then_x):
        total = lambda a, b, c: a.astype(F32) + b[:, :width].astype(F32) + c.astype(F32)
        return [total(block(x, 0, low), by_x, then_y), total(block(x, 0, high), by_y, then_x)]

    sum0 = pair_sum(0, rows)
    by_x0, by_y0 = together(first_sends(sum0))
    by_x0, by_y0 = swap(by_x0, 2), swap(by_y0, 4)
    sum1 = pair_sum(1, together(rows, sum0))
    then_y0, then_x0, by_x1, by_y1 = together(
        second_sends(sum0, *together([by_x0, by_y0], sum1)) + first_sends(sum1)
    )
    then_y0, then_x0 = swap(then_y0, 4), swap(then_x0, 2)
    by_x1, by_y1 = swap(by_x1, 2), swap(by_y1, 4)
    then_y1, then_x1 = together(second_sends(sum1, by_x1, by_y1))
    then_y1, then_x1 = swap(then_y1, 4), swap(then_x1, 2)
    kept = sums(sum0, by_x0, by_y0, then_y0, then_x0) + sums(sum1, by_x1, by_y1, then_y1, then_x1)
    return jnp.concatenate(kept).astype(sum0.dtype)


def moments(rotated, first_moment, second_moment):
    first_next = 0.9 * first_moment + 0.1 * rotated
    second_next = 0.95 * second_moment + 0.05 * rotated * rotated
    scaled_first = first_next / (1.0 - 0.9**10)
    scaled_second = second_next / (1.0 - 0.95**10)
    normalized = (scaled_first / (jnp.sqrt(scaled_second) + 1e-08)).astype(BF16)
    return first_next, second_next, normalized


STEPS = 2


def part_kernel(place, left, near, middle, out, first, second, basis, *rest):
    first_out, second_out, back, total, normalized = rest[-5:]
    step = pl.program_id(0)

    @pl.when(step == 0)
    def _():
        total[...] = jnp.zeros_like(total)

    def accumulate(right):
        depth = left.shape[2]
        for b in range(left.shape[0]):
            total[...] += jnp.dot(left[b], right[b * depth : (b + 1) * depth, :], preferred_element_type=F32)

    @pl.when(step < STEPS)
    def _():
        accumulate(near)

    far = (step >= STEPS) & (step < 2 * STEPS)

    @pl.when(far & (place[2] == 1))
    def _():
        accumulate(middle)

    @pl.when(far & (place[2] == 0))
    def _():
        accumulate(out)

    @pl.when(step == 2 * STEPS - 1)
    def _():
        first_out[...], second_out[...], normalized[...] = moments(total[...], first[...], second[...])

    @pl.when(step >= 2 * STEPS)
    def _():
        back[...] = jnp.dot(basis[...], normalized[...], preferred_element_type=F32).astype(BF16)


def part(number, place, left_rotated, near, middle, out, first_moment, second_moment, left_cols, before):
    height, width = first_moment.shape
    size = near.shape[1]
    deep = near.shape[0] // STEPS
    tall = left_cols.shape[0] // 2
    near_step = lambda s: jnp.minimum(s, STEPS - 1)
    far_step = lambda s: jnp.clip(s - STEPS, 0, STEPS - 1)
    last_step = lambda s: jnp.maximum(s - 2 * STEPS, 0)

    def left_block(s, place):
        return jnp.where(s < STEPS, place[0] + near_step(s), place[1] + far_step(s)), 0, 0

    moment = pl.BlockSpec((height, size), lambda s, place: (0, number))
    before = list(before)
    return pl.pallas_call(
        part_kernel,
        grid_spec=pltpu.PrefetchScalarGridSpec(
            num_scalar_prefetch=1,
            grid=(2 * STEPS + 2,),
            in_specs=[
                pl.BlockSpec((4 // STEPS, height, width), left_block),
                pl.BlockSpec((deep, size), lambda s, place: (near_step(s), 0)),
                pl.BlockSpec((deep, size), lambda s, place: (far_step(s) * place[2], 0)),
                pl.BlockSpec((deep, size), lambda s, place: (far_step(s) * (1 - place[2]), 0)),
                moment,
                moment,
                pl.BlockSpec((tall, height), lambda s, place: (last_step(s), 0)),
            ]
            + [pl.BlockSpec(memory_space=pl.ANY)] * len(before),
            out_specs=[moment, moment, pl.BlockSpec((tall, size), lambda s, place: (last_step(s), 0))],
            scratch_shapes=[pltpu.VMEM((height, size), F32), pltpu.VMEM((height, size), BF16)],
        ),
        out_shape=[
            jax.ShapeDtypeStruct((height, width), F32),
            jax.ShapeDtypeStruct((height, width), F32),
            jax.ShapeDtypeStruct((left_cols.shape[0], size), BF16),
        ],
        input_output_aliases={8: 0, 9: 1} if before else {},
        compiler_params=pltpu.CompilerParams(vmem_limit_bytes=VMEM),
        cost_estimate=QUICK,
    )(place, left_rotated, near, middle, out, first_moment, second_moment, left_cols, *before)


def body_on_line(gradient, left_stat, left_basis, right_basis, first_moment, second_moment):
    line = Line("row")
    send = line.send
    height, width = gradient.shape
    cuts = [slice(p * width // 3, (p + 1) * width // 3) for p in range(3)]
    left_cols = lax.all_gather(left_basis, "col", axis=0, tiled=True)
    own0, own1, own2 = [right_basis[:, cut] for cut in cuts]

    mirror = send(gradient, MIRROR)
    pair = send(gradient, PAIRS)
    relay = send(after(jnp.where(line.inner, mirror, gradient), pair), RELAY)
    turn = lambda x, bits: contract_first(line.block(left_cols, bits), x)
    left_sum = turn(gradient, 0) + turn(pair, 1) + turn(mirror, 3)
    pair0 = send(after(own0, left_sum), PAIRS)

    near0, own1 = together([line.near(own0, pair0), own1])
    middle0 = send(near0, MIDDLE)
    pair1 = send(own1, PAIRS)
    near1 = line.near(own1, pair1)
    pair2 = send(after(own2, near1), PAIRS)

    left_part = (left_sum + turn(after(relay, near0), 2)).astype(BF16)
    left_rotated = lax.all_gather(left_part, "col")

    middle0, near1 = together([middle0, near1], left_part, pair2)
    out0 = send(middle0, OUTWARD)
    middle1 = send(near1, MIDDLE)
    columns = jnp.zeros((4 * height, width), BF16)
    near2 = line.near(own2, pair2)
    for bits, piece in zip((0, 1, 3, 2), together([gradient, pair, mirror, relay], left_part, near2)):
        columns = line.placed(columns, piece, bits)
    product_here = contract_last(columns, gradient).astype(BF16)
    product = lax.psum_scatter(after(product_here, out0, middle1), "col", scatter_dimension=0, tiled=True)

    middle1, near2 = together([middle1, near2], out0, product_here)
    out1 = send(middle1, OUTWARD)
    middle2 = send(near2, MIDDLE)

    steps = jnp.where(line.lower, jnp.array([0, STEPS]), jnp.array([STEPS, 0]))
    place = jnp.concatenate([steps, line.inner[None]]).astype(jnp.int32)

    def next_part(number, near, middle, out, before):
        *before, back = part(
            number, place, left_rotated, near, middle, out, first_moment, second_moment, left_cols, before
        )
        return before, back

    moments0, back0 = next_part(0, near0, middle0, after(out0, near2), ())
    stay0, far0 = halves(line.lower, back0)
    got0 = send(far0, INWARD)
    out2 = send(after(middle2, out1, far0), OUTWARD)
    moments1, back1 = next_part(1, near1, middle1, after(out1, far0), moments0)
    stay1, far1 = halves(line.lower, after(back1, got0))
    got1 = send(far1, INWARD)
    through0 = send(add(far0, after(got0, far1)), MIDDLE)
    right0 = line.whole(near0, middle0, after(out0, far1))
    right1 = line.whole(near1, middle1, after(out1, far1))
    mine0, other0 = halves(line.even, stay0.astype(F32) + through0.astype(F32))
    other0 = other0.astype(BF16)
    through1 = add(far1, got1)
    moments2, back2 = next_part(2, near2, middle2, after(out2, other0, through1, right0, right1), moments1)
    other0 = send(other0, PAIRS)
    turned0 = (mine0 + other0.astype(F32)).astype(BF16)
    through1 = send(through1, MIDDLE)
    mine1, other1 = halves(line.even, stay1.astype(F32) + through1.astype(F32))
    turned1 = (mine1 + send(other1.astype(BF16), PAIRS).astype(F32)).astype(BF16)
    first_next, second_next = moments2

    relay = send(line.block(back2, 2), RELAY_BACK)
    pair = send(line.block(back2, 1), PAIRS)
    relay = after(relay, through1, other0)
    mirror = send(add(line.block(back2, 3), jnp.where(line.inner, relay, 0)), MIRROR)
    right2 = line.whole(near2, middle2, after(out2, relay))
    left_next = 0.95 * left_stat + 0.05 * after(product, relay).astype(F32)
    mirror, pair = together([mirror, pair], right2)
    turned2 = line.block(back2, 0).astype(F32) + jnp.where(line.inner, 0, relay).astype(F32)
    turned2 = (turned2 + pair.astype(F32) + mirror.astype(F32)).astype(BF16)

    right = together([right0, right1, right2], left_next)
    direction = scatter_columns([turned0, turned1, turned2], right, "col")
    return (left_next, first_next, second_next, direction)


def body(gradient, left_stat, left_basis, right_basis, first_moment, second_moment):
    columns = lax.all_gather(gradient, "row", axis=0, tiled=True)
    left_cols = lax.all_gather(left_basis, "col", axis=0, tiled=True)
    right_cols = lax.all_gather(right_basis, "row", axis=0, tiled=True)
    left_rotated = lax.all_gather(contract_first(left_cols, columns).astype(BF16), "col", axis=1, tiled=True)
    product = contract_last(columns, gradient).astype(BF16)
    product = lax.psum_scatter(product, "col", scatter_dimension=0, tiled=True).astype(F32)
    left_next = 0.95 * left_stat + 0.05 * product
    rotated = jnp.dot(left_rotated, right_cols, preferred_element_type=F32)
    first_next, second_next, normalized = moments(rotated, first_moment, second_moment)
    back = jnp.dot(left_cols, normalized, preferred_element_type=F32).astype(BF16)
    back = lax.psum_scatter(back, "row", scatter_dimension=0, tiled=True)
    direction = contract_last(back, right_cols).astype(BF16)
    direction = lax.psum_scatter(direction, "col", scatter_dimension=1, tiled=True)
    return (left_next, first_next, second_next, direction)


def solution(mesh):
    on_line = mesh.shape["row"] == 4 and mesh.shape["col"] == 8
    return jax.shard_map(
        body_on_line if on_line else body,
        mesh=mesh,
        in_specs=(
            P("row", "col"),
            P("col", "row"),
            P("col", "row"),
            P("row", "col"),
            P("row", "col"),
            P("row", "col"),
        ),
        out_specs=(P("col", "row"), P("row", "col"), P("row", "col"), P("row", "col")),
        check_vma=False,
    )
```

```python
import jax
import jax.numpy as jnp
from jax import lax
from jax.experimental import pallas as pl
from jax.experimental.pallas import tpu as pltpu
from jax.sharding import PartitionSpec as P

BF16 = jnp.bfloat16
F32 = jnp.float32
VMEM = 60 * 2**20
QUICK = pl.CostEstimate(flops=2**20, bytes_accessed=2**16, transcendentals=0)

PAIRS = [(0, 1), (1, 0), (2, 3), (3, 2)]
MIDDLE = [(1, 2), (2, 1)]
OUTWARD = [(1, 0), (2, 3)]
INWARD = [(0, 1), (3, 2)]
MIRROR = [(0, 3), (1, 2), (2, 1), (3, 0)]
RELAY = [(0, 2), (1, 0), (2, 3), (3, 1)]
RELAY_BACK = [(0, 1), (1, 3), (2, 0), (3, 2)]


def contract_last(first, second):
    return lax.dot_general(first, second, (((1,), (1,)), ((), ())), preferred_element_type=F32)


def contract_first(first, second):
    return lax.dot_general(first, second, (((0,), (0,)), ((), ())), preferred_element_type=F32)


def together(operands, *earlier):
    return lax.optimization_barrier(tuple(operands) + earlier)[: len(operands)]


def after(x, *earlier):
    return together([x], *earlier)[0]


def joined(keep_order, first, second):
    return jnp.where(keep_order, jnp.concatenate([first, second]), jnp.concatenate([second, first]))


def halves(keep_order, x):
    n = x.shape[0] // 2
    return jnp.where(keep_order, x[:n], x[n:]), jnp.where(keep_order, x[n:], x[:n])


class Line:
    def __init__(self, axis):
        self.axis = axis
        self.i = lax.axis_index(axis)
        self.even = self.i % 2 == 0
        self.lower = self.i < 2
        self.inner = (self.i == 1) | (self.i == 2)

    def send(self, x, pairs):
        return lax.ppermute(x, self.axis, pairs)

    def near(self, x, got):
        return joined(self.even, x, got)

    def whole(self, near, middle, out):
        return joined(self.lower, near, jnp.where(self.inner, middle, out))

    def placed(self, whole, piece, bits):
        return lax.dynamic_update_slice(whole, piece, ((self.i ^ bits) * piece.shape[0], 0))

    def block(self, x, bits):
        n = x.shape[0] // 4
        return lax.dynamic_slice_in_dim(x, (self.i ^ bits) * n, n, 0)


def add(first, second):
    return (first.astype(F32) + second.astype(F32)).astype(first.dtype)


def products_kernel(order, *refs):
    parts = len(refs) // 2
    total = sum(contract_last(rows[...], right[...]) for rows, right in zip(refs[:parts], refs[parts:]))
    refs[-1][...] = total.astype(refs[-1].dtype)


def products(rows, half, right, order, start):
    height, depth = rows[0].shape[0] // 2, rows[0].shape[1]
    width = right[0].shape[0] // 8
    return pl.pallas_call(
        products_kernel,
        grid_spec=pltpu.PrefetchScalarGridSpec(
            num_scalar_prefetch=1,
            grid=(4,),
            in_specs=[pl.BlockSpec((height, depth), lambda b, order: (half, 0))] * len(rows)
            + [pl.BlockSpec((width, depth), lambda b, order: (order[start + b], 0))] * len(right),
            out_specs=pl.BlockSpec((height, width), lambda b, order: (0, b)),
        ),
        out_shape=jax.ShapeDtypeStruct((height, 4 * width), rows[0].dtype),
        compiler_params=pltpu.CompilerParams(vmem_limit_bytes=VMEM // 2),
        cost_estimate=QUICK,
    )(order, *rows, *right)


def scatter_columns(rows, right, axis):
    def swap(x, bit):
        return lax.ppermute(x, axis, [(j, j ^ bit) for j in range(8)])

    order = lax.axis_index(axis) ^ jnp.array([0, 2, 4, 6, 1, 3, 5, 7], jnp.int32)
    width = right[0].shape[0] // 8
    height = rows[0].shape[0] // 2
    low, high = slice(0, height // 2), slice(height // 2, height)

    def pair_sum(half, rows):
        away = products(rows, half, right, order, 4)
        got = swap(away, 1)
        return add(products(together(rows, away), half, right, order, 0), got)

    def block(x, b, rows):
        return x[rows, b * width : (b + 1) * width]

    def first_sends(x):
        return [
            jnp.concatenate([block(x, 1, low), block(x, 3, low)], axis=1),
            jnp.concatenate([block(x, 2, high), block(x, 3, high)], axis=1),
        ]

    def second_sends(x, by_x, by_y):
        return [add(block(x, 2, low), by_x[:, width:]), add(block(x, 1, high), by_y[:, width:])]

    def sums(x, by_x, by_y, then_y, then_x):
        total = lambda a, b, c: a.astype(F32) + b[:, :width].astype(F32) + c.astype(F32)
        return [total(block(x, 0, low), by_x, then_y), total(block(x, 0, high), by_y, then_x)]

    sum0 = pair_sum(0, rows)
    by_x0, by_y0 = together(first_sends(sum0))
    by_x0, by_y0 = swap(by_x0, 2), swap(by_y0, 4)
    sum1 = pair_sum(1, together(rows, sum0))
    then_y0, then_x0, by_x1, by_y1 = together(
        second_sends(sum0, *together([by_x0, by_y0], sum1)) + first_sends(sum1)
    )
    then_y0, then_x0 = swap(then_y0, 4), swap(then_x0, 2)
    by_x1, by_y1 = swap(by_x1, 2), swap(by_y1, 4)
    then_y1, then_x1 = together(second_sends(sum1, by_x1, by_y1))
    then_y1, then_x1 = swap(then_y1, 4), swap(then_x1, 2)
    kept = sums(sum0, by_x0, by_y0, then_y0, then_x0) + sums(sum1, by_x1, by_y1, then_y1, then_x1)
    return jnp.concatenate(kept).astype(sum0.dtype)


def moments(rotated, first_moment, second_moment):
    first_next = 0.9 * first_moment + 0.1 * rotated
    second_next = 0.95 * second_moment + 0.05 * rotated * rotated
    scaled_first = first_next / (1.0 - 0.9**10)
    scaled_second = second_next / (1.0 - 0.95**10)
    normalized = (scaled_first / (jnp.sqrt(scaled_second) + 1e-08)).astype(BF16)
    return first_next, second_next, normalized


STEPS = 2


def accumulate(total, left, right):
    depth = left.shape[2]
    for b in range(left.shape[0]):
        total[...] += jnp.dot(left[b], right[b * depth : (b + 1) * depth, :], preferred_element_type=F32)


def near_kernel(place, left, near, total):
    @pl.when(pl.program_id(0) == 0)
    def _():
        total[...] = jnp.zeros_like(total)

    accumulate(total, left, near)


def near_product(place, left_rotated, near):
    blocks, height, width = left_rotated.shape
    size = near.shape[1]
    deep = near.shape[0] // STEPS
    return pl.pallas_call(
        near_kernel,
        grid_spec=pltpu.PrefetchScalarGridSpec(
            num_scalar_prefetch=1,
            grid=(STEPS,),
            in_specs=[
                pl.BlockSpec((blocks // 2 // STEPS, height, width), lambda s, place: (place[0] + s, 0, 0)),
                pl.BlockSpec((deep, size), lambda s, place: (s, 0)),
            ],
            out_specs=pl.BlockSpec((height, size), lambda s, place: (0, 0)),
        ),
        out_shape=jax.ShapeDtypeStruct((height, size), F32),
        compiler_params=pltpu.CompilerParams(vmem_limit_bytes=VMEM),
        cost_estimate=QUICK,
    )(place, left_rotated, near)


def part_kernel(place, left, middle, out, near, first, second, basis, *rest):
    first_out, second_out, back, total, normalized = rest[-5:]
    step = pl.program_id(0)

    @pl.when(step == 0)
    def _():
        total[...] = near[...]

    @pl.when((step < STEPS) & (place[2] == 1))
    def _():
        accumulate(total, left, middle)

    @pl.when((step < STEPS) & (place[2] == 0))
    def _():
        accumulate(total, left, out)

    @pl.when(step == STEPS - 1)
    def _():
        first_out[...], second_out[...], normalized[...] = moments(total[...], first[...], second[...])

    @pl.when(step >= STEPS)
    def _():
        back[...] = jnp.dot(basis[...], normalized[...], preferred_element_type=F32).astype(BF16)


def part(number, place, left_rotated, near, middle, out, first_moment, second_moment, left_cols, before):
    height, width = first_moment.shape
    size = middle.shape[1]
    deep = middle.shape[0] // STEPS
    tall = left_cols.shape[0] // 2
    step = lambda s: jnp.minimum(s, STEPS - 1)
    last_step = lambda s: jnp.maximum(s - STEPS, 0)
    moment = pl.BlockSpec((height, size), lambda s, place: (0, number))
    before = list(before)
    return pl.pallas_call(
        part_kernel,
        grid_spec=pltpu.PrefetchScalarGridSpec(
            num_scalar_prefetch=1,
            grid=(STEPS + 2,),
            in_specs=[
                pl.BlockSpec((4 // STEPS, height, width), lambda s, place: (place[1] + step(s), 0, 0)),
                pl.BlockSpec((deep, size), lambda s, place: (step(s) * place[2], 0)),
                pl.BlockSpec((deep, size), lambda s, place: (step(s) * (1 - place[2]), 0)),
                pl.BlockSpec((height, size), lambda s, place: (0, 0)),
                moment,
                moment,
                pl.BlockSpec((tall, height), lambda s, place: (last_step(s), 0)),
            ]
            + [pl.BlockSpec(memory_space=pl.ANY)] * len(before),
            out_specs=[moment, moment, pl.BlockSpec((tall, size), lambda s, place: (last_step(s), 0))],
            scratch_shapes=[pltpu.VMEM((height, size), F32), pltpu.VMEM((height, size), BF16)],
        ),
        out_shape=[
            jax.ShapeDtypeStruct((height, width), F32),
            jax.ShapeDtypeStruct((height, width), F32),
            jax.ShapeDtypeStruct((left_cols.shape[0], size), BF16),
        ],
        input_output_aliases={8: 0, 9: 1} if before else {},
        compiler_params=pltpu.CompilerParams(vmem_limit_bytes=VMEM),
        cost_estimate=QUICK,
    )(place, left_rotated, middle, out, near, first_moment, second_moment, left_cols, *before)


def body_on_line(gradient, left_stat, left_basis, right_basis, first_moment, second_moment):
    line = Line("row")
    send = line.send
    height, width = gradient.shape
    cuts = [slice(p * width // 3, (p + 1) * width // 3) for p in range(3)]
    left_cols = lax.all_gather(left_basis, "col", axis=0, tiled=True)
    own0, own1, own2 = [right_basis[:, cut] for cut in cuts]

    mirror = send(gradient, MIRROR)
    pair = send(gradient, PAIRS)
    relay = send(after(jnp.where(line.inner, mirror, gradient), pair), RELAY)
    turn = lambda x, bits: contract_first(line.block(left_cols, bits), x)
    left_sum = turn(gradient, 0) + turn(pair, 1) + turn(mirror, 3)
    pair0 = send(after(own0, left_sum), PAIRS)

    near0, own1 = together([line.near(own0, pair0), own1])
    middle0 = send(near0, MIDDLE)
    pair1 = send(own1, PAIRS)
    near1 = line.near(own1, pair1)
    pair2 = send(after(own2, near1), PAIRS)

    left_part = (left_sum + turn(after(relay, near0), 2)).astype(BF16)
    left_rotated = lax.all_gather(left_part, "col")

    middle0, near1 = together([middle0, near1], left_part, pair2)
    out0 = send(middle0, OUTWARD)
    middle1 = send(near1, MIDDLE)
    columns = jnp.zeros((4 * height, width), BF16)
    near2 = line.near(own2, pair2)
    for bits, piece in zip((0, 1, 3, 2), together([gradient, pair, mirror, relay], left_part, near2)):
        columns = line.placed(columns, piece, bits)
    product_here = contract_last(columns, gradient).astype(BF16)
    product = lax.psum_scatter(after(product_here, out0, middle1), "col", scatter_dimension=0, tiled=True)

    middle1, near2 = together([middle1, near2], out0, product_here)
    out1 = send(middle1, OUTWARD)
    middle2 = send(near2, MIDDLE)

    steps = jnp.where(line.lower, jnp.array([0, STEPS]), jnp.array([STEPS, 0]))
    place = jnp.concatenate([steps, line.inner[None]]).astype(jnp.int32)

    def next_part(number, near, middle, out, before):
        *before, back = part(
            number, place, left_rotated, near, middle, out, first_moment, second_moment, left_cols, before
        )
        return before, back

    half0 = near_product(place, left_rotated, after(near0, near2))
    moments0, back0 = next_part(0, half0, middle0, out0, ())
    stay0, far0 = halves(line.lower, back0)
    got0 = send(far0, INWARD)
    half1 = near_product(place, left_rotated, after(near1, far0))
    out1 = after(out1, half1)
    out2 = send(after(middle2, out1), OUTWARD)
    moments1, back1 = next_part(1, half1, middle1, out1, moments0)
    stay1, far1 = halves(line.lower, back1)
    got1 = send(far1, INWARD)
    through0 = send(add(far0, after(got0, far1)), MIDDLE)
    half2 = near_product(place, left_rotated, after(near2, far1))
    got1, out2 = together([got1, out2], half2)
    through1 = add(far1, got1)
    moments2, back2 = next_part(2, half2, middle2, after(out2, through1), moments1)
    through1 = send(through1, MIDDLE)
    mine0, other0 = halves(line.even, stay0.astype(F32) + through0.astype(F32))
    turned0 = (mine0 + send(other0.astype(BF16), PAIRS).astype(F32)).astype(BF16)
    mine1, other1 = halves(line.even, stay1.astype(F32) + through1.astype(F32))
    turned1 = (mine1 + send(other1.astype(BF16), PAIRS).astype(F32)).astype(BF16)
    first_next, second_next = moments2

    relay = send(line.block(back2, 2), RELAY_BACK)
    pair = send(line.block(back2, 1), PAIRS)
    relay = after(relay, through1)
    mirror = send(add(line.block(back2, 3), jnp.where(line.inner, relay, 0)), MIRROR)
    out0, out1, out2, product = together([out0, out1, out2, product], turned1)
    right = [line.whole(near0, middle0, out0), line.whole(near1, middle1, out1), line.whole(near2, middle2, out2)]
    left_next = 0.95 * left_stat + 0.05 * product.astype(F32)
    mirror, pair = together([mirror, pair], *right)
    turned2 = line.block(back2, 0).astype(F32) + jnp.where(line.inner, 0, relay).astype(F32)
    turned2 = (turned2 + pair.astype(F32) + mirror.astype(F32)).astype(BF16)

    right = together(right, left_next)
    direction = scatter_columns([turned0, turned1, turned2], right, "col")
    return (left_next, first_next, second_next, direction)


def body(gradient, left_stat, left_basis, right_basis, first_moment, second_moment):
    columns = lax.all_gather(gradient, "row", axis=0, tiled=True)
    left_cols = lax.all_gather(left_basis, "col", axis=0, tiled=True)
    right_cols = lax.all_gather(right_basis, "row", axis=0, tiled=True)
    left_rotated = lax.all_gather(contract_first(left_cols, columns).astype(BF16), "col", axis=1, tiled=True)
    product = contract_last(columns, gradient).astype(BF16)
    product = lax.psum_scatter(product, "col", scatter_dimension=0, tiled=True).astype(F32)
    left_next = 0.95 * left_stat + 0.05 * product
    rotated = jnp.dot(left_rotated, right_cols, preferred_element_type=F32)
    first_next, second_next, normalized = moments(rotated, first_moment, second_moment)
    back = jnp.dot(left_cols, normalized, preferred_element_type=F32).astype(BF16)
    back = lax.psum_scatter(back, "row", scatter_dimension=0, tiled=True)
    direction = contract_last(back, right_cols).astype(BF16)
    direction = lax.psum_scatter(direction, "col", scatter_dimension=1, tiled=True)
    return (left_next, first_next, second_next, direction)


def solution(mesh):
    on_line = mesh.shape["row"] == 4 and mesh.shape["col"] == 8
    return jax.shard_map(
        body_on_line if on_line else body,
        mesh=mesh,
        in_specs=(
            P("row", "col"),
            P("col", "row"),
            P("col", "row"),
            P("row", "col"),
            P("row", "col"),
            P("row", "col"),
        ),
        out_specs=(P("col", "row"), P("row", "col"), P("row", "col"), P("row", "col")),
        check_vma=False,
    )
```

```python
import jax
import jax.numpy as jnp
from jax import lax
from jax.experimental import pallas as pl
from jax.experimental.pallas import tpu as pltpu
from jax.sharding import PartitionSpec as P

BF16 = jnp.bfloat16
F32 = jnp.float32
VMEM = 60 * 2**20
QUICK = pl.CostEstimate(flops=2**20, bytes_accessed=2**16, transcendentals=0)

PAIRS = [(0, 1), (1, 0), (2, 3), (3, 2)]
MIDDLE = [(1, 2), (2, 1)]
OUTWARD = [(1, 0), (2, 3)]
INWARD = [(0, 1), (3, 2)]
MIRROR = [(0, 3), (1, 2), (2, 1), (3, 0)]
RELAY = [(0, 2), (1, 0), (2, 3), (3, 1)]
RELAY_BACK = [(0, 1), (1, 3), (2, 0), (3, 2)]


def contract_last(first, second):
    return lax.dot_general(first, second, (((1,), (1,)), ((), ())), preferred_element_type=F32)


def contract_first(first, second):
    return lax.dot_general(first, second, (((0,), (0,)), ((), ())), preferred_element_type=F32)


def together(operands, *earlier):
    return lax.optimization_barrier(tuple(operands) + earlier)[: len(operands)]


def after(x, *earlier):
    return together([x], *earlier)[0]


def joined(keep_order, first, second):
    return jnp.where(keep_order, jnp.concatenate([first, second]), jnp.concatenate([second, first]))


def halves(keep_order, x):
    n = x.shape[0] // 2
    return jnp.where(keep_order, x[:n], x[n:]), jnp.where(keep_order, x[n:], x[:n])


class Line:
    def __init__(self, axis):
        self.axis = axis
        self.i = lax.axis_index(axis)
        self.even = self.i % 2 == 0
        self.lower = self.i < 2
        self.inner = (self.i == 1) | (self.i == 2)

    def send(self, x, pairs):
        return lax.ppermute(x, self.axis, pairs)

    def near(self, x, got):
        return joined(self.even, x, got)

    def whole(self, near, middle, out):
        return joined(self.lower, near, jnp.where(self.inner, middle, out))

    def placed(self, whole, piece, bits):
        return lax.dynamic_update_slice(whole, piece, ((self.i ^ bits) * piece.shape[0], 0))

    def block(self, x, bits):
        n = x.shape[0] // 4
        return lax.dynamic_slice_in_dim(x, (self.i ^ bits) * n, n, 0)


def add(first, second):
    return (first.astype(F32) + second.astype(F32)).astype(first.dtype)


def products_kernel(order, *refs):
    parts = len(refs) // 2
    total = sum(contract_last(rows[...], right[...]) for rows, right in zip(refs[:parts], refs[parts:]))
    refs[-1][...] = total.astype(refs[-1].dtype)


def products(rows, half, right, order, start):
    height, depth = rows[-1].shape
    width = right[0].shape[0] // 8
    return pl.pallas_call(
        products_kernel,
        grid_spec=pltpu.PrefetchScalarGridSpec(
            num_scalar_prefetch=1,
            grid=(4,),
            in_specs=[pl.BlockSpec((height, depth), lambda b, order: (half, 0))] * (len(rows) - 1)
            + [pl.BlockSpec((height, depth), lambda b, order: (0, 0))]
            + [pl.BlockSpec((width, depth), lambda b, order: (order[start + b], 0))] * len(right),
            out_specs=pl.BlockSpec((height, width), lambda b, order: (0, b)),
        ),
        out_shape=jax.ShapeDtypeStruct((height, 4 * width), rows[0].dtype),
        compiler_params=pltpu.CompilerParams(vmem_limit_bytes=VMEM // 2),
        cost_estimate=QUICK,
    )(order, *rows, *right)


def scatter_columns(rows, rows_low, rows_high, right, axis):
    def swap(x, bit):
        return lax.ppermute(x, axis, [(j, j ^ bit) for j in range(8)])

    order = lax.axis_index(axis) ^ jnp.array([0, 2, 4, 6, 1, 3, 5, 7], jnp.int32)
    width = right[0].shape[0] // 8
    height = rows_low.shape[0]
    low, high = slice(0, height // 2), slice(height // 2, height)

    def pair_sum(half, rows):
        away = products(rows, half, right, order, 4)
        got = swap(away, 1)
        return add(products(together(rows, away), half, right, order, 0), got)

    def block(x, b, rows):
        return x[rows, b * width : (b + 1) * width]

    def first_sends(x):
        return [
            jnp.concatenate([block(x, 1, low), block(x, 3, low)], axis=1),
            jnp.concatenate([block(x, 2, high), block(x, 3, high)], axis=1),
        ]

    def second_sends(x, by_x, by_y):
        return [add(block(x, 2, low), by_x[:, width:]), add(block(x, 1, high), by_y[:, width:])]

    def sums(x, by_x, by_y, then_y, then_x):
        total = lambda a, b, c: a.astype(F32) + b[:, :width].astype(F32) + c.astype(F32)
        return [total(block(x, 0, low), by_x, then_y), total(block(x, 0, high), by_y, then_x)]

    sum0 = pair_sum(0, rows + [rows_low])
    by_x0, by_y0 = together(first_sends(sum0))
    by_x0, by_y0 = swap(by_x0, 2), swap(by_y0, 4)
    sum1 = pair_sum(1, rows + [rows_high(sum0)])
    then_y0, then_x0, by_x1, by_y1 = together(
        second_sends(sum0, *together([by_x0, by_y0], sum1)) + first_sends(sum1)
    )
    then_y0, then_x0 = swap(then_y0, 4), swap(then_x0, 2)
    by_x1, by_y1 = swap(by_x1, 2), swap(by_y1, 4)
    then_y1, then_x1 = together(second_sends(sum1, by_x1, by_y1))
    then_y1, then_x1 = swap(then_y1, 4), swap(then_x1, 2)
    kept = sums(sum0, by_x0, by_y0, then_y0, then_x0) + sums(sum1, by_x1, by_y1, then_y1, then_x1)
    return jnp.concatenate(kept).astype(sum0.dtype)


def moments(rotated, first_moment, second_moment):
    first_next = 0.9 * first_moment + 0.1 * rotated
    second_next = 0.95 * second_moment + 0.05 * rotated * rotated
    scaled_first = first_next / (1.0 - 0.9**10)
    scaled_second = second_next / (1.0 - 0.95**10)
    normalized = (scaled_first / (jnp.sqrt(scaled_second) + 1e-08)).astype(BF16)
    return first_next, second_next, normalized


STEPS = 2


def part_kernel(place, left, near, middle, out, first, second, basis, *rest):
    first_out, second_out, back, total, normalized = rest[-5:]
    step = pl.program_id(0)

    @pl.when(step == 0)
    def _():
        total[...] = jnp.zeros_like(total)

    def accumulate(right):
        depth = left.shape[2]
        for b in range(left.shape[0]):
            total[...] += jnp.dot(left[b], right[b * depth : (b + 1) * depth, :], preferred_element_type=F32)

    @pl.when(step < STEPS)
    def _():
        accumulate(near)

    far = (step >= STEPS) & (step < 2 * STEPS)

    @pl.when(far & (place[2] == 1))
    def _():
        accumulate(middle)

    @pl.when(far & (place[2] == 0))
    def _():
        accumulate(out)

    @pl.when(step == 2 * STEPS - 1)
    def _():
        first_out[...], second_out[...], normalized[...] = moments(total[...], first[...], second[...])

    @pl.when(step >= 2 * STEPS)
    def _():
        back[...] = jnp.dot(basis[...], normalized[...], preferred_element_type=F32).astype(BF16)


def part(number, place, left_rotated, near, middle, out, first_moment, second_moment, left_cols, before):
    height, width = first_moment.shape
    size = near.shape[1]
    deep = near.shape[0] // STEPS
    tall = left_cols.shape[0] // 2
    near_step = lambda s: jnp.minimum(s, STEPS - 1)
    far_step = lambda s: jnp.clip(s - STEPS, 0, STEPS - 1)
    last_step = lambda s: jnp.maximum(s - 2 * STEPS, 0)

    def left_block(s, place):
        return jnp.where(s < STEPS, place[0] + near_step(s), place[1] + far_step(s)), 0, 0

    moment = pl.BlockSpec((height, size), lambda s, place: (0, number))
    before = list(before)
    return pl.pallas_call(
        part_kernel,
        grid_spec=pltpu.PrefetchScalarGridSpec(
            num_scalar_prefetch=1,
            grid=(2 * STEPS + 2,),
            in_specs=[
                pl.BlockSpec((4 // STEPS, height, width), left_block),
                pl.BlockSpec((deep, size), lambda s, place: (near_step(s), 0)),
                pl.BlockSpec((deep, size), lambda s, place: (far_step(s) * place[2], 0)),
                pl.BlockSpec((deep, size), lambda s, place: (far_step(s) * (1 - place[2]), 0)),
                moment,
                moment,
                pl.BlockSpec((tall, height), lambda s, place: (last_step(s), 0)),
            ]
            + [pl.BlockSpec(memory_space=pl.ANY)] * len(before),
            out_specs=[moment, moment, pl.BlockSpec((tall, size), lambda s, place: (last_step(s), 0))],
            scratch_shapes=[pltpu.VMEM((height, size), F32), pltpu.VMEM((height, size), BF16)],
        ),
        out_shape=[
            jax.ShapeDtypeStruct((height, width), F32),
            jax.ShapeDtypeStruct((height, width), F32),
            jax.ShapeDtypeStruct((left_cols.shape[0], size), BF16),
        ],
        input_output_aliases={8: 0, 9: 1} if before else {},
        compiler_params=pltpu.CompilerParams(vmem_limit_bytes=VMEM),
        cost_estimate=QUICK,
    )(place, left_rotated, near, middle, out, first_moment, second_moment, left_cols, *before)


def body_on_line(gradient, left_stat, left_basis, right_basis, first_moment, second_moment):
    line = Line("row")
    send = line.send
    height, width = gradient.shape
    cuts = [slice(p * width // 3, (p + 1) * width // 3) for p in range(3)]
    left_cols = lax.all_gather(left_basis, "col", axis=0, tiled=True)
    own0, own1, own2 = [right_basis[:, cut] for cut in cuts]

    mirror = send(gradient, MIRROR)
    pair = send(gradient, PAIRS)
    relay = send(after(jnp.where(line.inner, mirror, gradient), pair), RELAY)
    turn = lambda x, bits: contract_first(line.block(left_cols, bits), x)
    left_sum = turn(gradient, 0) + turn(pair, 1) + turn(mirror, 3)
    pair0 = send(after(own0, left_sum), PAIRS)

    near0, own1 = together([line.near(own0, pair0), own1])
    middle0 = send(near0, MIDDLE)
    pair1 = send(own1, PAIRS)
    near1 = line.near(own1, pair1)
    pair2 = send(after(own2, near1), PAIRS)

    left_part = (left_sum + turn(after(relay, near0), 2)).astype(BF16)
    left_rotated = lax.all_gather(left_part, "col")

    middle0, near1 = together([middle0, near1], left_part, pair2)
    out0 = send(middle0, OUTWARD)
    middle1 = send(near1, MIDDLE)
    columns = jnp.zeros((4 * height, width), BF16)
    near2 = line.near(own2, pair2)
    for bits, piece in zip((0, 1, 3, 2), together([gradient, pair, mirror, relay], left_part, near2)):
        columns = line.placed(columns, piece, bits)
    product_here = contract_last(columns, gradient).astype(BF16)
    product = lax.psum_scatter(after(product_here, out0, middle1), "col", scatter_dimension=0, tiled=True)

    middle1, near2 = together([middle1, near2], out0, product_here)
    out1 = send(middle1, OUTWARD)
    middle2 = send(near2, MIDDLE)

    steps = jnp.where(line.lower, jnp.array([0, STEPS]), jnp.array([STEPS, 0]))
    place = jnp.concatenate([steps, line.inner[None]]).astype(jnp.int32)

    def next_part(number, near, middle, out, before):
        *before, back = part(
            number, place, left_rotated, near, middle, out, first_moment, second_moment, left_cols, before
        )
        return before, back

    moments0, back0 = next_part(0, near0, middle0, after(out0, near2), ())
    stay0, far0 = halves(line.lower, back0)
    got0 = send(far0, INWARD)
    out2 = send(after(middle2, out1, far0), OUTWARD)
    moments1, back1 = next_part(1, near1, middle1, after(out1, far0), moments0)
    stay1, far1 = halves(line.lower, after(back1, got0))
    got1 = send(far1, INWARD)
    through0 = send(add(far0, after(got0, far1)), MIDDLE)
    right0 = line.whole(near0, middle0, after(out0, far1))
    right1 = line.whole(near1, middle1, after(out1, far1))
    mine0, other0 = halves(line.even, stay0.astype(F32) + through0.astype(F32))
    other0 = other0.astype(BF16)
    through1 = add(far1, after(got1, right0, right1))
    moments2, back2 = next_part(2, near2, middle2, after(out2, through1), moments1)
    other0 = send(other0, PAIRS)
    turned0 = (mine0 + other0.astype(F32)).astype(BF16)
    through1 = send(through1, MIDDLE)
    mine1, other1 = halves(line.even, stay1.astype(F32) + through1.astype(F32))
    turned1 = (mine1 + send(other1.astype(BF16), PAIRS).astype(F32)).astype(BF16)
    first_next, second_next = moments2

    low, high = [
        [line.block(back2, bits)[h * height // 2 : (h + 1) * height // 2] for bits in range(4)] for h in range(2)
    ]

    def first_step(blocks):
        return send(blocks[2], RELAY_BACK), send(blocks[1], PAIRS)

    def second_step(blocks, relay):
        return send(add(blocks[3], jnp.where(line.inner, relay, 0)), MIRROR)

    def summed(blocks, relay, pair, mirror):
        total = blocks[0].astype(F32) + jnp.where(line.inner, 0, relay).astype(F32)
        return (total + pair.astype(F32) + mirror.astype(F32)).astype(BF16)

    relay_low, pair_low = first_step(low)
    relay_low = after(relay_low, through1)
    mirror_low = second_step(low, relay_low)
    relay_high, pair_high = first_step(together(high, relay_low))
    right2 = line.whole(near2, middle2, after(out2, relay_high))
    left_next = 0.95 * left_stat + 0.05 * after(product, relay_high).astype(F32)
    to_mirror = add(high[3], jnp.where(line.inner, relay_high, 0))
    mirror_high = send(to_mirror, MIRROR)
    turned_low = summed(low, relay_low, pair_low, after(mirror_low, right2, left_next, to_mirror))

    def turned_high(earlier):
        return summed(high, relay_high, pair_high, after(mirror_high, earlier))

    right = [right0, right1, right2]
    direction = scatter_columns([turned0, turned1], turned_low, turned_high, right, "col")
    return (left_next, first_next, second_next, direction)


def body(gradient, left_stat, left_basis, right_basis, first_moment, second_moment):
    columns = lax.all_gather(gradient, "row", axis=0, tiled=True)
    left_cols = lax.all_gather(left_basis, "col", axis=0, tiled=True)
    right_cols = lax.all_gather(right_basis, "row", axis=0, tiled=True)
    left_rotated = lax.all_gather(contract_first(left_cols, columns).astype(BF16), "col", axis=1, tiled=True)
    product = contract_last(columns, gradient).astype(BF16)
    product = lax.psum_scatter(product, "col", scatter_dimension=0, tiled=True).astype(F32)
    left_next = 0.95 * left_stat + 0.05 * product
    rotated = jnp.dot(left_rotated, right_cols, preferred_element_type=F32)
    first_next, second_next, normalized = moments(rotated, first_moment, second_moment)
    back = jnp.dot(left_cols, normalized, preferred_element_type=F32).astype(BF16)
    back = lax.psum_scatter(back, "row", scatter_dimension=0, tiled=True)
    direction = contract_last(back, right_cols).astype(BF16)
    direction = lax.psum_scatter(direction, "col", scatter_dimension=1, tiled=True)
    return (left_next, first_next, second_next, direction)


def solution(mesh):
    on_line = mesh.shape["row"] == 4 and mesh.shape["col"] == 8
    return jax.shard_map(
        body_on_line if on_line else body,
        mesh=mesh,
        in_specs=(
            P("row", "col"),
            P("col", "row"),
            P("col", "row"),
            P("row", "col"),
            P("row", "col"),
            P("row", "col"),
        ),
        out_specs=(P("col", "row"), P("row", "col"), P("row", "col"), P("row", "col")),
        check_vma=False,
    )
```

```python
import functools

import jax
import jax.numpy as jnp
from jax import lax
from jax.experimental import pallas as pl
from jax.experimental.pallas import tpu as pltpu
from jax.sharding import PartitionSpec as P

BF16 = jnp.bfloat16
F32 = jnp.float32
VMEM = 60 * 2**20
QUICK = pl.CostEstimate(flops=2**20, bytes_accessed=2**16, transcendentals=0)

PAIRS = [(0, 1), (1, 0), (2, 3), (3, 2)]
MIDDLE = [(1, 2), (2, 1)]
OUTWARD = [(1, 0), (2, 3)]
INWARD = [(0, 1), (3, 2)]
MIRROR = [(0, 3), (1, 2), (2, 1), (3, 0)]
RELAY = [(0, 2), (1, 0), (2, 3), (3, 1)]
RELAY_BACK = [(0, 1), (1, 3), (2, 0), (3, 2)]


def contract_last(first, second):
    return lax.dot_general(first, second, (((1,), (1,)), ((), ())), preferred_element_type=F32)


def contract_first(first, second):
    return lax.dot_general(first, second, (((0,), (0,)), ((), ())), preferred_element_type=F32)


def together(operands, *earlier):
    return lax.optimization_barrier(tuple(operands) + earlier)[: len(operands)]


def after(x, *earlier):
    return together([x], *earlier)[0]


def joined(keep_order, first, second):
    return jnp.where(keep_order, jnp.concatenate([first, second]), jnp.concatenate([second, first]))


def halves(keep_order, x):
    n = x.shape[0] // 2
    return jnp.where(keep_order, x[:n], x[n:]), jnp.where(keep_order, x[n:], x[:n])


class Line:
    def __init__(self, axis):
        self.axis = axis
        self.i = lax.axis_index(axis)
        self.even = self.i % 2 == 0
        self.lower = self.i < 2
        self.inner = (self.i == 1) | (self.i == 2)

    def send(self, x, pairs):
        return lax.ppermute(x, self.axis, pairs)

    def near(self, x, got):
        return joined(self.even, x, got)

    def whole(self, near, middle, out):
        return joined(self.lower, near, jnp.where(self.inner, middle, out))

    def placed(self, whole, piece, bits):
        return lax.dynamic_update_slice(whole, piece, ((self.i ^ bits) * piece.shape[0], 0))

    def block(self, x, bits):
        n = x.shape[0] // 4
        return lax.dynamic_slice_in_dim(x, (self.i ^ bits) * n, n, 0)


def add(first, second):
    return (first.astype(F32) + second.astype(F32)).astype(first.dtype)


def products_kernel(order, *refs):
    parts = len(refs) // 2
    total = sum(contract_last(rows[...], right[...]) for rows, right in zip(refs[:parts], refs[parts:]))
    refs[-1][...] = total.astype(refs[-1].dtype)


def products(rows, half, right, order, start):
    height, depth = rows[0].shape[0] // 2, rows[0].shape[1]
    width = right[0].shape[0] // 8
    return pl.pallas_call(
        products_kernel,
        grid_spec=pltpu.PrefetchScalarGridSpec(
            num_scalar_prefetch=1,
            grid=(4,),
            in_specs=[pl.BlockSpec((height, depth), lambda b, order: (half, 0))] * len(rows)
            + [pl.BlockSpec((width, depth), lambda b, order: (order[start + b], 0))] * len(right),
            out_specs=pl.BlockSpec((height, width), lambda b, order: (0, b)),
        ),
        out_shape=jax.ShapeDtypeStruct((height, 4 * width), rows[0].dtype),
        compiler_params=pltpu.CompilerParams(vmem_limit_bytes=VMEM // 2),
        cost_estimate=QUICK,
    )(order, *rows, *right)


def scatter_columns(rows, right, axis):
    def swap(x, bit):
        return lax.ppermute(x, axis, [(j, j ^ bit) for j in range(8)])

    order = lax.axis_index(axis) ^ jnp.array([0, 2, 4, 6, 1, 3, 5, 7], jnp.int32)
    width = right[0].shape[0] // 8
    height = rows[0].shape[0] // 2
    low, high = slice(0, height // 2), slice(height // 2, height)

    def pair_sum(half, rows):
        away = products(rows, half, right, order, 4)
        got = swap(away, 1)
        return add(products(together(rows, away), half, right, order, 0), got)

    def block(x, b, rows):
        return x[rows, b * width : (b + 1) * width]

    def first_sends(x):
        return [
            jnp.concatenate([block(x, 1, low), block(x, 3, low)], axis=1),
            jnp.concatenate([block(x, 2, high), block(x, 3, high)], axis=1),
        ]

    def second_sends(x, by_x, by_y):
        return [add(block(x, 2, low), by_x[:, width:]), add(block(x, 1, high), by_y[:, width:])]

    def sums(x, by_x, by_y, then_y, then_x):
        total = lambda a, b, c: a.astype(F32) + b[:, :width].astype(F32) + c.astype(F32)
        return [total(block(x, 0, low), by_x, then_y), total(block(x, 0, high), by_y, then_x)]

    sum0 = pair_sum(0, rows)
    by_x0, by_y0 = together(first_sends(sum0))
    by_x0, by_y0 = swap(by_x0, 2), swap(by_y0, 4)
    sum1 = pair_sum(1, together(rows, sum0))
    then_y0, then_x0, by_x1, by_y1 = together(
        second_sends(sum0, *together([by_x0, by_y0], sum1)) + first_sends(sum1)
    )
    then_y0, then_x0 = swap(then_y0, 4), swap(then_x0, 2)
    by_x1, by_y1 = swap(by_x1, 2), swap(by_y1, 4)
    then_y1, then_x1 = together(second_sends(sum1, by_x1, by_y1))
    then_y1, then_x1 = swap(then_y1, 4), swap(then_x1, 2)
    kept = sums(sum0, by_x0, by_y0, then_y0, then_x0) + sums(sum1, by_x1, by_y1, then_y1, then_x1)
    return jnp.concatenate(kept).astype(sum0.dtype)


def moments(rotated, first_moment, second_moment):
    first_next = 0.9 * first_moment + 0.1 * rotated
    second_next = 0.95 * second_moment + 0.05 * rotated * rotated
    scaled_first = first_next / (1.0 - 0.9**10)
    scaled_second = second_next / (1.0 - 0.95**10)
    normalized = (scaled_first / (jnp.sqrt(scaled_second) + 1e-08)).astype(BF16)
    return first_next, second_next, normalized


STEPS = 2


def part_kernel(place, left, near, middle, out, first, second, basis, *rest, results):
    first_out, second_out, *backs, total, normalized = rest[-4 - results :]
    step = pl.program_id(0)

    @pl.when(step == 0)
    def _():
        total[...] = jnp.zeros_like(total)

    def accumulate(right):
        depth = left.shape[2]
        for b in range(left.shape[0]):
            total[...] += jnp.dot(left[b], right[b * depth : (b + 1) * depth, :], preferred_element_type=F32)

    @pl.when(step < STEPS)
    def _():
        accumulate(near)

    far = (step >= STEPS) & (step < 2 * STEPS)

    @pl.when(far & (place[2] == 1))
    def _():
        accumulate(middle)

    @pl.when(far & (place[2] == 0))
    def _():
        accumulate(out)

    @pl.when(step == 2 * STEPS - 1)
    def _():
        first_out[...], second_out[...], normalized[...] = moments(total[...], first[...], second[...])

    for number, back in enumerate(backs):

        @pl.when(step == 2 * STEPS + number)
        def _(back=back):
            back[...] = jnp.dot(basis[...], normalized[...], preferred_element_type=F32).astype(BF16)


def part(number, place, results, left_rotated, near, middle, out, first_moment, second_moment, left_cols, before):
    height, width = first_moment.shape
    size = near.shape[1]
    deep = near.shape[0] // STEPS
    tall = left_cols.shape[0] // results
    near_step = lambda s: jnp.minimum(s, STEPS - 1)
    far_step = lambda s: jnp.clip(s - STEPS, 0, STEPS - 1)
    last_step = lambda s: jnp.maximum(s - 2 * STEPS, 0)

    def left_block(s, place):
        return jnp.where(s < STEPS, place[0] + near_step(s), place[1] + far_step(s)), 0, 0

    moment = pl.BlockSpec((height, size), lambda s, place: (0, number))
    before = list(before)
    first_next, second_next, *backs = pl.pallas_call(
        functools.partial(part_kernel, results=results),
        grid_spec=pltpu.PrefetchScalarGridSpec(
            num_scalar_prefetch=1,
            grid=(2 * STEPS + results,),
            in_specs=[
                pl.BlockSpec((4 // STEPS, height, width), left_block),
                pl.BlockSpec((deep, size), lambda s, place: (near_step(s), 0)),
                pl.BlockSpec((deep, size), lambda s, place: (far_step(s) * place[2], 0)),
                pl.BlockSpec((deep, size), lambda s, place: (far_step(s) * (1 - place[2]), 0)),
                moment,
                moment,
                pl.BlockSpec((tall, height), lambda s, place: (place[3 + last_step(s)], 0)),
            ]
            + [pl.BlockSpec(memory_space=pl.ANY)] * len(before),
            out_specs=[moment, moment] + [pl.BlockSpec((tall, size), lambda s, place: (0, 0))] * results,
            scratch_shapes=[pltpu.VMEM((height, size), F32), pltpu.VMEM((height, size), BF16)],
        ),
        out_shape=[jax.ShapeDtypeStruct((height, width), F32)] * 2
        + [jax.ShapeDtypeStruct((tall, size), BF16)] * results,
        input_output_aliases={8: 0, 9: 1} if before else {},
        compiler_params=pltpu.CompilerParams(vmem_limit_bytes=VMEM),
        cost_estimate=QUICK,
    )(place, left_rotated, near, middle, out, first_moment, second_moment, left_cols, *before)
    return (first_next, second_next), backs


def body_on_line(gradient, left_stat, left_basis, right_basis, first_moment, second_moment):
    line = Line("row")
    send = line.send
    height, width = gradient.shape
    cuts = [slice(p * width // 3, (p + 1) * width // 3) for p in range(3)]
    left_cols = lax.all_gather(left_basis, "col", axis=0, tiled=True)
    own0, own1, own2 = [right_basis[:, cut] for cut in cuts]

    mirror = send(gradient, MIRROR)
    pair = send(gradient, PAIRS)
    relay = send(after(jnp.where(line.inner, mirror, gradient), pair), RELAY)
    turn = lambda x, bits: contract_first(line.block(left_cols, bits), x)
    left_sum = turn(gradient, 0) + turn(pair, 1) + turn(mirror, 3)
    pair0 = send(after(own0, left_sum), PAIRS)

    near0, own1 = together([line.near(own0, pair0), own1])
    middle0 = send(near0, MIDDLE)
    pair1 = send(own1, PAIRS)
    near1 = line.near(own1, pair1)
    pair2 = send(after(own2, near1), PAIRS)

    left_part = (left_sum + turn(after(relay, near0), 2)).astype(BF16)
    left_rotated = lax.all_gather(left_part, "col")

    middle0, near1 = together([middle0, near1], left_part, pair2)
    out0 = send(middle0, OUTWARD)
    middle1 = send(near1, MIDDLE)
    columns = jnp.zeros((4 * height, width), BF16)
    near2 = line.near(own2, pair2)
    for bits, piece in zip((0, 1, 3, 2), together([gradient, pair, mirror, relay], left_part, near2)):
        columns = line.placed(columns, piece, bits)
    product_here = contract_last(columns, gradient).astype(BF16)
    product = lax.psum_scatter(after(product_here, out0, middle1), "col", scatter_dimension=0, tiled=True)

    middle1, near2 = together([middle1, near2], out0, product_here)
    out1 = send(middle1, OUTWARD)
    middle2 = send(near2, MIDDLE)

    halves_first = jnp.where(line.lower, jnp.array([0, STEPS]), jnp.array([STEPS, 0]))
    far_near = jnp.where(line.lower, jnp.array([1, 0]), jnp.array([0, 1]))
    place = jnp.concatenate([halves_first, line.inner[None]]).astype(jnp.int32)
    to_halves = jnp.concatenate([place, far_near]).astype(jnp.int32)
    to_blocks = jnp.concatenate([place, line.i ^ jnp.array([2, 1, 3, 0])]).astype(jnp.int32)

    def next_part(number, near, middle, out, before):
        order, results = (to_blocks, 4) if number == 2 else (to_halves, 2)
        return part(
            number, order, results, left_rotated, near, middle, out, first_moment, second_moment, left_cols, before
        )

    moments0, (far0, stay0) = next_part(0, near0, middle0, after(out0, near2), ())
    got0 = send(far0, INWARD)
    out2 = send(after(middle2, out1, far0), OUTWARD)
    moments1, (far1, stay1) = next_part(1, near1, middle1, after(out1, far0), moments0)
    got1 = send(far1, INWARD)
    through0 = send(add(far0, after(got0, far1)), MIDDLE)
    mine0, other0 = halves(line.even, stay0.astype(F32) + through0.astype(F32))
    other0 = other0.astype(BF16)
    got1, out2 = together([got1, out2])
    through1 = add(far1, got1)
    moments2, blocks2 = next_part(2, near2, middle2, after(out2, other0, through1), moments1)
    other0 = send(other0, PAIRS)
    turned0 = (mine0 + other0.astype(F32)).astype(BF16)
    through1 = send(through1, MIDDLE)
    mine1, other1 = halves(line.even, stay1.astype(F32) + through1.astype(F32))
    turned1 = (mine1 + send(other1.astype(BF16), PAIRS).astype(F32)).astype(BF16)
    first_next, second_next = moments2

    to_relay, to_pair, to_mirror, own = blocks2
    relay = send(to_relay, RELAY_BACK)
    pair = send(to_pair, PAIRS)
    relay = after(relay, through1, other0)
    mirror = send(add(to_mirror, jnp.where(line.inner, relay, 0)), MIRROR)
    out0, out1, out2, product = together([out0, out1, out2, product], turned1)
    right = [line.whole(near0, middle0, out0), line.whole(near1, middle1, out1), line.whole(near2, middle2, out2)]
    left_next = 0.95 * left_stat + 0.05 * product.astype(F32)
    mirror, pair = together([mirror, pair], *right)
    turned2 = own.astype(F32) + jnp.where(line.inner, 0, relay).astype(F32)
    turned2 = (turned2 + pair.astype(F32) + mirror.astype(F32)).astype(BF16)

    right = together(right, left_next)
    direction = scatter_columns([turned0, turned1, turned2], right, "col")
    return (left_next, first_next, second_next, direction)


def body(gradient, left_stat, left_basis, right_basis, first_moment, second_moment):
    columns = lax.all_gather(gradient, "row", axis=0, tiled=True)
    left_cols = lax.all_gather(left_basis, "col", axis=0, tiled=True)
    right_cols = lax.all_gather(right_basis, "row", axis=0, tiled=True)
    left_rotated = lax.all_gather(contract_first(left_cols, columns).astype(BF16), "col", axis=1, tiled=True)
    product = contract_last(columns, gradient).astype(BF16)
    product = lax.psum_scatter(product, "col", scatter_dimension=0, tiled=True).astype(F32)
    left_next = 0.95 * left_stat + 0.05 * product
    rotated = jnp.dot(left_rotated, right_cols, preferred_element_type=F32)
    first_next, second_next, normalized = moments(rotated, first_moment, second_moment)
    back = jnp.dot(left_cols, normalized, preferred_element_type=F32).astype(BF16)
    back = lax.psum_scatter(back, "row", scatter_dimension=0, tiled=True)
    direction = contract_last(back, right_cols).astype(BF16)
    direction = lax.psum_scatter(direction, "col", scatter_dimension=1, tiled=True)
    return (left_next, first_next, second_next, direction)


def solution(mesh):
    on_line = mesh.shape["row"] == 4 and mesh.shape["col"] == 8
    return jax.shard_map(
        body_on_line if on_line else body,
        mesh=mesh,
        in_specs=(
            P("row", "col"),
            P("col", "row"),
            P("col", "row"),
            P("row", "col"),
            P("row", "col"),
            P("row", "col"),
        ),
        out_specs=(P("col", "row"), P("row", "col"), P("row", "col"), P("row", "col")),
        check_vma=False,
    )
```

```python
import functools

import jax
import jax.numpy as jnp
from jax import lax
from jax.experimental import pallas as pl
from jax.experimental.pallas import tpu as pltpu
from jax.sharding import PartitionSpec as P

BF16 = jnp.bfloat16
F32 = jnp.float32
VMEM = 60 * 2**20
QUICK = pl.CostEstimate(flops=2**20, bytes_accessed=2**16, transcendentals=0)

PAIRS = [(0, 1), (1, 0), (2, 3), (3, 2)]
MIDDLE = [(1, 2), (2, 1)]
OUTWARD = [(1, 0), (2, 3)]
INWARD = [(0, 1), (3, 2)]
MIRROR = [(0, 3), (1, 2), (2, 1), (3, 0)]
RELAY = [(0, 2), (1, 0), (2, 3), (3, 1)]
RELAY_BACK = [(0, 1), (1, 3), (2, 0), (3, 2)]


def contract_last(first, second):
    return lax.dot_general(first, second, (((1,), (1,)), ((), ())), preferred_element_type=F32)


def contract_first(first, second):
    return lax.dot_general(first, second, (((0,), (0,)), ((), ())), preferred_element_type=F32)


def together(operands, *earlier):
    return lax.optimization_barrier(tuple(operands) + earlier)[: len(operands)]


def after(x, *earlier):
    return together([x], *earlier)[0]


def joined(keep_order, first, second):
    return jnp.where(keep_order, jnp.concatenate([first, second]), jnp.concatenate([second, first]))


def halves(keep_order, x):
    n = x.shape[0] // 2
    return jnp.where(keep_order, x[:n], x[n:]), jnp.where(keep_order, x[n:], x[:n])


class Line:
    def __init__(self, axis):
        self.axis = axis
        self.i = lax.axis_index(axis)
        self.even = self.i % 2 == 0
        self.lower = self.i < 2
        self.inner = (self.i == 1) | (self.i == 2)

    def send(self, x, pairs):
        return lax.ppermute(x, self.axis, pairs)

    def near(self, x, got):
        return joined(self.even, x, got)

    def whole(self, near, middle, out):
        return joined(self.lower, near, jnp.where(self.inner, middle, out))

    def placed(self, whole, piece, bits):
        return lax.dynamic_update_slice(whole, piece, ((self.i ^ bits) * piece.shape[0], 0))

    def block(self, x, bits):
        n = x.shape[0] // 4
        return lax.dynamic_slice_in_dim(x, (self.i ^ bits) * n, n, 0)


def add(first, second):
    return (first.astype(F32) + second.astype(F32)).astype(first.dtype)


def products_kernel(order, *refs):
    parts = len(refs) // 2
    total = sum(contract_last(rows[...], right[...]) for rows, right in zip(refs[:parts], refs[parts:]))
    refs[-1][...] = total.astype(refs[-1].dtype)


def products(rows, half, right, order, start):
    height, depth = rows[0].shape[0] // 2, rows[0].shape[1]
    width = right[0].shape[0] // 8
    return pl.pallas_call(
        products_kernel,
        grid_spec=pltpu.PrefetchScalarGridSpec(
            num_scalar_prefetch=1,
            grid=(4,),
            in_specs=[pl.BlockSpec((height, depth), lambda b, order: (half, 0))] * len(rows)
            + [pl.BlockSpec((width, depth), lambda b, order: (order[start + b], 0))] * len(right),
            out_specs=pl.BlockSpec((height, width), lambda b, order: (0, b)),
        ),
        out_shape=jax.ShapeDtypeStruct((height, 4 * width), rows[0].dtype),
        compiler_params=pltpu.CompilerParams(vmem_limit_bytes=VMEM // 2),
        cost_estimate=QUICK,
    )(order, *rows, *right)


def scatter_columns(rows, right, axis):
    def swap(x, bit):
        return lax.ppermute(x, axis, [(j, j ^ bit) for j in range(8)])

    order = lax.axis_index(axis) ^ jnp.array([0, 2, 4, 6, 1, 3, 5, 7], jnp.int32)
    width = right[0].shape[0] // 8
    height = rows[0].shape[0] // 2
    low, high = slice(0, height // 2), slice(height // 2, height)

    def pair_sum(half, rows):
        away = products(rows, half, right, order, 4)
        got = swap(away, 1)
        return add(products(together(rows, away), half, right, order, 0), got)

    def block(x, b, rows):
        return x[rows, b * width : (b + 1) * width]

    def first_sends(x):
        return [
            jnp.concatenate([block(x, 1, low), block(x, 3, low)], axis=1),
            jnp.concatenate([block(x, 2, high), block(x, 3, high)], axis=1),
        ]

    def second_sends(x, by_x, by_y):
        return [add(block(x, 2, low), by_x[:, width:]), add(block(x, 1, high), by_y[:, width:])]

    def sums(x, by_x, by_y, then_y, then_x):
        total = lambda a, b, c: a.astype(F32) + b[:, :width].astype(F32) + c.astype(F32)
        return [total(block(x, 0, low), by_x, then_y), total(block(x, 0, high), by_y, then_x)]

    sum0 = pair_sum(0, rows)
    by_x0, by_y0 = together(first_sends(sum0))
    by_x0, by_y0 = swap(by_x0, 2), swap(by_y0, 4)
    sum1 = pair_sum(1, together(rows, sum0))
    then_y0, then_x0, by_x1, by_y1 = together(
        second_sends(sum0, *together([by_x0, by_y0], sum1)) + first_sends(sum1)
    )
    then_y0, then_x0 = swap(then_y0, 4), swap(then_x0, 2)
    by_x1, by_y1 = swap(by_x1, 2), swap(by_y1, 4)
    then_y1, then_x1 = together(second_sends(sum1, by_x1, by_y1))
    then_y1, then_x1 = swap(then_y1, 4), swap(then_x1, 2)
    kept = sums(sum0, by_x0, by_y0, then_y0, then_x0) + sums(sum1, by_x1, by_y1, then_y1, then_x1)
    return jnp.concatenate(kept).astype(sum0.dtype)


def moments(rotated, first_moment, second_moment):
    first_next = 0.9 * first_moment + 0.1 * rotated
    second_next = 0.95 * second_moment + 0.05 * rotated * rotated
    scaled_first = first_next / (1.0 - 0.9**10)
    scaled_second = second_next / (1.0 - 0.95**10)
    normalized = (scaled_first / (jnp.sqrt(scaled_second) + 1e-08)).astype(BF16)
    return first_next, second_next, normalized


STEPS = 2


def part_kernel(place, left, near, middle, out, first, second, basis, *rest, results):
    first_out, second_out, *backs, total, normalized = rest[-4 - results :]
    step = pl.program_id(0)

    @pl.when(step == 0)
    def _():
        total[...] = jnp.zeros_like(total)

    def accumulate(right):
        depth = left.shape[2]
        for b in range(left.shape[0]):
            total[...] += jnp.dot(left[b], right[b * depth : (b + 1) * depth, :], preferred_element_type=F32)

    @pl.when(step < STEPS)
    def _():
        accumulate(near)

    far = (step >= STEPS) & (step < 2 * STEPS)

    @pl.when(far & (place[2] == 1))
    def _():
        accumulate(middle)

    @pl.when(far & (place[2] == 0))
    def _():
        accumulate(out)

    @pl.when(step == 2 * STEPS - 1)
    def _():
        first_out[...], second_out[...], normalized[...] = moments(total[...], first[...], second[...])

    for number, back in enumerate(backs):

        @pl.when(step == 2 * STEPS + number)
        def _(back=back):
            back[...] = jnp.dot(basis[...], normalized[...], preferred_element_type=F32).astype(BF16)


def part(number, place, results, left_rotated, near, middle, out, first_moment, second_moment, left_cols, before):
    height, width = first_moment.shape
    size = near.shape[1]
    deep = near.shape[0] // STEPS
    tall = left_cols.shape[0] // results
    near_step = lambda s: jnp.minimum(s, STEPS - 1)
    far_step = lambda s: jnp.clip(s - STEPS, 0, STEPS - 1)
    last_step = lambda s: jnp.maximum(s - 2 * STEPS, 0)

    def left_block(s, place):
        return jnp.where(s < STEPS, place[0] + near_step(s), place[1] + far_step(s)), 0, 0

    moment = pl.BlockSpec((height, size), lambda s, place: (0, number))
    before = list(before)
    first_next, second_next, *backs = pl.pallas_call(
        functools.partial(part_kernel, results=results),
        grid_spec=pltpu.PrefetchScalarGridSpec(
            num_scalar_prefetch=1,
            grid=(2 * STEPS + results,),
            in_specs=[
                pl.BlockSpec((4 // STEPS, height, width), left_block),
                pl.BlockSpec((deep, size), lambda s, place: (near_step(s), 0)),
                pl.BlockSpec((deep, size), lambda s, place: (far_step(s) * place[2], 0)),
                pl.BlockSpec((deep, size), lambda s, place: (far_step(s) * (1 - place[2]), 0)),
                moment,
                moment,
                pl.BlockSpec((tall, height), lambda s, place: (place[3 + last_step(s)], 0)),
            ]
            + [pl.BlockSpec(memory_space=pl.ANY)] * len(before),
            out_specs=[moment, moment] + [pl.BlockSpec((tall, size), lambda s, place: (0, 0))] * results,
            scratch_shapes=[pltpu.VMEM((height, size), F32), pltpu.VMEM((height, size), BF16)],
        ),
        out_shape=[jax.ShapeDtypeStruct((height, width), F32)] * 2
        + [jax.ShapeDtypeStruct((tall, size), BF16)] * results,
        input_output_aliases={8: 0, 9: 1} if before else {},
        compiler_params=pltpu.CompilerParams(vmem_limit_bytes=VMEM),
        cost_estimate=QUICK,
    )(place, left_rotated, near, middle, out, first_moment, second_moment, left_cols, *before)
    return (first_next, second_next), backs


def body_on_line(gradient, left_stat, left_basis, right_basis, first_moment, second_moment):
    line = Line("row")
    send = line.send
    height, width = gradient.shape
    cuts = [slice(p * width // 3, (p + 1) * width // 3) for p in range(3)]
    left_cols = lax.all_gather(left_basis, "col", axis=0, tiled=True)
    own0, own1, own2 = [right_basis[:, cut] for cut in cuts]

    mirror = send(gradient, MIRROR)
    pair = send(gradient, PAIRS)
    relay = send(after(jnp.where(line.inner, mirror, gradient), pair), RELAY)
    turn = lambda x, bits: contract_first(line.block(left_cols, bits), x)
    left_sum = turn(gradient, 0) + turn(pair, 1) + turn(mirror, 3)
    pair0 = send(after(own0, left_sum), PAIRS)

    near0, own1 = together([line.near(own0, pair0), own1])
    middle0 = send(near0, MIDDLE)
    pair1 = send(own1, PAIRS)
    near1 = line.near(own1, pair1)
    pair2 = send(after(own2, near1), PAIRS)

    left_part = (left_sum + turn(after(relay, near0), 2)).astype(BF16)
    left_rotated = lax.all_gather(left_part, "col")

    middle0, near1 = together([middle0, near1], left_part, pair2)
    out0 = send(middle0, OUTWARD)
    middle1 = send(near1, MIDDLE)
    columns = jnp.zeros((4 * height, width), BF16)
    near2 = line.near(own2, pair2)
    for bits, piece in zip((0, 1, 3, 2), together([gradient, pair, mirror, relay], left_part, near2)):
        columns = line.placed(columns, piece, bits)
    product_here = contract_last(columns, gradient).astype(BF16)
    product = lax.psum_scatter(after(product_here, out0, middle1), "col", scatter_dimension=0, tiled=True)

    middle1, near2 = together([middle1, near2], out0, product_here)
    out1 = send(middle1, OUTWARD)
    middle2 = send(near2, MIDDLE)

    halves_first = jnp.where(line.lower, jnp.array([0, STEPS]), jnp.array([STEPS, 0]))
    far_near = jnp.where(line.lower, jnp.array([1, 0]), jnp.array([0, 1]))
    place = jnp.concatenate([halves_first, line.inner[None]]).astype(jnp.int32)
    to_halves = jnp.concatenate([place, far_near]).astype(jnp.int32)
    to_blocks = jnp.concatenate([place, line.i ^ jnp.array([2, 1, 3, 0])]).astype(jnp.int32)

    def next_part(number, near, middle, out, before):
        order, results = (to_blocks, 4) if number else (to_halves, 2)
        return part(
            number, order, results, left_rotated, near, middle, out, first_moment, second_moment, left_cols, before
        )

    def first_step(blocks):
        return send(blocks[0], RELAY_BACK), send(blocks[1], PAIRS)

    def to_mirror(blocks, relay):
        return add(blocks[2], jnp.where(line.inner, relay, 0))

    def summed(blocks, relay, pair, mirror):
        total = blocks[3].astype(F32) + jnp.where(line.inner, 0, relay).astype(F32)
        return (total + pair.astype(F32) + mirror.astype(F32)).astype(BF16)

    moments0, (far0, stay0) = next_part(0, near0, middle0, after(out0, near2), ())
    got0 = send(far0, INWARD)
    out2 = send(after(middle2, out1, far0), OUTWARD)
    moments1, blocks1 = next_part(1, near1, middle1, after(out1, far0), moments0)
    relay1, pair1 = first_step(blocks1)
    through0 = send(add(far0, after(got0, blocks1[0])), MIDDLE)
    relay1, out2 = together([relay1, out2])
    mirror1 = to_mirror(blocks1, relay1)
    moments2, blocks2 = next_part(2, near2, middle2, after(out2, mirror1), moments1)
    mirror1 = send(mirror1, MIRROR)
    relay2, pair2 = first_step(blocks2)
    turned1 = summed(blocks1, relay1, pair1, mirror1)
    mine0, other0 = halves(line.even, stay0.astype(F32) + after(through0, blocks2[0]).astype(F32))
    other0 = other0.astype(BF16)
    turned0 = (mine0 + send(other0, PAIRS).astype(F32)).astype(BF16)
    first_next, second_next = moments2

    out0, out1, out2, product = together([out0, out1, out2, product], other0)
    right = [line.whole(near0, middle0, out0), line.whole(near1, middle1, out1), line.whole(near2, middle2, out2)]
    mirror2 = send(to_mirror(blocks2, after(relay2, turned1, *right)), MIRROR)
    left_next = 0.95 * left_stat + 0.05 * product.astype(F32)
    turned2 = summed(blocks2, relay2, pair2, mirror2)

    right = together(right, left_next)
    direction = scatter_columns([turned0, turned1, turned2], right, "col")
    return (left_next, first_next, second_next, direction)


def body(gradient, left_stat, left_basis, right_basis, first_moment, second_moment):
    columns = lax.all_gather(gradient, "row", axis=0, tiled=True)
    left_cols = lax.all_gather(left_basis, "col", axis=0, tiled=True)
    right_cols = lax.all_gather(right_basis, "row", axis=0, tiled=True)
    left_rotated = lax.all_gather(contract_first(left_cols, columns).astype(BF16), "col", axis=1, tiled=True)
    product = contract_last(columns, gradient).astype(BF16)
    product = lax.psum_scatter(product, "col", scatter_dimension=0, tiled=True).astype(F32)
    left_next = 0.95 * left_stat + 0.05 * product
    rotated = jnp.dot(left_rotated, right_cols, preferred_element_type=F32)
    first_next, second_next, normalized = moments(rotated, first_moment, second_moment)
    back = jnp.dot(left_cols, normalized, preferred_element_type=F32).astype(BF16)
    back = lax.psum_scatter(back, "row", scatter_dimension=0, tiled=True)
    direction = contract_last(back, right_cols).astype(BF16)
    direction = lax.psum_scatter(direction, "col", scatter_dimension=1, tiled=True)
    return (left_next, first_next, second_next, direction)


def solution(mesh):
    on_line = mesh.shape["row"] == 4 and mesh.shape["col"] == 8
    return jax.shard_map(
        body_on_line if on_line else body,
        mesh=mesh,
        in_specs=(
            P("row", "col"),
            P("col", "row"),
            P("col", "row"),
            P("row", "col"),
            P("row", "col"),
            P("row", "col"),
        ),
        out_specs=(P("col", "row"), P("row", "col"), P("row", "col"), P("row", "col")),
        check_vma=False,
    )
```

```python
import functools

import jax
import jax.numpy as jnp
from jax import lax
from jax.experimental import pallas as pl
from jax.experimental.pallas import tpu as pltpu
from jax.sharding import PartitionSpec as P

BF16 = jnp.bfloat16
F32 = jnp.float32
VMEM = 60 * 2**20
QUICK = pl.CostEstimate(flops=2**20, bytes_accessed=2**16, transcendentals=0)

PAIRS = [(0, 1), (1, 0), (2, 3), (3, 2)]
MIDDLE = [(1, 2), (2, 1)]
OUTWARD = [(1, 0), (2, 3)]
INWARD = [(0, 1), (3, 2)]
MIRROR = [(0, 3), (1, 2), (2, 1), (3, 0)]
RELAY = [(0, 2), (1, 0), (2, 3), (3, 1)]
RELAY_BACK = [(0, 1), (1, 3), (2, 0), (3, 2)]


def contract_last(first, second):
    return lax.dot_general(first, second, (((1,), (1,)), ((), ())), preferred_element_type=F32)


def contract_first(first, second):
    return lax.dot_general(first, second, (((0,), (0,)), ((), ())), preferred_element_type=F32)


def together(operands, *earlier):
    return lax.optimization_barrier(tuple(operands) + earlier)[: len(operands)]


def after(x, *earlier):
    return together([x], *earlier)[0]


def joined(keep_order, first, second):
    return jnp.where(keep_order, jnp.concatenate([first, second]), jnp.concatenate([second, first]))


def halves(keep_order, x):
    n = x.shape[0] // 2
    return jnp.where(keep_order, x[:n], x[n:]), jnp.where(keep_order, x[n:], x[:n])


class Line:
    def __init__(self, axis):
        self.axis = axis
        self.i = lax.axis_index(axis)
        self.even = self.i % 2 == 0
        self.lower = self.i < 2
        self.inner = (self.i == 1) | (self.i == 2)

    def send(self, x, pairs):
        return lax.ppermute(x, self.axis, pairs)

    def near(self, x, got):
        return joined(self.even, x, got)

    def whole(self, near, middle, out):
        return joined(self.lower, near, jnp.where(self.inner, middle, out))

    def placed(self, whole, piece, bits):
        return lax.dynamic_update_slice(whole, piece, ((self.i ^ bits) * piece.shape[0], 0))

    def block(self, x, bits):
        n = x.shape[0] // 4
        return lax.dynamic_slice_in_dim(x, (self.i ^ bits) * n, n, 0)


def add(first, second):
    return (first.astype(F32) + second.astype(F32)).astype(first.dtype)


def products_kernel(order, *refs):
    parts = len(refs) // 2
    total = sum(contract_last(rows[...], right[...]) for rows, right in zip(refs[:parts], refs[parts:]))
    refs[-1][...] = total.astype(refs[-1].dtype)


def products(rows, half, right, order, start):
    height, depth = rows[0].shape[0] // 2, rows[0].shape[1]
    width = right[0].shape[0] // 8
    return pl.pallas_call(
        products_kernel,
        grid_spec=pltpu.PrefetchScalarGridSpec(
            num_scalar_prefetch=1,
            grid=(4,),
            in_specs=[pl.BlockSpec((height, depth), lambda b, order: (half, 0))] * len(rows)
            + [pl.BlockSpec((width, depth), lambda b, order: (order[start + b], 0))] * len(right),
            out_specs=pl.BlockSpec((height, width), lambda b, order: (0, b)),
        ),
        out_shape=jax.ShapeDtypeStruct((height, 4 * width), rows[0].dtype),
        compiler_params=pltpu.CompilerParams(vmem_limit_bytes=VMEM // 2),
        cost_estimate=QUICK,
    )(order, *rows, *right)


def scatter_columns(rows, right, axis):
    def swap(x, bit):
        return lax.ppermute(x, axis, [(j, j ^ bit) for j in range(8)])

    order = lax.axis_index(axis) ^ jnp.array([0, 2, 4, 6, 1, 3, 5, 7], jnp.int32)
    width = right[0].shape[0] // 8
    height = rows[0].shape[0] // 2
    low, high = slice(0, height // 2), slice(height // 2, height)

    def pair_sum(half, rows):
        away = products(rows, half, right, order, 4)
        got = swap(away, 1)
        return add(products(together(rows, away), half, right, order, 0), got)

    def block(x, b, rows):
        return x[rows, b * width : (b + 1) * width]

    def first_sends(x):
        return [
            jnp.concatenate([block(x, 1, low), block(x, 3, low)], axis=1),
            jnp.concatenate([block(x, 2, high), block(x, 3, high)], axis=1),
        ]

    def second_sends(x, by_x, by_y):
        return [add(block(x, 2, low), by_x[:, width:]), add(block(x, 1, high), by_y[:, width:])]

    def sums(x, by_x, by_y, then_y, then_x):
        total = lambda a, b, c: a.astype(F32) + b[:, :width].astype(F32) + c.astype(F32)
        return [total(block(x, 0, low), by_x, then_y), total(block(x, 0, high), by_y, then_x)]

    sum0 = pair_sum(0, rows)
    by_x0, by_y0 = together(first_sends(sum0))
    by_x0, by_y0 = swap(by_x0, 2), swap(by_y0, 4)
    sum1 = pair_sum(1, together(rows, sum0))
    then_y0, then_x0, by_x1, by_y1 = together(
        second_sends(sum0, *together([by_x0, by_y0], sum1)) + first_sends(sum1)
    )
    then_y0, then_x0 = swap(then_y0, 4), swap(then_x0, 2)
    by_x1, by_y1 = swap(by_x1, 2), swap(by_y1, 4)
    then_y1, then_x1 = together(second_sends(sum1, by_x1, by_y1))
    then_y1, then_x1 = swap(then_y1, 4), swap(then_x1, 2)
    kept = sums(sum0, by_x0, by_y0, then_y0, then_x0) + sums(sum1, by_x1, by_y1, then_y1, then_x1)
    return jnp.concatenate(kept).astype(sum0.dtype)


def moments(rotated, first_moment, second_moment):
    first_next = 0.9 * first_moment + 0.1 * rotated
    second_next = 0.95 * second_moment + 0.05 * rotated * rotated
    scaled_first = first_next / (1.0 - 0.9**10)
    scaled_second = second_next / (1.0 - 0.95**10)
    normalized = (scaled_first / (jnp.sqrt(scaled_second) + 1e-08)).astype(BF16)
    return first_next, second_next, normalized


STEPS = 2


def part_kernel(place, left, near, middle, out, first, second, basis, *rest, results):
    first_out, second_out, *backs, total, normalized = rest[-4 - results :]
    step = pl.program_id(0)

    @pl.when(step == 0)
    def _():
        total[...] = jnp.zeros_like(total)

    def accumulate(right):
        depth = left.shape[2]
        for b in range(left.shape[0]):
            total[...] += jnp.dot(left[b], right[b * depth : (b + 1) * depth, :], preferred_element_type=F32)

    @pl.when(step < STEPS)
    def _():
        accumulate(near)

    far = (step >= STEPS) & (step < 2 * STEPS)

    @pl.when(far & (place[2] == 1))
    def _():
        accumulate(middle)

    @pl.when(far & (place[2] == 0))
    def _():
        accumulate(out)

    @pl.when(step == 2 * STEPS - 1)
    def _():
        first_out[...], second_out[...], normalized[...] = moments(total[...], first[...], second[...])

    for number, back in enumerate(backs):

        @pl.when(step == 2 * STEPS + number)
        def _(back=back):
            back[...] = jnp.dot(basis[...], normalized[...], preferred_element_type=F32).astype(BF16)


def part(number, place, results, left_rotated, near, middle, out, first_moment, second_moment, left_cols, before):
    height, width = first_moment.shape
    size = near.shape[1]
    deep = near.shape[0] // STEPS
    tall = left_cols.shape[0] // results
    near_step = lambda s: jnp.minimum(s, STEPS - 1)
    far_step = lambda s: jnp.clip(s - STEPS, 0, STEPS - 1)
    last_step = lambda s: jnp.maximum(s - 2 * STEPS, 0)

    def left_block(s, place):
        return jnp.where(s < STEPS, place[0] + near_step(s), place[1] + far_step(s)), 0, 0

    moment = pl.BlockSpec((height, size), lambda s, place: (0, number))
    before = list(before)
    first_next, second_next, *backs = pl.pallas_call(
        functools.partial(part_kernel, results=results),
        grid_spec=pltpu.PrefetchScalarGridSpec(
            num_scalar_prefetch=1,
            grid=(2 * STEPS + results,),
            in_specs=[
                pl.BlockSpec((4 // STEPS, height, width), left_block),
                pl.BlockSpec((deep, size), lambda s, place: (near_step(s), 0)),
                pl.BlockSpec((deep, size), lambda s, place: (far_step(s) * place[2], 0)),
                pl.BlockSpec((deep, size), lambda s, place: (far_step(s) * (1 - place[2]), 0)),
                moment,
                moment,
                pl.BlockSpec((tall, height), lambda s, place: (place[3 + last_step(s)], 0)),
            ]
            + [pl.BlockSpec(memory_space=pl.ANY)] * len(before),
            out_specs=[moment, moment] + [pl.BlockSpec((tall, size), lambda s, place: (0, 0))] * results,
            scratch_shapes=[pltpu.VMEM((height, size), F32), pltpu.VMEM((height, size), BF16)],
        ),
        out_shape=[jax.ShapeDtypeStruct((height, width), F32)] * 2
        + [jax.ShapeDtypeStruct((tall, size), BF16)] * results,
        input_output_aliases={8: 0, 9: 1} if before else {},
        compiler_params=pltpu.CompilerParams(vmem_limit_bytes=VMEM),
        cost_estimate=QUICK,
    )(place, left_rotated, near, middle, out, first_moment, second_moment, left_cols, *before)
    return (first_next, second_next), backs


def body_on_line(gradient, left_stat, left_basis, right_basis, first_moment, second_moment):
    line = Line("row")
    send = line.send
    height, width = gradient.shape
    cuts = [slice(p * width // 3, (p + 1) * width // 3) for p in range(3)]
    left_cols = lax.all_gather(left_basis, "col", axis=0, tiled=True)
    own0, own1, own2 = [right_basis[:, cut] for cut in cuts]

    mirror = send(gradient, MIRROR)
    pair = send(gradient, PAIRS)
    relay = send(after(jnp.where(line.inner, mirror, gradient), pair), RELAY)
    turn = lambda x, bits: contract_first(line.block(left_cols, bits), x)
    left_sum = turn(gradient, 0) + turn(pair, 1) + turn(mirror, 3)
    pair0 = send(after(own0, left_sum), PAIRS)

    near0, own1 = together([line.near(own0, pair0), own1])
    middle0 = send(near0, MIDDLE)
    pair1 = send(own1, PAIRS)
    near1 = line.near(own1, pair1)
    pair2 = send(after(own2, near1), PAIRS)

    left_part = (left_sum + turn(after(relay, near0), 2)).astype(BF16)
    left_rotated = lax.all_gather(left_part, "col")

    middle0, near1 = together([middle0, near1], left_part, pair2)
    out0 = send(middle0, OUTWARD)
    middle1 = send(near1, MIDDLE)
    columns = jnp.zeros((4 * height, width), BF16)
    near2 = line.near(own2, pair2)
    for bits, piece in zip((0, 1, 3, 2), together([gradient, pair, mirror, relay], left_part, near2)):
        columns = line.placed(columns, piece, bits)
    product_here = contract_last(columns, gradient).astype(BF16)
    product = lax.psum_scatter(after(product_here, out0, middle1), "col", scatter_dimension=0, tiled=True)

    middle1, near2 = together([middle1, near2], out0, product_here)
    out1 = send(middle1, OUTWARD)
    middle2 = send(near2, MIDDLE)

    halves_first = jnp.where(line.lower, jnp.array([0, STEPS]), jnp.array([STEPS, 0]))
    far_near = jnp.where(line.lower, jnp.array([1, 0]), jnp.array([0, 1]))
    place = jnp.concatenate([halves_first, line.inner[None]]).astype(jnp.int32)
    to_halves = jnp.concatenate([place, far_near]).astype(jnp.int32)
    to_blocks = jnp.concatenate([place, line.i ^ jnp.array([2, 1, 3, 0])]).astype(jnp.int32)

    def next_part(number, near, middle, out, before):
        order, results = (to_blocks, 4) if number == 2 else (to_halves, 2)
        return part(
            number, order, results, left_rotated, near, middle, out, first_moment, second_moment, left_cols, before
        )

    moments0, (far0, stay0) = next_part(0, near0, middle0, after(out0, near2), ())
    got0 = send(far0, INWARD)
    out2 = send(after(middle2, out1, far0), OUTWARD)
    moments1, (far1, stay1) = next_part(1, near1, middle1, after(out1, far0), moments0)
    got1 = send(far1, INWARD)
    through0 = send(add(far0, after(got0, far1)), MIDDLE)
    got1, out2 = together([got1, out2])
    through1 = add(far1, got1)
    mine0, other0 = halves(line.even, stay0.astype(F32) + after(through0, through1).astype(F32))
    other0 = other0.astype(BF16)
    moments2, blocks2 = next_part(2, near2, middle2, after(out2, other0, through1), moments1)
    other0 = send(other0, PAIRS)
    turned0 = (mine0 + other0.astype(F32)).astype(BF16)
    through1 = send(through1, MIDDLE)
    mine1, other1 = halves(line.even, stay1.astype(F32) + through1.astype(F32))
    turned1 = (mine1 + send(other1.astype(BF16), PAIRS).astype(F32)).astype(BF16)
    first_next, second_next = moments2

    to_relay, to_pair, to_mirror, own = blocks2
    relay = send(to_relay, RELAY_BACK)
    pair = send(to_pair, PAIRS)
    relay = after(relay, through1, other0)
    mirror = send(add(to_mirror, jnp.where(line.inner, relay, 0)), MIRROR)
    out0, out1, out2, product = together([out0, out1, out2, product], turned0)
    right = [line.whole(near0, middle0, out0), line.whole(near1, middle1, out1), line.whole(near2, middle2, out2)]
    left_next = 0.95 * left_stat + 0.05 * product.astype(F32)
    mirror, pair = together([mirror, pair], *right)
    turned2 = own.astype(F32) + jnp.where(line.inner, 0, relay).astype(F32)
    turned2 = (turned2 + pair.astype(F32) + mirror.astype(F32)).astype(BF16)

    right = together(right, left_next)
    direction = scatter_columns([turned0, turned1, turned2], right, "col")
    return (left_next, first_next, second_next, direction)


def body(gradient, left_stat, left_basis, right_basis, first_moment, second_moment):
    columns = lax.all_gather(gradient, "row", axis=0, tiled=True)
    left_cols = lax.all_gather(left_basis, "col", axis=0, tiled=True)
    right_cols = lax.all_gather(right_basis, "row", axis=0, tiled=True)
    left_rotated = lax.all_gather(contract_first(left_cols, columns).astype(BF16), "col", axis=1, tiled=True)
    product = contract_last(columns, gradient).astype(BF16)
    product = lax.psum_scatter(product, "col", scatter_dimension=0, tiled=True).astype(F32)
    left_next = 0.95 * left_stat + 0.05 * product
    rotated = jnp.dot(left_rotated, right_cols, preferred_element_type=F32)
    first_next, second_next, normalized = moments(rotated, first_moment, second_moment)
    back = jnp.dot(left_cols, normalized, preferred_element_type=F32).astype(BF16)
    back = lax.psum_scatter(back, "row", scatter_dimension=0, tiled=True)
    direction = contract_last(back, right_cols).astype(BF16)
    direction = lax.psum_scatter(direction, "col", scatter_dimension=1, tiled=True)
    return (left_next, first_next, second_next, direction)


def solution(mesh):
    on_line = mesh.shape["row"] == 4 and mesh.shape["col"] == 8
    return jax.shard_map(
        body_on_line if on_line else body,
        mesh=mesh,
        in_specs=(
            P("row", "col"),
            P("col", "row"),
            P("col", "row"),
            P("row", "col"),
            P("row", "col"),
            P("row", "col"),
        ),
        out_specs=(P("col", "row"), P("row", "col"), P("row", "col"), P("row", "col")),
        check_vma=False,
    )
```

```python
import functools

import jax
import jax.numpy as jnp
from jax import lax
from jax.experimental import pallas as pl
from jax.experimental.pallas import tpu as pltpu
from jax.sharding import PartitionSpec as P

BF16 = jnp.bfloat16
F32 = jnp.float32
VMEM = 60 * 2**20
QUICK = pl.CostEstimate(flops=2**20, bytes_accessed=2**16, transcendentals=0)

PAIRS = [(0, 1), (1, 0), (2, 3), (3, 2)]
MIDDLE = [(1, 2), (2, 1)]
OUTWARD = [(1, 0), (2, 3)]
INWARD = [(0, 1), (3, 2)]
MIRROR = [(0, 3), (1, 2), (2, 1), (3, 0)]
RELAY = [(0, 2), (1, 0), (2, 3), (3, 1)]
RELAY_BACK = [(0, 1), (1, 3), (2, 0), (3, 2)]


def contract_last(first, second):
    return lax.dot_general(first, second, (((1,), (1,)), ((), ())), preferred_element_type=F32)


def contract_first(first, second):
    return lax.dot_general(first, second, (((0,), (0,)), ((), ())), preferred_element_type=F32)


def together(operands, *earlier):
    return lax.optimization_barrier(tuple(operands) + earlier)[: len(operands)]


def after(x, *earlier):
    return together([x], *earlier)[0]


def joined(keep_order, first, second):
    return jnp.where(keep_order, jnp.concatenate([first, second]), jnp.concatenate([second, first]))


def halves(keep_order, x):
    n = x.shape[0] // 2
    return jnp.where(keep_order, x[:n], x[n:]), jnp.where(keep_order, x[n:], x[:n])


class Line:
    def __init__(self, axis):
        self.axis = axis
        self.i = lax.axis_index(axis)
        self.even = self.i % 2 == 0
        self.lower = self.i < 2
        self.inner = (self.i == 1) | (self.i == 2)

    def send(self, x, pairs):
        return lax.ppermute(x, self.axis, pairs)

    def near(self, x, got):
        return joined(self.even, x, got)

    def whole(self, near, middle, out):
        return joined(self.lower, near, jnp.where(self.inner, middle, out))

    def placed(self, whole, piece, bits):
        return lax.dynamic_update_slice(whole, piece, ((self.i ^ bits) * piece.shape[0], 0))

    def block(self, x, bits):
        n = x.shape[0] // 4
        return lax.dynamic_slice_in_dim(x, (self.i ^ bits) * n, n, 0)


def add(first, second):
    return (first.astype(F32) + second.astype(F32)).astype(first.dtype)


def products_kernel(order, *refs):
    parts = len(refs) // 2
    total = sum(contract_last(rows[...], right[...]) for rows, right in zip(refs[:parts], refs[parts:]))
    refs[-1][...] = total.astype(refs[-1].dtype)


def products(rows, half, right, order, start):
    height, depth = rows[-1].shape
    width = right[0].shape[0] // 8
    return pl.pallas_call(
        products_kernel,
        grid_spec=pltpu.PrefetchScalarGridSpec(
            num_scalar_prefetch=1,
            grid=(4,),
            in_specs=[pl.BlockSpec((height, depth), lambda b, order: (half, 0))] * (len(rows) - 1)
            + [pl.BlockSpec((height, depth), lambda b, order: (0, 0))]
            + [pl.BlockSpec((width, depth), lambda b, order: (order[start + b], 0))] * len(right),
            out_specs=pl.BlockSpec((height, width), lambda b, order: (0, b)),
        ),
        out_shape=jax.ShapeDtypeStruct((height, 4 * width), rows[0].dtype),
        compiler_params=pltpu.CompilerParams(vmem_limit_bytes=VMEM // 2),
        cost_estimate=QUICK,
    )(order, *rows, *right)


def scatter_columns(rows, rows_low, rows_high, right, axis):
    def swap(x, bit):
        return lax.ppermute(x, axis, [(j, j ^ bit) for j in range(8)])

    order = lax.axis_index(axis) ^ jnp.array([0, 2, 4, 6, 1, 3, 5, 7], jnp.int32)
    width = right[0].shape[0] // 8
    height = rows_low.shape[0]
    low, high = slice(0, height // 2), slice(height // 2, height)

    def pair_sum(half, rows):
        away = products(rows, half, right, order, 4)
        got = swap(away, 1)
        return add(products(together(rows, away), half, right, order, 0), got)

    def block(x, b, rows):
        return x[rows, b * width : (b + 1) * width]

    def first_sends(x):
        return [
            jnp.concatenate([block(x, 1, low), block(x, 3, low)], axis=1),
            jnp.concatenate([block(x, 2, high), block(x, 3, high)], axis=1),
        ]

    def second_sends(x, by_x, by_y):
        return [add(block(x, 2, low), by_x[:, width:]), add(block(x, 1, high), by_y[:, width:])]

    def sums(x, by_x, by_y, then_y, then_x):
        total = lambda a, b, c: a.astype(F32) + b[:, :width].astype(F32) + c.astype(F32)
        return [total(block(x, 0, low), by_x, then_y), total(block(x, 0, high), by_y, then_x)]

    sum0 = pair_sum(0, rows + [rows_low])
    by_x0, by_y0 = together(first_sends(sum0))
    by_x0, by_y0 = swap(by_x0, 2), swap(by_y0, 4)
    then_y0, then_x0 = together(second_sends(sum0, by_x0, by_y0))
    sum1 = pair_sum(1, rows + [rows_high(then_y0)])
    then_y0, then_x0 = swap(then_y0, 4), swap(then_x0, 2)
    by_x1, by_y1 = together(first_sends(sum1), then_y0, then_x0)
    by_x1, by_y1 = swap(by_x1, 2), swap(by_y1, 4)
    then_y1, then_x1 = together(second_sends(sum1, by_x1, by_y1))
    then_y1, then_x1 = swap(then_y1, 4), swap(then_x1, 2)
    kept = sums(sum0, by_x0, by_y0, then_y0, then_x0) + sums(sum1, by_x1, by_y1, then_y1, then_x1)
    return jnp.concatenate(kept).astype(sum0.dtype)


def moments(rotated, first_moment, second_moment):
    first_next = 0.9 * first_moment + 0.1 * rotated
    second_next = 0.95 * second_moment + 0.05 * rotated * rotated
    scaled_first = first_next / (1.0 - 0.9**10)
    scaled_second = second_next / (1.0 - 0.95**10)
    normalized = (scaled_first / (jnp.sqrt(scaled_second) + 1e-08)).astype(BF16)
    return first_next, second_next, normalized


STEPS = 2


def part_kernel(place, left, near, middle, out, first, second, basis, *rest, results):
    first_out, second_out, *backs, total, normalized = rest[-4 - results :]
    step = pl.program_id(0)

    @pl.when(step == 0)
    def _():
        total[...] = jnp.zeros_like(total)

    def accumulate(right):
        depth = left.shape[2]
        for b in range(left.shape[0]):
            total[...] += jnp.dot(left[b], right[b * depth : (b + 1) * depth, :], preferred_element_type=F32)

    @pl.when(step < STEPS)
    def _():
        accumulate(near)

    far = (step >= STEPS) & (step < 2 * STEPS)

    @pl.when(far & (place[2] == 1))
    def _():
        accumulate(middle)

    @pl.when(far & (place[2] == 0))
    def _():
        accumulate(out)

    @pl.when(step == 2 * STEPS - 1)
    def _():
        first_out[...], second_out[...], normalized[...] = moments(total[...], first[...], second[...])

    for number, back in enumerate(backs):

        @pl.when(step == 2 * STEPS + number)
        def _(back=back):
            back[...] = jnp.dot(basis[...], normalized[...], preferred_element_type=F32).astype(BF16)


def part(number, place, results, left_rotated, near, middle, out, first_moment, second_moment, left_cols, before):
    height, width = first_moment.shape
    size = near.shape[1]
    deep = near.shape[0] // STEPS
    tall = left_cols.shape[0] // results
    near_step = lambda s: jnp.minimum(s, STEPS - 1)
    far_step = lambda s: jnp.clip(s - STEPS, 0, STEPS - 1)
    last_step = lambda s: jnp.maximum(s - 2 * STEPS, 0)

    def left_block(s, place):
        return jnp.where(s < STEPS, place[0] + near_step(s), place[1] + far_step(s)), 0, 0

    moment = pl.BlockSpec((height, size), lambda s, place: (0, number))
    before = list(before)
    first_next, second_next, *backs = pl.pallas_call(
        functools.partial(part_kernel, results=results),
        grid_spec=pltpu.PrefetchScalarGridSpec(
            num_scalar_prefetch=1,
            grid=(2 * STEPS + results,),
            in_specs=[
                pl.BlockSpec((4 // STEPS, height, width), left_block),
                pl.BlockSpec((deep, size), lambda s, place: (near_step(s), 0)),
                pl.BlockSpec((deep, size), lambda s, place: (far_step(s) * place[2], 0)),
                pl.BlockSpec((deep, size), lambda s, place: (far_step(s) * (1 - place[2]), 0)),
                moment,
                moment,
                pl.BlockSpec((tall, height), lambda s, place: (place[3 + last_step(s)], 0)),
            ]
            + [pl.BlockSpec(memory_space=pl.ANY)] * len(before),
            out_specs=[moment, moment] + [pl.BlockSpec((tall, size), lambda s, place: (0, 0))] * results,
            scratch_shapes=[pltpu.VMEM((height, size), F32), pltpu.VMEM((height, size), BF16)],
        ),
        out_shape=[jax.ShapeDtypeStruct((height, width), F32)] * 2
        + [jax.ShapeDtypeStruct((tall, size), BF16)] * results,
        input_output_aliases={8: 0, 9: 1} if before else {},
        compiler_params=pltpu.CompilerParams(vmem_limit_bytes=VMEM),
        cost_estimate=QUICK,
    )(place, left_rotated, near, middle, out, first_moment, second_moment, left_cols, *before)
    return (first_next, second_next), backs


def body_on_line(gradient, left_stat, left_basis, right_basis, first_moment, second_moment):
    line = Line("row")
    send = line.send
    height, width = gradient.shape
    cuts = [slice(p * width // 3, (p + 1) * width // 3) for p in range(3)]
    left_cols = lax.all_gather(left_basis, "col", axis=0, tiled=True)
    own0, own1, own2 = [right_basis[:, cut] for cut in cuts]

    mirror = send(gradient, MIRROR)
    pair = send(gradient, PAIRS)
    relay = send(after(jnp.where(line.inner, mirror, gradient), pair), RELAY)
    turn = lambda x, bits: contract_first(line.block(left_cols, bits), x)
    left_sum = turn(gradient, 0) + turn(pair, 1) + turn(mirror, 3)
    pair0 = send(after(own0, left_sum), PAIRS)

    near0, own1 = together([line.near(own0, pair0), own1])
    middle0 = send(near0, MIDDLE)
    pair1 = send(own1, PAIRS)
    near1 = line.near(own1, pair1)
    pair2 = send(after(own2, near1), PAIRS)

    left_part = (left_sum + turn(after(relay, near0), 2)).astype(BF16)
    left_rotated = lax.all_gather(left_part, "col")

    middle0, near1 = together([middle0, near1], left_part, pair2)
    out0 = send(middle0, OUTWARD)
    middle1 = send(near1, MIDDLE)
    columns = jnp.zeros((4 * height, width), BF16)
    near2 = line.near(own2, pair2)
    for bits, piece in zip((0, 1, 3, 2), together([gradient, pair, mirror, relay], left_part, near2)):
        columns = line.placed(columns, piece, bits)
    product_here = contract_last(columns, gradient).astype(BF16)
    product = lax.psum_scatter(after(product_here, out0, middle1), "col", scatter_dimension=0, tiled=True)

    middle1, near2 = together([middle1, near2], out0, product_here)
    out1 = send(middle1, OUTWARD)
    middle2 = send(near2, MIDDLE)

    halves_first = jnp.where(line.lower, jnp.array([0, STEPS]), jnp.array([STEPS, 0]))
    far_near = jnp.where(line.lower, jnp.array([1, 0]), jnp.array([0, 1]))
    place = jnp.concatenate([halves_first, line.inner[None]]).astype(jnp.int32)
    to_halves = jnp.concatenate([place, far_near]).astype(jnp.int32)
    to_blocks = jnp.concatenate([place, line.i ^ jnp.array([2, 1, 3, 0])]).astype(jnp.int32)

    def next_part(number, near, middle, out, before):
        order, results = (to_blocks, 4) if number == 2 else (to_halves, 2)
        return part(
            number, order, results, left_rotated, near, middle, out, first_moment, second_moment, left_cols, before
        )

    moments0, (far0, stay0) = next_part(0, near0, middle0, after(out0, near2), ())
    got0 = send(far0, INWARD)
    out2 = send(after(middle2, out1, far0), OUTWARD)
    moments1, (far1, stay1) = next_part(1, near1, middle1, after(out1, far0), moments0)
    got1 = send(far1, INWARD)
    through0 = send(add(far0, after(got0, far1)), MIDDLE)
    got1, out2 = together([got1, out2])
    through1 = add(far1, got1)
    mine0, other0 = halves(line.even, stay0.astype(F32) + after(through0, through1).astype(F32))
    other0 = other0.astype(BF16)
    moments2, blocks2 = next_part(2, near2, middle2, after(out2, other0, through1), moments1)
    other0 = send(other0, PAIRS)
    turned0 = (mine0 + other0.astype(F32)).astype(BF16)
    through1 = send(through1, MIDDLE)
    mine1, other1 = halves(line.even, stay1.astype(F32) + through1.astype(F32))
    turned1 = (mine1 + send(other1.astype(BF16), PAIRS).astype(F32)).astype(BF16)
    first_next, second_next = moments2

    half = height // 2
    low, high = [x[:half] for x in blocks2], [x[half:] for x in blocks2]

    def summed(blocks, relay, pair, mirror):
        total = blocks[3].astype(F32) + jnp.where(line.inner, 0, relay).astype(F32)
        return (total + pair.astype(F32) + mirror.astype(F32)).astype(BF16)

    relay_low = send(low[0], RELAY_BACK)
    pair_low = send(low[1], PAIRS)
    relay_low = after(relay_low, through1, other0)
    to_mirror = add(low[2], jnp.where(line.inner, relay_low, 0))
    mirror_low = send(to_mirror, MIRROR)
    to_relay, to_pair = together(high[:2], relay_low)
    relay_high = send(to_relay, RELAY_BACK)
    pair_high = send(to_pair, PAIRS)
    out0, out1, out2, product = together([out0, out1, out2, product], turned0)
    right = [line.whole(near0, middle0, out0), line.whole(near1, middle1, out1), line.whole(near2, middle2, out2)]
    left_next = 0.95 * left_stat + 0.05 * product.astype(F32)
    relay_high = after(relay_high, to_mirror)
    mirror_high = send(add(high[2], jnp.where(line.inner, relay_high, 0)), MIRROR)
    turned_low = summed(low, relay_low, pair_low, after(mirror_low, *right))

    def turned_high(earlier):
        return summed(high, relay_high, pair_high, after(mirror_high, earlier))

    right = together(right, left_next)
    direction = scatter_columns([turned0, turned1], turned_low, turned_high, right, "col")
    return (left_next, first_next, second_next, direction)


def body(gradient, left_stat, left_basis, right_basis, first_moment, second_moment):
    columns = lax.all_gather(gradient, "row", axis=0, tiled=True)
    left_cols = lax.all_gather(left_basis, "col", axis=0, tiled=True)
    right_cols = lax.all_gather(right_basis, "row", axis=0, tiled=True)
    left_rotated = lax.all_gather(contract_first(left_cols, columns).astype(BF16), "col", axis=1, tiled=True)
    product = contract_last(columns, gradient).astype(BF16)
    product = lax.psum_scatter(product, "col", scatter_dimension=0, tiled=True).astype(F32)
    left_next = 0.95 * left_stat + 0.05 * product
    rotated = jnp.dot(left_rotated, right_cols, preferred_element_type=F32)
    first_next, second_next, normalized = moments(rotated, first_moment, second_moment)
    back = jnp.dot(left_cols, normalized, preferred_element_type=F32).astype(BF16)
    back = lax.psum_scatter(back, "row", scatter_dimension=0, tiled=True)
    direction = contract_last(back, right_cols).astype(BF16)
    direction = lax.psum_scatter(direction, "col", scatter_dimension=1, tiled=True)
    return (left_next, first_next, second_next, direction)


def solution(mesh):
    on_line = mesh.shape["row"] == 4 and mesh.shape["col"] == 8
    return jax.shard_map(
        body_on_line if on_line else body,
        mesh=mesh,
        in_specs=(
            P("row", "col"),
            P("col", "row"),
            P("col", "row"),
            P("row", "col"),
            P("row", "col"),
            P("row", "col"),
        ),
        out_specs=(P("col", "row"), P("row", "col"), P("row", "col"), P("row", "col")),
        check_vma=False,
    )
```

```python
import functools

import jax
import jax.numpy as jnp
from jax import lax
from jax.experimental import pallas as pl
from jax.experimental.pallas import tpu as pltpu
from jax.sharding import PartitionSpec as P

BF16 = jnp.bfloat16
F32 = jnp.float32
VMEM = 60 * 2**20
QUICK = pl.CostEstimate(flops=2**20, bytes_accessed=2**16, transcendentals=0)

PAIRS = [(0, 1), (1, 0), (2, 3), (3, 2)]
MIDDLE = [(1, 2), (2, 1)]
OUTWARD = [(1, 0), (2, 3)]
INWARD = [(0, 1), (3, 2)]
MIRROR = [(0, 3), (1, 2), (2, 1), (3, 0)]
RELAY = [(0, 2), (1, 0), (2, 3), (3, 1)]
RELAY_BACK = [(0, 1), (1, 3), (2, 0), (3, 2)]


def contract_last(first, second):
    return lax.dot_general(first, second, (((1,), (1,)), ((), ())), preferred_element_type=F32)


def contract_first(first, second):
    return lax.dot_general(first, second, (((0,), (0,)), ((), ())), preferred_element_type=F32)


def together(operands, *earlier):
    return lax.optimization_barrier(tuple(operands) + earlier)[: len(operands)]


def after(x, *earlier):
    return together([x], *earlier)[0]


def joined(keep_order, first, second):
    return jnp.where(keep_order, jnp.concatenate([first, second]), jnp.concatenate([second, first]))


def halves(keep_order, x):
    n = x.shape[0] // 2
    return jnp.where(keep_order, x[:n], x[n:]), jnp.where(keep_order, x[n:], x[:n])


class Line:
    def __init__(self, axis):
        self.axis = axis
        self.i = lax.axis_index(axis)
        self.even = self.i % 2 == 0
        self.lower = self.i < 2
        self.inner = (self.i == 1) | (self.i == 2)

    def send(self, x, pairs):
        return lax.ppermute(x, self.axis, pairs)

    def near(self, x, got):
        return joined(self.even, x, got)

    def whole(self, near, middle, out):
        return joined(self.lower, near, jnp.where(self.inner, middle, out))

    def placed(self, whole, piece, bits):
        return lax.dynamic_update_slice(whole, piece, ((self.i ^ bits) * piece.shape[0], 0))

    def block(self, x, bits):
        n = x.shape[0] // 4
        return lax.dynamic_slice_in_dim(x, (self.i ^ bits) * n, n, 0)


def add(first, second):
    return (first.astype(F32) + second.astype(F32)).astype(first.dtype)


def products_kernel(order, *refs):
    parts = len(refs) // 2
    total = sum(contract_last(rows[...], right[...]) for rows, right in zip(refs[:parts], refs[parts:]))
    refs[-1][...] = total.astype(refs[-1].dtype)


def products(rows, half, right, order, start):
    height, depth = rows[-1].shape
    width = right[0].shape[0] // 8
    return pl.pallas_call(
        products_kernel,
        grid_spec=pltpu.PrefetchScalarGridSpec(
            num_scalar_prefetch=1,
            grid=(4,),
            in_specs=[pl.BlockSpec((height, depth), lambda b, order: (half, 0))] * (len(rows) - 1)
            + [pl.BlockSpec((height, depth), lambda b, order: (0, 0))]
            + [pl.BlockSpec((width, depth), lambda b, order: (order[start + b], 0))] * len(right),
            out_specs=pl.BlockSpec((height, width), lambda b, order: (0, b)),
        ),
        out_shape=jax.ShapeDtypeStruct((height, 4 * width), rows[0].dtype),
        compiler_params=pltpu.CompilerParams(vmem_limit_bytes=VMEM // 2),
        cost_estimate=QUICK,
    )(order, *rows, *right)


def scatter_columns(rows, rows_low, rows_high, right, axis):
    def swap(x, bit):
        return lax.ppermute(x, axis, [(j, j ^ bit) for j in range(8)])

    order = lax.axis_index(axis) ^ jnp.array([0, 2, 4, 6, 1, 3, 5, 7], jnp.int32)
    width = right[0].shape[0] // 8
    height = rows_low.shape[0]
    low, high = slice(0, height // 2), slice(height // 2, height)

    def pair_sum(half, rows):
        away = products(rows, half, right, order, 4)
        got = swap(away, 1)
        return add(products(together(rows, away), half, right, order, 0), got)

    def block(x, b, rows):
        return x[rows, b * width : (b + 1) * width]

    def first_sends(x):
        return [
            jnp.concatenate([block(x, 1, low), block(x, 3, low)], axis=1),
            jnp.concatenate([block(x, 2, high), block(x, 3, high)], axis=1),
        ]

    def second_sends(x, by_x, by_y):
        return [add(block(x, 2, low), by_x[:, width:]), add(block(x, 1, high), by_y[:, width:])]

    def sums(x, by_x, by_y, then_y, then_x):
        total = lambda a, b, c: a.astype(F32) + b[:, :width].astype(F32) + c.astype(F32)
        return [total(block(x, 0, low), by_x, then_y), total(block(x, 0, high), by_y, then_x)]

    sum0 = pair_sum(0, rows + [rows_low])
    by_x0, by_y0 = together(first_sends(sum0))
    by_x0, by_y0 = swap(by_x0, 2), swap(by_y0, 4)
    then_y0, then_x0 = together(second_sends(sum0, by_x0, by_y0))
    sum1 = pair_sum(1, rows + [rows_high(then_y0)])
    then_y0, then_x0 = swap(then_y0, 4), swap(then_x0, 2)
    by_x1, by_y1 = together(first_sends(sum1), then_y0, then_x0)
    by_x1, by_y1 = swap(by_x1, 2), swap(by_y1, 4)
    then_y1, then_x1 = together(second_sends(sum1, by_x1, by_y1))
    then_y1, then_x1 = swap(then_y1, 4), swap(then_x1, 2)
    kept = sums(sum0, by_x0, by_y0, then_y0, then_x0) + sums(sum1, by_x1, by_y1, then_y1, then_x1)
    return jnp.concatenate(kept).astype(sum0.dtype)


def moments(rotated, first_moment, second_moment):
    first_next = 0.9 * first_moment + 0.1 * rotated
    second_next = 0.95 * second_moment + 0.05 * rotated * rotated
    scaled_first = first_next / (1.0 - 0.9**10)
    scaled_second = second_next / (1.0 - 0.95**10)
    normalized = (scaled_first / (jnp.sqrt(scaled_second) + 1e-08)).astype(BF16)
    return first_next, second_next, normalized


STEPS = 2


def part_kernel(place, left, near, middle, out, first, second, basis, *rest, results):
    first_out, second_out, *backs, total, normalized = rest[-4 - results :]
    step = pl.program_id(0)

    @pl.when(step == 0)
    def _():
        total[...] = jnp.zeros_like(total)

    def accumulate(right):
        depth = left.shape[2]
        for b in range(left.shape[0]):
            total[...] += jnp.dot(left[b], right[b * depth : (b + 1) * depth, :], preferred_element_type=F32)

    @pl.when(step < STEPS)
    def _():
        accumulate(near)

    far = (step >= STEPS) & (step < 2 * STEPS)

    @pl.when(far & (place[2] == 1))
    def _():
        accumulate(middle)

    @pl.when(far & (place[2] == 0))
    def _():
        accumulate(out)

    @pl.when(step == 2 * STEPS - 1)
    def _():
        first_out[...], second_out[...], normalized[...] = moments(total[...], first[...], second[...])

    for number, back in enumerate(backs):

        @pl.when(step == 2 * STEPS + number)
        def _(back=back):
            back[...] = jnp.dot(basis[...], normalized[...], preferred_element_type=F32).astype(BF16)


def part(number, place, results, left_rotated, near, middle, out, first_moment, second_moment, left_cols, before):
    height, width = first_moment.shape
    size = near.shape[1]
    deep = near.shape[0] // STEPS
    tall = left_cols.shape[0] // results
    near_step = lambda s: jnp.minimum(s, STEPS - 1)
    far_step = lambda s: jnp.clip(s - STEPS, 0, STEPS - 1)
    last_step = lambda s: jnp.maximum(s - 2 * STEPS, 0)

    def left_block(s, place):
        return jnp.where(s < STEPS, place[0] + near_step(s), place[1] + far_step(s)), 0, 0

    moment = pl.BlockSpec((height, size), lambda s, place: (0, number))
    before = list(before)
    first_next, second_next, *backs = pl.pallas_call(
        functools.partial(part_kernel, results=results),
        grid_spec=pltpu.PrefetchScalarGridSpec(
            num_scalar_prefetch=1,
            grid=(2 * STEPS + results,),
            in_specs=[
                pl.BlockSpec((4 // STEPS, height, width), left_block),
                pl.BlockSpec((deep, size), lambda s, place: (near_step(s), 0)),
                pl.BlockSpec((deep, size), lambda s, place: (far_step(s) * place[2], 0)),
                pl.BlockSpec((deep, size), lambda s, place: (far_step(s) * (1 - place[2]), 0)),
                moment,
                moment,
                pl.BlockSpec((tall, height), lambda s, place: (place[3 + last_step(s)], 0)),
            ]
            + [pl.BlockSpec(memory_space=pl.ANY)] * len(before),
            out_specs=[moment, moment] + [pl.BlockSpec((tall, size), lambda s, place: (0, 0))] * results,
            scratch_shapes=[pltpu.VMEM((height, size), F32), pltpu.VMEM((height, size), BF16)],
        ),
        out_shape=[jax.ShapeDtypeStruct((height, width), F32)] * 2
        + [jax.ShapeDtypeStruct((tall, size), BF16)] * results,
        input_output_aliases={8: 0, 9: 1} if before else {},
        compiler_params=pltpu.CompilerParams(vmem_limit_bytes=VMEM),
        cost_estimate=QUICK,
    )(place, left_rotated, near, middle, out, first_moment, second_moment, left_cols, *before)
    return (first_next, second_next), backs


def body_on_line(gradient, left_stat, left_basis, right_basis, first_moment, second_moment):
    line = Line("row")
    send = line.send
    height, width = gradient.shape
    cuts = [slice(p * width // 3, (p + 1) * width // 3) for p in range(3)]
    left_cols = lax.all_gather(left_basis, "col", axis=0, tiled=True)
    own0, own1, own2 = [right_basis[:, cut] for cut in cuts]

    mirror = send(gradient, MIRROR)
    pair = send(gradient, PAIRS)
    relay = send(after(jnp.where(line.inner, mirror, gradient), pair), RELAY)
    turn = lambda x, bits: contract_first(line.block(left_cols, bits), x)
    left_sum = turn(gradient, 0) + turn(pair, 1) + turn(mirror, 3)
    pair0 = send(after(own0, left_sum), PAIRS)

    near0, own1 = together([line.near(own0, pair0), own1])
    middle0 = send(near0, MIDDLE)
    pair1 = send(own1, PAIRS)
    near1 = line.near(own1, pair1)
    pair2 = send(after(own2, near1), PAIRS)

    left_part = (left_sum + turn(after(relay, near0), 2)).astype(BF16)
    left_rotated = lax.all_gather(left_part, "col")

    middle0, near1 = together([middle0, near1], left_part, pair2)
    out0 = send(middle0, OUTWARD)
    middle1 = send(near1, MIDDLE)
    columns = jnp.zeros((4 * height, width), BF16)
    near2 = line.near(own2, pair2)
    for bits, piece in zip((0, 1, 3, 2), together([gradient, pair, mirror, relay], left_part, near2)):
        columns = line.placed(columns, piece, bits)
    product_here = contract_last(columns, gradient).astype(BF16)
    product = lax.psum_scatter(after(product_here, out0, middle1), "col", scatter_dimension=0, tiled=True)

    middle1, near2 = together([middle1, near2], out0, product_here)
    out1 = send(middle1, OUTWARD)
    middle2 = send(near2, MIDDLE)

    halves_first = jnp.where(line.lower, jnp.array([0, STEPS]), jnp.array([STEPS, 0]))
    far_near = jnp.where(line.lower, jnp.array([1, 0]), jnp.array([0, 1]))
    place = jnp.concatenate([halves_first, line.inner[None]]).astype(jnp.int32)
    to_halves = jnp.concatenate([place, far_near]).astype(jnp.int32)
    to_blocks = jnp.concatenate([place, line.i ^ jnp.array([2, 1, 3, 0])]).astype(jnp.int32)

    def next_part(number, near, middle, out, before):
        order, results = (to_blocks, 4) if number == 2 else (to_halves, 2)
        return part(
            number, order, results, left_rotated, near, middle, out, first_moment, second_moment, left_cols, before
        )

    moments0, (far0, stay0) = next_part(0, near0, middle0, after(out0, near2), ())
    got0 = send(far0, INWARD)
    out2 = send(after(middle2, out1, far0), OUTWARD)
    moments1, (far1, stay1) = next_part(1, near1, middle1, after(out1, far0), moments0)
    got1 = send(far1, INWARD)
    through0 = send(add(far0, after(got0, far1)), MIDDLE)
    got1, out2 = together([got1, out2])
    through1 = add(far1, got1)
    mine0, other0 = halves(line.even, stay0.astype(F32) + after(through0, through1).astype(F32))
    other0 = other0.astype(BF16)
    moments2, blocks2 = next_part(2, near2, middle2, after(out2, other0, through1), moments1)
    other0 = send(other0, PAIRS)
    turned0 = (mine0 + other0.astype(F32)).astype(BF16)
    through1 = send(through1, MIDDLE)
    mine1, other1 = halves(line.even, stay1.astype(F32) + through1.astype(F32))
    other1 = other1.astype(BF16)
    turned1 = (mine1 + send(other1, PAIRS).astype(F32)).astype(BF16)
    first_next, second_next = moments2

    half = height // 2
    low, high = [x[:half] for x in blocks2], [x[half:] for x in blocks2]

    def summed(blocks, relay, pair, mirror):
        total = blocks[3].astype(F32) + jnp.where(line.inner, 0, relay).astype(F32)
        return (total + pair.astype(F32) + mirror.astype(F32)).astype(BF16)

    relay_low = send(low[0], RELAY_BACK)
    pair_low = send(low[1], PAIRS)
    relay_low = after(relay_low, through1, other0)
    to_mirror = add(low[2], jnp.where(line.inner, relay_low, 0))
    mirror_low = send(to_mirror, MIRROR)
    to_relay, to_pair = together(high[:2], relay_low)
    relay_high = send(to_relay, RELAY_BACK)
    pair_high = send(to_pair, PAIRS)
    out0, out1, out2, product = together([out0, out1, out2, product], turned0, to_mirror, other1)
    right = [line.whole(near0, middle0, out0), line.whole(near1, middle1, out1), line.whole(near2, middle2, out2)]
    left_next = 0.95 * left_stat + 0.05 * product.astype(F32)
    relay_high = after(relay_high, to_mirror)
    mirror_high = send(add(high[2], jnp.where(line.inner, relay_high, 0)), MIRROR)
    turned_low = summed(low, relay_low, pair_low, after(mirror_low, *right))

    def turned_high(earlier):
        return summed(high, relay_high, pair_high, after(mirror_high, earlier))

    right = together(right, left_next)
    direction = scatter_columns([turned0, turned1], turned_low, turned_high, right, "col")
    return (left_next, first_next, second_next, direction)


def body(gradient, left_stat, left_basis, right_basis, first_moment, second_moment):
    columns = lax.all_gather(gradient, "row", axis=0, tiled=True)
    left_cols = lax.all_gather(left_basis, "col", axis=0, tiled=True)
    right_cols = lax.all_gather(right_basis, "row", axis=0, tiled=True)
    left_rotated = lax.all_gather(contract_first(left_cols, columns).astype(BF16), "col", axis=1, tiled=True)
    product = contract_last(columns, gradient).astype(BF16)
    product = lax.psum_scatter(product, "col", scatter_dimension=0, tiled=True).astype(F32)
    left_next = 0.95 * left_stat + 0.05 * product
    rotated = jnp.dot(left_rotated, right_cols, preferred_element_type=F32)
    first_next, second_next, normalized = moments(rotated, first_moment, second_moment)
    back = jnp.dot(left_cols, normalized, preferred_element_type=F32).astype(BF16)
    back = lax.psum_scatter(back, "row", scatter_dimension=0, tiled=True)
    direction = contract_last(back, right_cols).astype(BF16)
    direction = lax.psum_scatter(direction, "col", scatter_dimension=1, tiled=True)
    return (left_next, first_next, second_next, direction)


def solution(mesh):
    on_line = mesh.shape["row"] == 4 and mesh.shape["col"] == 8
    return jax.shard_map(
        body_on_line if on_line else body,
        mesh=mesh,
        in_specs=(
            P("row", "col"),
            P("col", "row"),
            P("col", "row"),
            P("row", "col"),
            P("row", "col"),
            P("row", "col"),
        ),
        out_specs=(P("col", "row"), P("row", "col"), P("row", "col"), P("row", "col")),
        check_vma=False,
    )
```

```python
import functools

import jax
import jax.numpy as jnp
from jax import lax
from jax.experimental import pallas as pl
from jax.experimental.pallas import tpu as pltpu
from jax.sharding import PartitionSpec as P

BF16 = jnp.bfloat16
F32 = jnp.float32
VMEM = 40 * 2**20
QUICK = pl.CostEstimate(flops=2**20, bytes_accessed=2**16, transcendentals=0)

PAIRS = [(0, 1), (1, 0), (2, 3), (3, 2)]
MIDDLE = [(1, 2), (2, 1)]
OUTWARD = [(1, 0), (2, 3)]
INWARD = [(0, 1), (3, 2)]
MIRROR = [(0, 3), (1, 2), (2, 1), (3, 0)]
RELAY = [(0, 2), (1, 0), (2, 3), (3, 1)]
RELAY_BACK = [(0, 1), (1, 3), (2, 0), (3, 2)]


def contract_last(first, second):
    return lax.dot_general(first, second, (((1,), (1,)), ((), ())), preferred_element_type=F32)


def contract_first(first, second):
    return lax.dot_general(first, second, (((0,), (0,)), ((), ())), preferred_element_type=F32)


def together(operands, *earlier):
    return lax.optimization_barrier(tuple(operands) + earlier)[: len(operands)]


def after(x, *earlier):
    return together([x], *earlier)[0]


def joined(keep_order, first, second):
    return jnp.where(keep_order, jnp.concatenate([first, second]), jnp.concatenate([second, first]))


def halves(keep_order, x):
    n = x.shape[0] // 2
    return jnp.where(keep_order, x[:n], x[n:]), jnp.where(keep_order, x[n:], x[:n])


class Line:
    def __init__(self, axis):
        self.axis = axis
        self.i = lax.axis_index(axis)
        self.even = self.i % 2 == 0
        self.lower = self.i < 2
        self.inner = (self.i == 1) | (self.i == 2)

    def send(self, x, pairs):
        return lax.ppermute(x, self.axis, pairs)

    def near(self, x, got):
        return joined(self.even, x, got)

    def whole(self, near, middle, out):
        return joined(self.lower, near, jnp.where(self.inner, middle, out))

    def placed(self, whole, piece, bits):
        return lax.dynamic_update_slice(whole, piece, ((self.i ^ bits) * piece.shape[0], 0))

    def block(self, x, bits):
        n = x.shape[0] // 4
        return lax.dynamic_slice_in_dim(x, (self.i ^ bits) * n, n, 0)


def add(first, second):
    return (first.astype(F32) + second.astype(F32)).astype(first.dtype)


def products_kernel(order, *refs):
    parts = len(refs) // 2
    total = sum(contract_last(rows[...], right[...]) for rows, right in zip(refs[:parts], refs[parts:]))
    refs[-1][...] = total.astype(refs[-1].dtype)


def products(rows, half, right, order, start):
    height, depth = rows[-1].shape
    width = right[0].shape[0] // 8
    return pl.pallas_call(
        products_kernel,
        grid_spec=pltpu.PrefetchScalarGridSpec(
            num_scalar_prefetch=1,
            grid=(4,),
            in_specs=[pl.BlockSpec((height, depth), lambda b, order: (half, 0))] * (len(rows) - 1)
            + [pl.BlockSpec((height, depth), lambda b, order: (0, 0))]
            + [pl.BlockSpec((width, depth), lambda b, order: (order[start + b], 0))] * len(right),
            out_specs=pl.BlockSpec((height, width), lambda b, order: (0, b)),
        ),
        out_shape=jax.ShapeDtypeStruct((height, 4 * width), rows[0].dtype),
        compiler_params=pltpu.CompilerParams(vmem_limit_bytes=VMEM // 2),
        cost_estimate=QUICK,
    )(order, *rows, *right)


def scatter_columns(rows, rows_low, rows_high, right, axis):
    def swap(x, bit):
        return lax.ppermute(x, axis, [(j, j ^ bit) for j in range(8)])

    order = lax.axis_index(axis) ^ jnp.array([0, 2, 4, 6, 1, 3, 5, 7], jnp.int32)
    width = right[0].shape[0] // 8
    height = rows_low.shape[0]
    low, high = slice(0, height // 2), slice(height // 2, height)

    def pair_sum(half, rows):
        away = products(rows, half, right, order, 4)
        got = swap(away, 1)
        return add(products(together(rows, away), half, right, order, 0), got)

    def block(x, b, rows):
        return x[rows, b * width : (b + 1) * width]

    def first_sends(x):
        return [
            jnp.concatenate([block(x, 1, low), block(x, 3, low)], axis=1),
            jnp.concatenate([block(x, 2, high), block(x, 3, high)], axis=1),
        ]

    def second_sends(x, by_x, by_y):
        return [add(block(x, 2, low), by_x[:, width:]), add(block(x, 1, high), by_y[:, width:])]

    def sums(x, by_x, by_y, then_y, then_x):
        total = lambda a, b, c: a.astype(F32) + b[:, :width].astype(F32) + c.astype(F32)
        return [total(block(x, 0, low), by_x, then_y), total(block(x, 0, high), by_y, then_x)]

    sum0 = pair_sum(0, rows + [rows_low])
    by_x0, by_y0 = together(first_sends(sum0))
    by_x0, by_y0 = swap(by_x0, 2), swap(by_y0, 4)
    then_y0, then_x0 = together(second_sends(sum0, by_x0, by_y0))
    sum1 = pair_sum(1, rows + [rows_high(then_y0)])
    then_y0, then_x0 = swap(then_y0, 4), swap(then_x0, 2)
    by_x1, by_y1 = together(first_sends(sum1), then_y0, then_x0)
    by_x1, by_y1 = swap(by_x1, 2), swap(by_y1, 4)
    then_y1, then_x1 = together(second_sends(sum1, by_x1, by_y1))
    then_y1, then_x1 = swap(then_y1, 4), swap(then_x1, 2)
    kept = sums(sum0, by_x0, by_y0, then_y0, then_x0) + sums(sum1, by_x1, by_y1, then_y1, then_x1)
    return jnp.concatenate(kept).astype(sum0.dtype)


def moments(rotated, first_moment, second_moment):
    first_next = 0.9 * first_moment + 0.1 * rotated
    second_next = 0.95 * second_moment + 0.05 * rotated * rotated
    scaled_first = first_next / (1.0 - 0.9**10)
    scaled_second = second_next / (1.0 - 0.95**10)
    normalized = (scaled_first / (jnp.sqrt(scaled_second) + 1e-08)).astype(BF16)
    return first_next, second_next, normalized


STEPS = 2


def part_kernel(place, left, near, middle, out, first, second, basis, *rest, results):
    first_out, second_out, *backs, total, normalized = rest[-4 - results :]
    step = pl.program_id(0)

    @pl.when(step == 0)
    def _():
        total[...] = jnp.zeros_like(total)

    def accumulate(right):
        depth = left.shape[2]
        for b in range(left.shape[0]):
            total[...] += jnp.dot(left[b], right[b * depth : (b + 1) * depth, :], preferred_element_type=F32)

    @pl.when(step < STEPS)
    def _():
        accumulate(near)

    far = (step >= STEPS) & (step < 2 * STEPS)

    @pl.when(far & (place[2] == 1))
    def _():
        accumulate(middle)

    @pl.when(far & (place[2] == 0))
    def _():
        accumulate(out)

    @pl.when(step == 2 * STEPS - 1)
    def _():
        first_out[...], second_out[...], normalized[...] = moments(total[...], first[...], second[...])

    for number, back in enumerate(backs):

        @pl.when(step == 2 * STEPS + number)
        def _(back=back):
            back[...] = jnp.dot(basis[...], normalized[...], preferred_element_type=F32).astype(BF16)


def part(number, place, results, left_rotated, near, middle, out, first_moment, second_moment, left_cols, before):
    height, width = first_moment.shape
    size = near.shape[1]
    deep = near.shape[0] // STEPS
    tall = left_cols.shape[0] // results
    near_step = lambda s: jnp.minimum(s, STEPS - 1)
    far_step = lambda s: jnp.clip(s - STEPS, 0, STEPS - 1)
    last_step = lambda s: jnp.maximum(s - 2 * STEPS, 0)

    def left_block(s, place):
        return jnp.where(s < STEPS, place[0] + near_step(s), place[1] + far_step(s)), 0, 0

    moment = pl.BlockSpec((height, size), lambda s, place: (0, number))
    before = list(before)
    first_next, second_next, *backs = pl.pallas_call(
        functools.partial(part_kernel, results=results),
        grid_spec=pltpu.PrefetchScalarGridSpec(
            num_scalar_prefetch=1,
            grid=(2 * STEPS + results,),
            in_specs=[
                pl.BlockSpec((4 // STEPS, height, width), left_block),
                pl.BlockSpec((deep, size), lambda s, place: (near_step(s), 0)),
                pl.BlockSpec((deep, size), lambda s, place: (far_step(s) * place[2], 0)),
                pl.BlockSpec((deep, size), lambda s, place: (far_step(s) * (1 - place[2]), 0)),
                moment,
                moment,
                pl.BlockSpec((tall, height), lambda s, place: (place[3 + last_step(s)], 0)),
            ]
            + [pl.BlockSpec(memory_space=pl.ANY)] * len(before),
            out_specs=[moment, moment] + [pl.BlockSpec((tall, size), lambda s, place: (0, 0))] * results,
            scratch_shapes=[pltpu.VMEM((height, size), F32), pltpu.VMEM((height, size), BF16)],
        ),
        out_shape=[jax.ShapeDtypeStruct((height, width), F32)] * 2
        + [jax.ShapeDtypeStruct((tall, size), BF16)] * results,
        input_output_aliases={8: 0, 9: 1} if before else {},
        compiler_params=pltpu.CompilerParams(vmem_limit_bytes=VMEM),
        cost_estimate=QUICK,
    )(place, left_rotated, near, middle, out, first_moment, second_moment, left_cols, *before)
    return (first_next, second_next), backs


def body_on_line(gradient, left_stat, left_basis, right_basis, first_moment, second_moment):
    line = Line("row")
    send = line.send
    height, width = gradient.shape
    cuts = [slice(p * width // 3, (p + 1) * width // 3) for p in range(3)]
    left_cols = lax.all_gather(left_basis, "col", axis=0, tiled=True)
    own0, own1, own2 = [right_basis[:, cut] for cut in cuts]

    mirror = send(gradient, MIRROR)
    pair = send(gradient, PAIRS)
    relay = send(after(jnp.where(line.inner, mirror, gradient), pair), RELAY)
    turn = lambda x, bits: contract_first(line.block(left_cols, bits), x)
    left_sum = turn(gradient, 0) + turn(pair, 1) + turn(mirror, 3)
    pair0 = send(after(own0, left_sum), PAIRS)

    near0, own1 = together([line.near(own0, pair0), own1])
    middle0 = send(near0, MIDDLE)
    pair1 = send(own1, PAIRS)
    near1 = line.near(own1, pair1)
    pair2 = send(after(own2, near1), PAIRS)

    left_part = (left_sum + turn(after(relay, near0), 2)).astype(BF16)
    left_rotated = lax.all_gather(left_part, "col")

    middle0, near1 = together([middle0, near1], left_part, pair2)
    out0 = send(middle0, OUTWARD)
    middle1 = send(near1, MIDDLE)
    columns = jnp.zeros((4 * height, width), BF16)
    near2 = line.near(own2, pair2)
    for bits, piece in zip((0, 1, 3, 2), together([gradient, pair, mirror, relay], left_part, near2)):
        columns = line.placed(columns, piece, bits)
    product_here = contract_last(columns, gradient).astype(BF16)
    product = lax.psum_scatter(after(product_here, out0, middle1), "col", scatter_dimension=0, tiled=True)

    middle1, near2 = together([middle1, near2], out0, product_here)
    out1 = send(middle1, OUTWARD)
    middle2 = send(near2, MIDDLE)

    halves_first = jnp.where(line.lower, jnp.array([0, STEPS]), jnp.array([STEPS, 0]))
    far_near = jnp.where(line.lower, jnp.array([1, 0]), jnp.array([0, 1]))
    place = jnp.concatenate([halves_first, line.inner[None]]).astype(jnp.int32)
    to_halves = jnp.concatenate([place, far_near]).astype(jnp.int32)
    to_blocks = jnp.concatenate([place, line.i ^ jnp.array([2, 1, 3, 0])]).astype(jnp.int32)

    def next_part(number, near, middle, out, before):
        order, results = (to_blocks, 4) if number == 2 else (to_halves, 2)
        return part(
            number, order, results, left_rotated, near, middle, out, first_moment, second_moment, left_cols, before
        )

    moments0, (far0, stay0) = next_part(0, near0, middle0, after(out0, near2), ())
    got0 = send(far0, INWARD)
    out2 = send(after(middle2, out1, far0), OUTWARD)
    moments1, (far1, stay1) = next_part(1, near1, middle1, after(out1, far0), moments0)
    got1 = send(far1, INWARD)
    through0 = send(add(far0, after(got0, far1)), MIDDLE)
    got1, out2 = together([got1, out2])
    through1 = add(far1, got1)
    mine0, other0 = halves(line.even, stay0.astype(F32) + after(through0, through1).astype(F32))
    other0 = other0.astype(BF16)
    moments2, blocks2 = next_part(2, near2, middle2, after(out2, other0, through1), moments1)
    other0 = send(other0, PAIRS)
    turned0 = (mine0 + other0.astype(F32)).astype(BF16)
    through1 = send(through1, MIDDLE)
    mine1, other1 = halves(line.even, stay1.astype(F32) + through1.astype(F32))
    turned1 = (mine1 + send(other1.astype(BF16), PAIRS).astype(F32)).astype(BF16)
    first_next, second_next = moments2

    half = height // 2
    low, high = [x[:half] for x in blocks2], [x[half:] for x in blocks2]

    def summed(blocks, relay, pair, mirror):
        total = blocks[3].astype(F32) + jnp.where(line.inner, 0, relay).astype(F32)
        return (total + pair.astype(F32) + mirror.astype(F32)).astype(BF16)

    relay_low = send(low[0], RELAY_BACK)
    pair_low = send(low[1], PAIRS)
    relay_low = after(relay_low, through1, other0)
    to_mirror = add(low[2], jnp.where(line.inner, relay_low, 0))
    mirror_low = send(to_mirror, MIRROR)
    to_relay, to_pair = together(high[:2], relay_low)
    relay_high = send(to_relay, RELAY_BACK)
    pair_high = send(to_pair, PAIRS)
    out0, out1, out2, product = together([out0, out1, out2, product], turned0)
    right = [line.whole(near0, middle0, out0), line.whole(near1, middle1, out1), line.whole(near2, middle2, out2)]
    left_next = 0.95 * left_stat + 0.05 * product.astype(F32)
    relay_high = after(relay_high, to_mirror)
    mirror_high = send(add(high[2], jnp.where(line.inner, relay_high, 0)), MIRROR)
    turned_low = summed(low, relay_low, pair_low, after(mirror_low, *right))

    def turned_high(earlier):
        return summed(high, relay_high, pair_high, after(mirror_high, earlier))

    right = together(right, left_next)
    direction = scatter_columns([turned0, turned1], turned_low, turned_high, right, "col")
    return (left_next, first_next, second_next, direction)


def body(gradient, left_stat, left_basis, right_basis, first_moment, second_moment):
    columns = lax.all_gather(gradient, "row", axis=0, tiled=True)
    left_cols = lax.all_gather(left_basis, "col", axis=0, tiled=True)
    right_cols = lax.all_gather(right_basis, "row", axis=0, tiled=True)
    left_rotated = lax.all_gather(contract_first(left_cols, columns).astype(BF16), "col", axis=1, tiled=True)
    product = contract_last(columns, gradient).astype(BF16)
    product = lax.psum_scatter(product, "col", scatter_dimension=0, tiled=True).astype(F32)
    left_next = 0.95 * left_stat + 0.05 * product
    rotated = jnp.dot(left_rotated, right_cols, preferred_element_type=F32)
    first_next, second_next, normalized = moments(rotated, first_moment, second_moment)
    back = jnp.dot(left_cols, normalized, preferred_element_type=F32).astype(BF16)
    back = lax.psum_scatter(back, "row", scatter_dimension=0, tiled=True)
    direction = contract_last(back, right_cols).astype(BF16)
    direction = lax.psum_scatter(direction, "col", scatter_dimension=1, tiled=True)
    return (left_next, first_next, second_next, direction)


def solution(mesh):
    on_line = mesh.shape["row"] == 4 and mesh.shape["col"] == 8
    return jax.shard_map(
        body_on_line if on_line else body,
        mesh=mesh,
        in_specs=(
            P("row", "col"),
            P("col", "row"),
            P("col", "row"),
            P("row", "col"),
            P("row", "col"),
            P("row", "col"),
        ),
        out_specs=(P("col", "row"), P("row", "col"), P("row", "col"), P("row", "col")),
        check_vma=False,
    )
```
